32 devices in a mesh: step: 4 (over y, x), head: 4 (over z), fsdp: 2 (over core).
Axes of the slice: x: 2, y: 2, z: 4, core: 2. Of those that a mesh axis runs over, the one named last changes fastest.
Arguments:
- states: float32 [4, 2, 512, 5120], P('step', 'fsdp', 'head'), may hold values from -10.5 to 10.5
- timesteps: int32 [4, 2], P('step'), may hold values from 0 to 1000, as said below
- lengths: int32 [2], P('fsdp'), may hold values from 256 to 512, as said below
- modulation: float32 [4, 3, 5120], P('step'), may hold values from -4 to 4
- w_query: bfloat16 [5120, 3072], P(('step', 'fsdp'), 'head'), may hold values from -0.1118034 to 0.1118034
- w_key: bfloat16 [5120, 3072], P(('step', 'fsdp'), 'head'), may hold values from -0.1118034 to 0.1118034
- w_value: bfloat16 [5120, 3072], P(('step', 'fsdp'), 'head'), may hold values from -0.078125 to 0.078125
- w_out: bfloat16 [3072, 5120], P('head', ('step', 'fsdp')), may hold values from -0.109375 to 0.109375
- q_gain: float32 [3072], P('head'), may hold values from 0.5 to 12
- k_gain: float32 [3072], P('head'), may hold values from 0.5 to 12
Outputs:
- next_states: float32 [4, 2, 512, 5120], P('step', 'fsdp', 'head')
- update: bfloat16 [4, 2, 512, 5120], P('step', 'fsdp', 'head')
The draws below stay inside these ranges and needn't reach their ends.
Inputs may be any that keep to these rules, and one draw needn't show every extreme that they name: `timesteps`: A row holds a step's start above its end; each row's end is the next row's start; the first row starts at 1000 and the last ends at 0. `lengths`: positions from a clip's length on are padding; at least one clip is full.
All inputs are finite; a program needn't handle non-finite values.
Results may differ from the reference program's by a relative error of at most 0.02.
The reference program's roundings to bfloat16 on the way count: a program that leaves them out, or rounds other values in their place, can miss the bound.
Values may be sent and summed in bfloat16 or wider, within the bound.
No kernel may reach another device: no remote copies, remote signals or barrier semaphores. Data moves between devices by JAX's collectives and lax.ppermute only.
A program may use at most 128 MiB of HBM per device.

```python
import math
import jax
import jax.numpy as jnp
from jax import lax

D = 5120
HD = 128
HEADS = 24
INNER = 3072
SEQ = 512
STEPS = 4
PROMPTS = 2
N_HEAD = 4


def draw_states(key, part):
    key = jax.random.fold_in(key, 11)
    base_key, row_key, col_key = jax.random.split(key, 3)
    shape_all = (STEPS, PROMPTS, SEQ, D)
    noise = jax.random.truncated_normal(base_key, -3.0, 3.0, shape_all, jnp.float32)
    row_scale = jnp.exp(jax.random.uniform(row_key, (STEPS, PROMPTS, SEQ, 1), jnp.float32, math.log(0.3), math.log(3.0)))
    col_scale = jnp.exp(jax.random.uniform(col_key, (1, 1, 1, D), jnp.float32, math.log(0.4), math.log(4.0)))
    return 0.2 * noise * row_scale * col_scale


def draw_timesteps(key, part):
    key = jax.random.fold_in(key, 23)
    widths = jax.random.randint(key, (STEPS,), 2, 5, dtype=jnp.int32)
    reached = jnp.cumsum(widths, dtype=jnp.int32)
    ends = (1000 - 1000 * reached // reached[-1]).astype(jnp.int32)
    starts = jnp.concatenate([jnp.full((1,), 1000, jnp.int32), ends[:-1]])
    return jnp.stack([starts, ends], axis=1).astype(jnp.int32)


def draw_lengths(key, part):
    key = jax.random.fold_in(key, 37)
    base_key, full_key = jax.random.split(key, 2)
    drawn = jax.random.randint(base_key, (PROMPTS,), SEQ // 2, SEQ + 1, dtype=jnp.int32)
    chosen = jax.random.randint(full_key, (), 0, PROMPTS, dtype=jnp.int32)
    return jnp.where(jnp.arange(PROMPTS, dtype=jnp.int32) == chosen, SEQ, drawn).astype(jnp.int32)


def draw_modulation(key, part):
    key = jax.random.fold_in(key, 67)
    base_key, sign_key, size_key = jax.random.split(key, 3)
    leading = 0.6 * jax.random.truncated_normal(base_key, -6.0, 6.0, (STEPS, 2, D), jnp.float32)
    magnitude = jnp.exp(jax.random.uniform(size_key, (STEPS, 1, D), jnp.float32, math.log(2.5), math.log(4.0)))
    signs = jnp.where(jax.random.bernoulli(sign_key, 0.5, (STEPS, 1, D)), 1.0, -1.0).astype(jnp.float32)
    return jnp.concatenate([leading, signs * magnitude], axis=1)


def rising_matrix(key, rise):
    entries = jax.random.truncated_normal(key, -4.0, 4.0, (D, INNER), jnp.float32)
    place = jnp.arange(INNER, dtype=jnp.float32) / float(INNER - 1) - 0.5
    column_scale = jnp.exp(math.log(rise) * place)
    return entries * column_scale[None, :] / math.sqrt(D)


def draw_w_query(key, part):
    key = jax.random.fold_in(key, 53)
    result = rising_matrix(key, 2.5)
    return result.astype(jnp.bfloat16)


def draw_w_key(key, part):
    key = jax.random.fold_in(key, 59)
    result = rising_matrix(key, 2.5)
    return result.astype(jnp.bfloat16)


def draw_q_gain(key, part):
    key = jax.random.fold_in(key, 41)
    result = jnp.exp(jax.random.uniform(key, (INNER,), jnp.float32, math.log(2.0), math.log(4.0)))
    return result


def draw_k_gain(key, part):
    key = jax.random.fold_in(key, 43)
    result = jnp.exp(jax.random.uniform(key, (INNER,), jnp.float32, math.log(2.0), math.log(4.0)))
    return result


def level_of(own_key, shape, pieces, least, largest):
    gain = 1.0
    for position, shards_of in pieces:
        steps = jax.random.uniform(jax.random.fold_in(jax.random.fold_in(own_key, 6), position), (shards_of,), jnp.float32, least / len(pieces), largest / len(pieces))
        gain = gain * jnp.repeat(jnp.exp(steps), shape[position] // shards_of).reshape((-1,) + (1,) * (len(shape) - 1 - position))
    return gain


def normal_values(stream_key, shape, deviation, bound, shards=(), held_as=jnp.bfloat16):
    values = deviation * jax.random.normal(stream_key, shape, jnp.float32)
    if shards:
        values = values * level_of(stream_key, shape, shards, -0.22, 0.18)
    return jnp.clip(values, -bound, bound).astype(held_as)


def setup_inputs(seed: int = 0) -> dict:
    streams_of = jax.random.split(jax.random.key(seed), 11)
    states = draw_states(jax.random.fold_in(streams_of[10], 71), 0)
    timesteps = draw_timesteps(jax.random.fold_in(streams_of[10], 71), 0)
    lengths = draw_lengths(jax.random.fold_in(streams_of[10], 71), 0)
    modulation = draw_modulation(jax.random.fold_in(streams_of[10], 71), 0)
    w_query = draw_w_query(jax.random.fold_in(streams_of[10], 71), 0)
    w_key = draw_w_key(jax.random.fold_in(streams_of[10], 71), 0)
    w_value = normal_values(streams_of[6], (D, INNER), D ** -0.5, 0.078125, ((0, 8), (1, 4)))
    w_out = normal_values(streams_of[7], (INNER, D), INNER ** -0.5, 0.109375, ((0, 4), (1, 8)))
    q_gain = draw_q_gain(jax.random.fold_in(streams_of[10], 71), 0)
    k_gain = draw_k_gain(jax.random.fold_in(streams_of[10], 71), 0)
    return dict(states=states, timesteps=timesteps, lengths=lengths, modulation=modulation, w_query=w_query, w_key=w_key, w_value=w_value, w_out=w_out, q_gain=q_gain, k_gain=k_gain)


def normed_rows(current, shift_row, scale_row):
    centre = lax.optimization_barrier(jnp.mean(current, axis=-1, keepdims=True))
    centred = current - centre
    spread = lax.optimization_barrier(jnp.mean(centred * centred, axis=-1, keepdims=True))
    return (centred * lax.rsqrt(spread + 1e-06) * (1.0 + scale_row) + shift_row).astype(jnp.bfloat16)

def width_norm(values, gain_vec):
    row_count = values.shape[0]
    square = lax.optimization_barrier(jnp.mean(values * values, axis=-1, keepdims=True))
    normed = (values * lax.rsqrt(square + 1e-06) * gain_vec).astype(jnp.bfloat16)
    return normed.reshape(row_count, values.shape[1] // HD, HD)

def reference(states, timesteps, lengths, modulation, w_query, w_key, w_value, w_out, q_gain, k_gain):
    scaling = 1.0 / math.sqrt(HD)
    group_width = HEADS * HD // N_HEAD
    positions = jnp.arange(SEQ, dtype=jnp.int32)

    def one_pair(pair_index):
        step_at = pair_index // PROMPTS
        prompt_at = pair_index % PROMPTS
        current = states[step_at, prompt_at]
        mod_rows = modulation[step_at]
        modulated = normed_rows(current, mod_rows[0], mod_rows[1])
        queries = width_norm(jnp.dot(modulated, w_query, preferred_element_type=jnp.float32), q_gain)
        keys_normed = width_norm(jnp.dot(modulated, w_key, preferred_element_type=jnp.float32), k_gain)
        value_rows = jnp.dot(modulated, w_value, preferred_element_type=jnp.float32).astype(jnp.bfloat16)
        value_rows = value_rows.reshape(SEQ, HEADS, HD)
        valid_keys = positions < lengths[prompt_at]

        def one_head(triple):
            query_head, key_head, value_head = triple
            scores = jnp.dot(query_head, key_head.T, preferred_element_type=jnp.float32) * scaling
            scores = jnp.where(valid_keys[None, :], scores, -jnp.inf)
            highest = lax.optimization_barrier(jnp.max(scores, axis=-1, keepdims=True))
            raised = jnp.exp(scores - highest)
            soft_rows = (raised / lax.optimization_barrier(jnp.sum(raised, axis=-1, keepdims=True))).astype(jnp.bfloat16)
            return jnp.dot(soft_rows, value_head, preferred_element_type=jnp.float32).astype(jnp.bfloat16)
        heads_out = lax.map(one_head, (queries.transpose(1, 0, 2), keys_normed.transpose(1, 0, 2), value_rows.transpose(1, 0, 2)))
        attended = heads_out.transpose(1, 0, 2).reshape(SEQ, HEADS * HD)
        projected = jnp.zeros((SEQ, D), jnp.float32)
        for group_at in range(N_HEAD):
            part_sum = jnp.dot(attended[:, group_at * group_width:(group_at + 1) * group_width], w_out[group_at * group_width:(group_at + 1) * group_width], preferred_element_type=jnp.float32)
            projected = projected + lax.optimization_barrier(part_sum.astype(jnp.bfloat16)).astype(jnp.float32)
        branch = mod_rows[2] * projected
        step_width = (timesteps[step_at, 1] - timesteps[step_at, 0]).astype(jnp.float32) / 1000.0
        return (branch.astype(jnp.bfloat16), step_width * (current + branch))
    updates, drifts = lax.map(one_pair, jnp.arange(STEPS * PROMPTS, dtype=jnp.int32))
    updates = updates.reshape(STEPS, PROMPTS, SEQ, D)
    drifts = drifts.reshape(STEPS, PROMPTS, SEQ, D)
    next_states = states[0][None] + jnp.cumsum(drifts, axis=0)
    return (next_states, updates)
```

```python
import functools
import math

import jax
import jax.numpy as jnp
from jax import lax
from jax.experimental import pallas as pl
from jax.experimental.pallas import tpu as pltpu
from jax.sharding import PartitionSpec as P

HD = 128
MIB = 1 << 20
SMEM = pl.BlockSpec(memory_space=pltpu.SMEM)
VMEM = pl.BlockSpec(memory_space=pltpu.VMEM)
ANY = pl.BlockSpec(memory_space=pl.ANY)


def swap(x, axis, offset):
    return lax.ppermute(x, axis, [(i, i ^ offset) for i in range(lax.axis_size(axis))])


def spread(x, turn):
    held = [x]
    for offset in range(1, lax.axis_size("step")):
        low, high = offset & -offset, 1 << (offset.bit_length() - 1)
        last = low if turn % 2 else high
        held.append(swap(held[offset ^ last], "step", last))
    return held


def along_line(x):
    size = lax.axis_size("head")
    below, above = [x], [x]
    for hop in range(1, size):
        below.append(lax.ppermute(below[-1], "head", [(i, i + 1) for i in range(hop - 1, size - 1)]))
        above.append(lax.ppermute(above[-1], "head", [(i, i - 1) for i in range(1, size - hop + 1)]))
    return below, above


def params(mib=56):
    return pltpu.CompilerParams(vmem_limit_bytes=mib * MIB)


def cost(flops, moved, raised=0):
    return pl.CostEstimate(flops=int(flops), bytes_accessed=int(moved), transcendentals=int(raised))


def modulate_kernel(place, states, rows, mine, other):
    current = states[...]
    centre = jnp.mean(current, axis=-1, keepdims=True)
    centred = current - centre
    spread_of = jnp.mean(centred * centred, axis=-1, keepdims=True)
    shift, scale = rows[0:1, :], rows[1:2, :]
    modulated = (centred * lax.rsqrt(spread_of + 1e-06) * (1.0 + scale) + shift).astype(jnp.bfloat16)
    steps, _, width = mine.shape
    step, core = place[0], place[1]
    for block in range(2 * steps):
        piece = modulated[:, block * width : (block + 1) * width]
        at = jnp.bitwise_xor(step, block // 2)

        @pl.when(core == block % 2)
        def _(piece=piece, at=at):
            mine[at] = piece

        @pl.when(core != block % 2)
        def _(piece=piece, at=at):
            other[at] = piece


def modulate(place, states, rows, steps):
    tokens, width = states.shape
    block = width // (2 * steps)
    tile = 32
    out = jax.ShapeDtypeStruct((steps, tokens, block), jnp.bfloat16)
    spec = pl.BlockSpec((steps, tile, block), lambda i: (0, i, 0))
    return pl.pallas_call(
        modulate_kernel,
        grid=(tokens // tile,),
        in_specs=[SMEM, pl.BlockSpec((tile, width), lambda i: (i, 0)), pl.BlockSpec(rows.shape, lambda i: (0, 0))],
        out_specs=[spec, spec],
        out_shape=[out, out],
        compiler_params=params(),
        cost_estimate=cost(10 * tokens * width, 6 * tokens * width),
        name="modulate",
    )(place, states, rows)


def project_kernel(size, steps, chunks, place, *refs):
    at = 0
    slots = []
    for _ in range(2):
        own = refs[at]
        below = refs[at + 1 : at + size]
        above = refs[at + size : at + 2 * size - 1]
        slots.append((own, below, above))
        at += 2 * size - 1
    weights = refs[at : at + steps * chunks]
    at += steps * chunks
    here, there, x_held, w_held, x_sems, w_sems = refs[at:]
    tokens = slots[0][0].shape[1]
    position = place[2]
    piece_rows = w_held.shape[1] // chunks

    def x_copy(ref, clip, away, step):
        block = pl.ds((clip * size + away) * tokens, tokens)
        return pltpu.make_async_copy(ref.at[step], x_held.at[step, block], x_sems.at[step, clip * size + away])

    def w_copy(step, part):
        block = pl.ds(part * piece_rows, piece_rows)
        return pltpu.make_async_copy(weights[step * chunks + part], w_held.at[step, block], w_sems.at[step, part])

    for step in range(steps):
        for part in range(chunks):
            w_copy(step, part).start()
        for clip, (own, below, above) in enumerate(slots):
            x_copy(own, clip, 0, step).start()
            for away in range(1, size):

                @pl.when(position + away < size)
                def _(clip=clip, away=away, step=step, above=above):
                    x_copy(above[away - 1], clip, away, step).start()

                @pl.when(position + away >= size)
                def _(clip=clip, away=away, step=step, below=below):
                    x_copy(below[size - away - 1], clip, away, step).start()

    for step in range(steps):
        for part in range(chunks):
            w_copy(step, part).wait()
        for clip, (own, _, _) in enumerate(slots):
            for away in range(size):
                x_copy(own, clip, away, step).wait()
        rows = size * tokens
        tile = min(rows, 256)
        for clip, out in enumerate((here, there)):

            @pl.loop(0, rows // tile)
            def _(i, clip=clip, out=out, step=step):
                block = pl.ds(pl.multiple_of(i * tile, tile), tile)
                source = pl.ds(pl.multiple_of(clip * rows + i * tile, tile), tile)
                product = jnp.dot(x_held[step, source], w_held[step], preferred_element_type=jnp.float32)
                if step == 0:
                    out[block] = product
                else:
                    out[block] += product


def project(place, lines, weights, chunks, name):
    size = lax.axis_size("head")
    steps = lax.axis_size("step")
    operands = []
    for below, above in lines:
        operands += [below[0]] + below[1:] + above[1:]
    tokens, block = operands[0].shape[1:]
    columns = weights[0].shape[1]
    out = jax.ShapeDtypeStruct((size * tokens, columns), jnp.float32)
    rows = 2 * size * tokens
    return pl.pallas_call(
        functools.partial(project_kernel, size, steps, chunks),
        in_specs=[SMEM] + [ANY] * (len(operands) + len(weights)),
        out_specs=[VMEM, VMEM],
        out_shape=[out, out],
        scratch_shapes=[
            pltpu.VMEM((steps, rows, block), jnp.bfloat16),
            pltpu.VMEM((steps, block, columns), jnp.bfloat16),
            pltpu.SemaphoreType.DMA((steps, 2 * size)),
            pltpu.SemaphoreType.DMA((steps, chunks)),
        ],
        compiler_params=params(),
        cost_estimate=cost(2 * rows * steps * block * columns, 2 * steps * block * (rows + columns) + 4 * rows * columns),
        name=name,
    )(place, *operands, *weights)


def probs_kernel(tokens, size, place, q_a, q_b, k_a, k_b, q_scale, k_scale, q_gain, k_gain, out):
    queries = ((q_a[...] + q_b[...]) * q_scale[...] * q_gain[...]).astype(jnp.bfloat16)
    keys = ((k_a[...] + k_b[...]) * k_scale[...] * k_gain[...]).astype(jnp.bfloat16)
    scores = lax.dot_general(queries, keys, (((1,), (1,)), ((), ())), preferred_element_type=jnp.float32)
    scores = scores * (1.0 / math.sqrt(HD))
    rows = keys.shape[0]
    column = lax.broadcasted_iota(jnp.int32, (1, rows), 1)
    turned = column + place[2] * tokens
    absolute = jnp.where(turned >= rows, turned - rows, turned)
    scores = jnp.where(absolute < place[3], scores, -jnp.inf)
    highest = jnp.max(scores, axis=-1, keepdims=True)
    raised = jnp.exp(scores - highest)
    out[0] = (raised / jnp.sum(raised, axis=-1, keepdims=True)).astype(jnp.bfloat16)


def probabilities(place, q_parts, k_parts, q_scale, k_scale, q_gain, k_gain, size):
    rows, columns = q_parts[0].shape
    heads = columns // HD
    by_head = pl.BlockSpec((rows, HD), lambda i: (0, i))
    gain = pl.BlockSpec((1, HD), lambda i: (0, i))
    per_row = pl.BlockSpec((rows, 1), lambda i: (0, 0))
    return pl.pallas_call(
        functools.partial(probs_kernel, rows // size, size),
        grid=(heads,),
        in_specs=[SMEM] + [by_head] * 4 + [per_row] * 2 + [gain] * 2,
        out_specs=pl.BlockSpec((1, rows, rows), lambda i: (i, 0, 0)),
        out_shape=jax.ShapeDtypeStruct((heads, rows, rows), jnp.bfloat16),
        compiler_params=params(),
        cost_estimate=cost(2 * heads * rows * rows * HD, 16 * rows * columns + 2 * heads * rows * rows, heads * rows * rows),
        name="probs",
    )(place, *q_parts, *k_parts, q_scale, k_scale, q_gain[None], k_gain[None])


def attend_kernel(probs, v_a, v_b, *outs):
    values = (v_a[...] + v_b[...]).astype(jnp.bfloat16)
    attended = jnp.dot(probs[0], values, preferred_element_type=jnp.float32).astype(jnp.bfloat16)
    tokens = outs[0].shape[0]
    for away, out in enumerate(outs):
        out[...] = attended[away * tokens : (away + 1) * tokens]


def attend(probs, v_parts, size):
    heads, rows, _ = probs.shape
    tokens = rows // size
    by_head = pl.BlockSpec((rows, HD), lambda i: (0, i))
    return pl.pallas_call(
        attend_kernel,
        grid=(heads,),
        in_specs=[pl.BlockSpec((1, rows, rows), lambda i: (i, 0, 0)), by_head, by_head],
        out_specs=[pl.BlockSpec((tokens, HD), lambda i: (0, i))] * size,
        out_shape=[jax.ShapeDtypeStruct((tokens, heads * HD), jnp.bfloat16)] * size,
        compiler_params=params(),
        cost_estimate=cost(2 * heads * rows * rows * HD, 2 * heads * rows * rows + 10 * rows * heads * HD),
        name="attend",
    )(probs, *v_parts)


def out_kernel(size, steps, place, coefs, *refs):
    rows_in = refs[: steps * size]
    weights = refs[steps * size : steps * size + 2 * size]
    gates = refs[steps * size + 2 * size]
    at = steps * size + 2 * size + 1
    updates, sums = refs[at : at + steps], refs[at + steps : at + 2 * steps]
    a_held, w_held, total, a_sems, w_sems = refs[at + 2 * steps :]
    tokens = rows_in[0].shape[0]
    width = weights[0].shape[1]
    core = place[1]

    def a_copy(step, away):
        return pltpu.make_async_copy(
            rows_in[step * size + away], a_held.at[away, pl.ds(step * tokens, tokens)], a_sems.at[step, away]
        )

    def w_copy(half, away):
        return pltpu.make_async_copy(
            weights[half * size + away], w_held.at[jnp.bitwise_xor(core, half), away], w_sems.at[half, away]
        )

    for away in range(size):
        for half in range(2):
            w_copy(half, (size - away) % size).start()
        for step in range(steps):
            a_copy(step, away).start()
    for away in range(size):
        for half in range(2):
            w_copy(half, (size - away) % size).wait()
        for step in range(steps):
            a_copy(step, away).wait()
        for half in range(2):
            part = jnp.dot(a_held[away], w_held[half, (size - away) % size], preferred_element_type=jnp.float32)
            part = part.astype(jnp.bfloat16).astype(jnp.float32)
            if away == 0:
                total[half] = part
            else:
                total[half] += part
    for half in range(2):
        columns = slice(half * width, (half + 1) * width)
        branches = []
        for step in range(steps):
            branch = total[half, step * tokens : (step + 1) * tokens] * gates[step : step + 1, columns]
            updates[step][:, columns] = branch.astype(jnp.bfloat16)
            branches.append(branch)
        for step in range(steps):
            reached = branches[0] * coefs[step, 0]
            for other in range(1, steps):
                reached += branches[other] * coefs[step, other]
            sums[step][:, columns] = reached.astype(jnp.bfloat16)


def project_out(place, coefs, gathered, weights, gates):
    steps, size = len(gathered), len(gathered[0])
    tokens, inner = gathered[0][0].shape
    width = weights[0][0].shape[1]
    out = jax.ShapeDtypeStruct((tokens, 2 * width), jnp.bfloat16)
    rows = steps * tokens
    operands = [x for step in gathered for x in step] + [w for half in weights for w in half]
    outs = pl.pallas_call(
        functools.partial(out_kernel, size, steps),
        in_specs=[SMEM, SMEM] + [ANY] * len(operands) + [VMEM],
        out_specs=[VMEM] * (2 * steps),
        out_shape=[out] * (2 * steps),
        scratch_shapes=[
            pltpu.VMEM((size, rows, inner), jnp.bfloat16),
            pltpu.VMEM((2, size, inner, width), jnp.bfloat16),
            pltpu.VMEM((2, rows, width), jnp.float32),
            pltpu.SemaphoreType.DMA((steps, size)),
            pltpu.SemaphoreType.DMA((2, size)),
        ],
        compiler_params=params(),
        cost_estimate=cost(4 * rows * size * inner * width, 2 * size * inner * (rows + 2 * width) + 8 * rows * width),
        name="project_out",
    )(place, coefs, *operands, gates)
    return outs[:steps], outs[steps:]


def finish_kernel(steps, place, base, *refs):
    updates, sums = refs[:steps], refs[steps : 2 * steps]
    reached, update = refs[2 * steps :]
    width = updates[0].shape[1]
    for offset in range(steps):
        at = jnp.bitwise_xor(place[0], offset)
        columns = pl.ds(pl.multiple_of(at * width, width), width)
        reached[:, columns] = base[:, columns] + sums[offset][...].astype(jnp.float32)
        update[:, columns] = updates[offset][...]


def finish(place, base, updates, sums):
    steps = len(updates)
    return pl.pallas_call(
        functools.partial(finish_kernel, steps),
        in_specs=[SMEM] + [VMEM] * (1 + 2 * steps),
        out_specs=[VMEM, VMEM],
        out_shape=[jax.ShapeDtypeStruct(base.shape, jnp.float32), jax.ShapeDtypeStruct(base.shape, jnp.bfloat16)],
        compiler_params=params(),
        cost_estimate=cost(base.size, 14 * base.size),
        name="finish",
    )(place, base, *updates, *sums)


def body(states, timesteps, lengths, modulation, w_query, w_key, w_value, w_out, q_gain, k_gain):
    steps, size = lax.axis_size("step"), lax.axis_size("head")
    step, core, position = (lax.axis_index(axis) for axis in ("step", "fsdp", "head"))
    current = states[0, 0]
    place = jnp.stack([step, core, position, lengths[0]]).astype(jnp.int32)

    q_shards = spread(w_query, 0)
    k_shards = spread(w_key, 1)
    half_rows = w_value.shape[0] // 2
    v_top = spread(w_value[:half_rows], 0)
    v_bottom = spread(w_value[half_rows:], 1)
    v_shards = [piece for pair in zip(v_top, v_bottom) for piece in pair]

    mine, other = modulate(place, current, modulation[0], steps)
    lines = [along_line(mine), along_line(swap(other, "fsdp", 1))]

    def projected(shards, chunks, name):
        here, there = project(place, lines, shards, chunks, name)
        return here, swap(there, "fsdp", 1)

    q_parts = projected(q_shards, 1, "query")
    k_parts = projected(k_shards, 1, "key")
    squares = jnp.stack([jnp.sum(jnp.square(a + b), axis=1) for a, b in (q_parts, k_parts)])
    square_sum = squares
    for away in range(1, size):
        arrived = lax.ppermute(squares, "head", [(i, (i + away) % size) for i in range(size)])
        square_sum = square_sum + jnp.roll(arrived, -away * current.shape[0], axis=1)
    full_width = float(w_query.shape[1] * size)
    scales = lax.rsqrt(square_sum / full_width + 1e-06)[..., None]
    probs = probabilities(place, q_parts, k_parts, scales[0], scales[1], q_gain, k_gain, size)
    v_parts = projected(v_shards, 2, "value")
    attended = attend(probs, v_parts, size)

    pieces = [attended[0]]
    for away in range(1, size):
        pieces.append(lax.ppermute(attended[away], "head", [(i, (i + away) % size) for i in range(size)]))
    gathered = list(zip(*[spread(piece, turn) for turn, piece in enumerate(pieces)]))

    below, above = along_line(w_out)
    own_columns = [w_out] + [
        jnp.where(position + away < size, above[away], below[size - away]) for away in range(1, size)
    ]
    out_weights = (own_columns, [swap(w, "fsdp", 1) for w in own_columns])

    step_width = (timesteps[0, 1] - timesteps[0, 0]).astype(jnp.float32) / 1000.0
    told = jnp.concatenate([modulation[0, 2], jnp.full((HD,), step_width)])[None]
    heard = jnp.concatenate(
        [told] + [lax.ppermute(told, "step", [(i, i ^ o) for i in range(steps)]) for o in range(1, steps)]
    )
    columns = current.shape[1] // steps
    gates = lax.dynamic_slice(heard, (0, step * columns), (steps, columns))
    offsets = jnp.arange(steps, dtype=jnp.int32)
    order = jnp.bitwise_xor(offsets, step)
    coefs = jnp.where(order[None, :] <= order[:, None], heard[:, -1][None, :], 0.0)

    updates, sums = project_out(place, coefs, gathered, out_weights, gates)
    updates = [updates[0]] + [swap(updates[o], "step", o) for o in range(1, steps)]
    sums = [sums[0]] + [swap(sums[o], "step", o) for o in range(1, steps)]

    carried = step_width * current + jnp.where(step == 0, current, jnp.zeros_like(current))
    base, total = carried, carried
    bit = 1
    while bit < steps:
        arrived = swap(total.astype(jnp.bfloat16), "step", bit).astype(jnp.float32)
        base = base + jnp.where(jnp.bitwise_and(step, bit) != 0, arrived, jnp.zeros_like(arrived))
        total = total + arrived
        bit *= 2
    reached, update = finish(place, base, updates, sums)
    return reached[None, None], update[None, None]


def solution(mesh):
    in_specs = (
        P("step", "fsdp", "head", None),
        P("step", None),
        P("fsdp"),
        P("step", None, None),
        P(("step", "fsdp"), "head"),
        P(("step", "fsdp"), "head"),
        P(("step", "fsdp"), "head"),
        P("head", ("step", "fsdp")),
        P("head"),
        P("head"),
    )
    out_specs = (P("step", "fsdp", "head", None), P("step", "fsdp", "head", None))
    return jax.shard_map(body, mesh=mesh, in_specs=in_specs, out_specs=out_specs, check_vma=False)
```

```python
import functools
import math

import jax
import jax.numpy as jnp
from jax import lax
from jax.experimental import pallas as pl
from jax.experimental.pallas import tpu as pltpu
from jax.sharding import PartitionSpec as P

HD = 128
MIB = 1 << 20
SMEM = pl.BlockSpec(memory_space=pltpu.SMEM)
VMEM = pl.BlockSpec(memory_space=pltpu.VMEM)
ANY = pl.BlockSpec(memory_space=pl.ANY)


def swap(x, axis, offset):
    return lax.ppermute(x, axis, [(i, i ^ offset) for i in range(lax.axis_size(axis))])


def spread(x):
    held = [[x]]
    half = x.shape[0] // 2
    for offset in range(1, lax.axis_size("step")):
        low, high = offset & -offset, 1 << (offset.bit_length() - 1)
        if low == high:
            held.append([swap(x, "step", offset)])
            continue
        top, bottom = held[offset ^ low], held[offset ^ high]
        top = top[0][:half] if len(top) == 1 else top[0]
        bottom = bottom[0][half:] if len(bottom) == 1 else bottom[1]
        held.append([swap(top, "step", low), swap(bottom, "step", high)])
    return held


def after(x, *others):
    return lax.optimization_barrier((x,) + others)[0]


def along_line(x):
    size = lax.axis_size("head")
    below, above = [x], [x]
    for hop in range(1, size):
        below.append(lax.ppermute(below[-1], "head", [(i, i + 1) for i in range(hop - 1, size - 1)]))
        above.append(lax.ppermute(above[-1], "head", [(i, i - 1) for i in range(1, size - hop + 1)]))
    return below, above


def params(mib=56):
    return pltpu.CompilerParams(vmem_limit_bytes=mib * MIB)


def cost(flops, moved, raised=0):
    return pl.CostEstimate(flops=int(flops), bytes_accessed=int(moved), transcendentals=int(raised))


def modulate_kernel(place, states, rows, mine, other):
    current = states[...]
    centre = jnp.mean(current, axis=-1, keepdims=True)
    centred = current - centre
    spread_of = jnp.mean(centred * centred, axis=-1, keepdims=True)
    shift, scale = rows[0:1, :], rows[1:2, :]
    modulated = (centred * lax.rsqrt(spread_of + 1e-06) * (1.0 + scale) + shift).astype(jnp.bfloat16)
    steps, _, width = mine.shape
    core = place[1]
    for block in range(2 * steps):
        piece = modulated[:, block * width : (block + 1) * width]

        @pl.when(core == block % 2)
        def _(piece=piece, at=block // 2):
            mine[at] = piece

        @pl.when(core != block % 2)
        def _(piece=piece, at=block // 2):
            other[at] = piece


def modulate(place, states, rows, steps):
    tokens, width = states.shape
    block = width // (2 * steps)
    tile = 32
    out = jax.ShapeDtypeStruct((steps, tokens, block), jnp.bfloat16)
    spec = pl.BlockSpec((steps, tile, block), lambda i: (0, i, 0))
    return pl.pallas_call(
        modulate_kernel,
        grid=(tokens // tile,),
        in_specs=[SMEM, pl.BlockSpec((tile, width), lambda i: (i, 0)), pl.BlockSpec(rows.shape, lambda i: (0, 0))],
        out_specs=[spec, spec],
        out_shape=[out, out],
        compiler_params=params(),
        cost_estimate=cost(10 * tokens * width, 6 * tokens * width),
        name="modulate",
    )(place, states, rows)


def project_kernel(size, parts, layout, place, *refs):
    count = 2 * size - 1
    own, below, above = refs[0], refs[1:size], refs[size:count]
    weights = refs[count : count + len(layout)]
    here, there, x_held, w_held, x_sems, w_sems = refs[count + len(layout) :]
    steps, tokens = own.shape[1:3]
    step_at, position = place[0], place[2]
    low = position < size // 2
    shift = jnp.where(low, 0, 1)
    early = size - 1

    def x_copy(ref, clip, step, block):
        if parts == "first":
            row = (clip * early + block) * tokens
        elif parts == "last":
            row = clip * tokens
        else:
            row = (clip * size + block) * tokens
        return pltpu.make_async_copy(
            ref.at[clip, step], x_held.at[step, pl.ds(pl.multiple_of(row, tokens), tokens)], x_sems.at[step, clip, block]
        )

    def start_weights():
        for index, (ref, (kind, offset, start, rows)) in enumerate(zip(weights, layout)):
            if kind == "whole":
                for step in range(steps):
                    pltpu.make_async_copy(ref.at[pl.ds(step * rows, rows)], w_held.at[step], w_sems.at[step, 0]).start()
            else:
                at = jnp.bitwise_xor(step_at, offset)
                pltpu.make_async_copy(ref, w_held.at[at, pl.ds(start, rows)], w_sems.at[0, index]).start()

    def wait_weights(step):
        for index, (ref, (kind, offset, start, rows)) in enumerate(zip(weights, layout)):
            if kind == "whole":
                pltpu.make_async_copy(ref.at[pl.ds(step * rows, rows)], w_held.at[step], w_sems.at[step, 0]).wait()
            elif step == 0:
                pltpu.make_async_copy(ref, w_held.at[0, pl.ds(start, rows)], w_sems.at[0, index]).wait()

    def start_rows(step):
        for clip in range(2):
            for away in range(size):
                for sign, held in ((1, above), (-1, below)):
                    if away == 0 and sign < 0:
                        continue
                    source = own if away == 0 else held[away - 1]
                    block_at = position + sign * away
                    block = lax.rem(block_at - shift + size, size)
                    inside = jnp.logical_and(block_at >= 0, block_at < size)
                    if parts == "first":
                        inside = jnp.logical_and(inside, block < early)
                    elif parts == "last":
                        inside = jnp.logical_and(inside, block == early)

                    @pl.when(inside)
                    def _(source=source, block=block, clip=clip):
                        x_copy(source, clip, step, block).start()

    blocks = {"first": range(early), "last": range(early, size), "all": range(size)}[parts]
    for step in range(steps):
        start_rows(step)
        if step == 0:
            start_weights()
    half = here.shape[0]
    for step in range(steps):
        wait_weights(step)
        for clip in range(2):
            for block in blocks:
                x_copy(own, clip, step, block).wait()
        product = jnp.dot(x_held[step], w_held[step], preferred_element_type=jnp.float32)
        if step == 0:
            here[...] = product[:half]
            there[...] = product[half:]
        else:
            here[...] += product[:half]
            there[...] += product[half:]


def project(place, line, shards, parts, name):
    size = lax.axis_size("head")
    below, above = line
    operands = [below[0]] + below[1:] + above[1:]
    _, steps, tokens, block = operands[0].shape
    layout, weights = [], []
    for offset, pieces in enumerate(shards):
        start = 0
        for piece in pieces:
            kind = "whole" if len(shards) == 1 else "piece"
            rows = block if kind == "whole" else piece.shape[0]
            layout.append((kind, offset, start, rows))
            weights.append(piece)
            start += rows
    columns = weights[0].shape[1]
    rows = {"first": size - 1, "last": 1, "all": size}[parts] * tokens
    out = jax.ShapeDtypeStruct((rows, columns), jnp.float32)
    return pl.pallas_call(
        functools.partial(project_kernel, size, parts, tuple(layout)),
        in_specs=[SMEM] + [ANY] * (len(operands) + len(weights)),
        out_specs=[VMEM, VMEM],
        out_shape=[out, out],
        scratch_shapes=[
            pltpu.VMEM((steps, 2 * rows, block), jnp.bfloat16),
            pltpu.VMEM((steps, block, columns), jnp.bfloat16),
            pltpu.SemaphoreType.DMA((steps, 2, size)),
            pltpu.SemaphoreType.DMA((steps, len(layout))),
        ],
        compiler_params=params(),
        cost_estimate=cost(4 * rows * steps * block * columns, 2 * steps * block * (2 * rows + columns) + 8 * rows * columns),
        name=name,
    )(place, *operands, *weights)


def probs_kernel(tokens, place, *refs):
    parts, (q_scale, k_scale, q_gain, k_gain, out) = refs[:8], refs[8:]
    joined = [jnp.concatenate([parts[i][...] + parts[i + 1][...], parts[i + 2][...] + parts[i + 3][...]]) for i in (0, 4)]
    queries = (joined[0] * q_scale[...] * q_gain[...]).astype(jnp.bfloat16)
    keys = (joined[1] * k_scale[...] * k_gain[...]).astype(jnp.bfloat16)
    scores = lax.dot_general(queries, keys, (((1,), (1,)), ((), ())), preferred_element_type=jnp.float32)
    scores = scores * (1.0 / math.sqrt(HD))
    rows = keys.shape[0]
    turned = lax.broadcasted_iota(jnp.int32, (1, rows), 1) + place[4] * tokens
    absolute = jnp.where(turned >= rows, turned - rows, turned)
    scores = jnp.where(absolute < place[3], scores, -jnp.inf)
    highest = jnp.max(scores, axis=-1, keepdims=True)
    raised = jnp.exp(scores - highest)
    out[0] = (raised / jnp.sum(raised, axis=-1, keepdims=True)).astype(jnp.bfloat16)


def probabilities(place, q_parts, k_parts, q_scale, k_scale, q_gain, k_gain):
    columns = q_parts[0].shape[1]
    rows = q_parts[0].shape[0] + q_parts[2].shape[0]
    heads = columns // HD
    by_head = [pl.BlockSpec((part.shape[0], HD), lambda i: (0, i)) for part in q_parts + k_parts]
    gain = pl.BlockSpec((1, HD), lambda i: (0, i))
    per_row = pl.BlockSpec((rows, 1), lambda i: (0, 0))
    return pl.pallas_call(
        functools.partial(probs_kernel, q_parts[2].shape[0]),
        grid=(heads,),
        in_specs=[SMEM] + by_head + [per_row] * 2 + [gain] * 2,
        out_specs=pl.BlockSpec((1, rows, rows), lambda i: (i, 0, 0)),
        out_shape=jax.ShapeDtypeStruct((heads, rows, rows), jnp.bfloat16),
        compiler_params=params(),
        cost_estimate=cost(2 * heads * rows * rows * HD, 16 * rows * columns + 2 * heads * rows * rows, heads * rows * rows),
        name="probs",
    )(place, *q_parts, *k_parts, q_scale, k_scale, q_gain[None], k_gain[None])


def attend_kernel(place, probs, v_a, v_b, out, held):
    values = (v_a[...] + v_b[...]).astype(jnp.bfloat16)
    held[...] = jnp.dot(probs[0], values, preferred_element_type=jnp.float32)
    size, tokens, _ = out.shape
    for block in range(size):
        at = lax.rem(block - place[4] + size, size) * tokens
        out[block] = held[pl.ds(pl.multiple_of(at, tokens), tokens)].astype(jnp.bfloat16)


def attend(place, probs, v_parts, size):
    heads, rows, _ = probs.shape
    tokens = rows // size
    by_head = pl.BlockSpec((rows, HD), lambda i: (0, i))
    return pl.pallas_call(
        attend_kernel,
        grid=(heads,),
        in_specs=[SMEM, pl.BlockSpec((1, rows, rows), lambda i: (i, 0, 0)), by_head, by_head],
        out_specs=pl.BlockSpec((size, tokens, HD), lambda i: (0, 0, i)),
        out_shape=jax.ShapeDtypeStruct((size, tokens, heads * HD), jnp.bfloat16),
        scratch_shapes=[pltpu.VMEM((rows, HD), jnp.float32)],
        compiler_params=params(),
        cost_estimate=cost(2 * heads * rows * rows * HD, 2 * heads * rows * rows + 10 * rows * heads * HD),
        name="attend",
    )(place, probs, *v_parts)


def out_kernel(size, layout, place, widths, *refs):
    pieces, weights = refs[: len(layout)], refs[len(layout) : len(layout) + 2 * size]
    gates, out, a_held, w_held, total, a_sems, w_sems = refs[len(layout) + 2 * size :]
    steps, _, tokens, columns = out.shape
    width = columns // 2
    step_at, core, position = place[0], place[1], place[2]

    def a_copies():
        for index, (offset, start, count) in enumerate(layout):
            row = pl.multiple_of(jnp.bitwise_xor(step_at, offset) * tokens, tokens)
            for group in range(count):
                yield pltpu.make_async_copy(
                    pieces[index].at[group], a_held.at[start + group, pl.ds(row, tokens)], a_sems.at[index, group]
                )

    def w_copy(half, away):
        group = lax.rem(position + away, size)
        return pltpu.make_async_copy(
            weights[half * size + away], w_held.at[jnp.bitwise_xor(core, half), group], w_sems.at[half, away]
        )

    for copy in a_copies():
        copy.start()
    for away in range(size):
        for half in range(2):
            w_copy(half, away).start()
    for copy in a_copies():
        copy.wait()
    for away in range(size):
        group = lax.rem(position + away, size)
        for half in range(2):
            w_copy(half, away).wait()
        for half in range(2):
            part = jnp.dot(a_held[group], w_held[half, group], preferred_element_type=jnp.float32)
            part = part.astype(jnp.bfloat16).astype(jnp.float32)
            if away == 0:
                total[half] = part
            else:
                total[half] += part
    for half in range(2):
        span = slice(half * width, (half + 1) * width)
        reached = None
        for step in range(steps):
            told = jnp.bitwise_xor(step_at, step)
            branch = total[half, step * tokens : (step + 1) * tokens] * gates[pl.ds(told, 1), span]
            out[step, 0, :, span] = branch.astype(jnp.bfloat16)
            drift = branch * widths[told]
            reached = drift if step == 0 else reached + drift
            out[step, 1, :, span] = reached.astype(jnp.bfloat16)


def project_out(place, widths, gathered, weights, gates):
    size = lax.axis_size("head")
    steps = len(gathered)
    _, tokens, inner = gathered[0][0].shape
    width = weights[0][0].shape[1]
    layout, pieces = [], []
    for offset, held in enumerate(gathered):
        start = 0
        for piece in held:
            layout.append((offset, start, piece.shape[0]))
            pieces.append(piece)
            start += piece.shape[0]
    rows = steps * tokens
    operands = pieces + [w for half in weights for w in half]
    return pl.pallas_call(
        functools.partial(out_kernel, size, tuple(layout)),
        in_specs=[SMEM, SMEM] + [ANY] * len(operands) + [VMEM],
        out_specs=VMEM,
        out_shape=jax.ShapeDtypeStruct((steps, 2, tokens, 2 * width), jnp.bfloat16),
        scratch_shapes=[
            pltpu.VMEM((size, rows, inner), jnp.bfloat16),
            pltpu.VMEM((2, size, inner, width), jnp.bfloat16),
            pltpu.VMEM((2, rows, width), jnp.float32),
            pltpu.SemaphoreType.DMA((len(layout), size)),
            pltpu.SemaphoreType.DMA((2, size)),
        ],
        compiler_params=params(),
        cost_estimate=cost(4 * rows * size * inner * width, 2 * size * inner * (rows + 2 * width) + 8 * rows * width),
        name="project_out",
    )(place, widths, *operands, gates)


def finish_kernel(base, arrived, reached, update):
    reached[...] = base[...] + arrived[0, 1].astype(jnp.float32)
    update[...] = arrived[0, 0]


def finish(base, arrived):
    steps, _, tokens, width = arrived.shape
    by_columns = pl.BlockSpec((tokens, width), lambda i: (0, i))
    return pl.pallas_call(
        finish_kernel,
        grid=(steps,),
        in_specs=[by_columns, pl.BlockSpec((1, 2, tokens, width), lambda i: (i, 0, 0, 0))],
        out_specs=[by_columns, by_columns],
        out_shape=[jax.ShapeDtypeStruct(base.shape, jnp.float32), jax.ShapeDtypeStruct(base.shape, jnp.bfloat16)],
        compiler_params=params(),
        cost_estimate=cost(base.size, 14 * base.size),
        name="finish",
    )(base, arrived)


def body(states, timesteps, lengths, modulation, w_query, w_key, w_value, w_out, q_gain, k_gain):
    steps, size = lax.axis_size("step"), lax.axis_size("head")
    step, core, position = (lax.axis_index(axis) for axis in ("step", "fsdp", "head"))
    current = states[0, 0]
    tokens = current.shape[0]
    shift = (position >= size // 2).astype(jnp.int32)
    place = jnp.stack([step, core, position, lengths[0], shift]).astype(jnp.int32)

    mine, other = modulate(place, current, modulation[0], steps)
    line = along_line(jnp.stack([mine, swap(other, "fsdp", 1)]))

    q_shards = [[lax.all_gather(w_query, "step", axis=0, tiled=True)]]
    k_shards = spread(w_key)
    v_shards = [[lax.all_gather(w_value, "step", axis=0, tiled=True)]]

    def projected(shards, parts, name):
        here, there = project(place, line, shards, parts, name)
        return [here, swap(there, "fsdp", 1)]

    def early(held):
        return held[: size - 1]

    whole_line, line = line, tuple(early(held) + [held[0]] for held in line)
    q_parts = projected(q_shards, "first", "query")
    k_parts = projected(k_shards, "first", "key")
    line = whole_line
    q_parts = q_parts + projected(q_shards, "last", "query_last")
    k_parts = k_parts + projected(k_shards, "last", "key_last")

    def squares_of(parts):
        return jnp.concatenate([jnp.sum(jnp.square(parts[i] + parts[i + 1]), axis=1) for i in (0, 2)])

    squares = jnp.stack([squares_of(q_parts), squares_of(k_parts)])
    squares = jnp.where(shift == 0, squares, jnp.roll(squares, tokens, axis=1))
    square_sum = squares
    for away in range(1, size):
        square_sum = square_sum + lax.ppermute(squares, "head", [(i, (i + away) % size) for i in range(size)])
    square_sum = jnp.where(shift == 0, square_sum, jnp.roll(square_sum, -tokens, axis=1))
    full_width = float(w_query.shape[1] * size)
    scales = lax.rsqrt(square_sum / full_width + 1e-06)[..., None]
    probs = probabilities(place, q_parts, k_parts, scales[0], scales[1], q_gain, k_gain)
    v_parts = projected(v_shards, "all", "value")
    attended = attend(place, probs, v_parts, size)

    gathered = spread(lax.all_to_all(attended, "head", 0, 0))

    below, above = along_line(after(w_out, line[0][-1], line[1][-1]))
    own_columns = [w_out] + [
        jnp.where(position + away < size, above[away], below[size - away]) for away in range(1, size)
    ]
    out_weights = (own_columns, [swap(w, "fsdp", 1) for w in own_columns])

    step_width = (timesteps[0, 1] - timesteps[0, 0]).astype(jnp.float32) / 1000.0
    told = jnp.concatenate([modulation[0, 2], jnp.full((HD,), step_width)])[None]
    heard = jnp.concatenate([told] + [swap(told, "step", offset) for offset in range(1, steps)])
    columns = current.shape[1] // steps
    gates = lax.dynamic_slice(heard, (0, step * columns), (steps, columns))

    sent = project_out(place, heard[:, -1], gathered, out_weights, gates)
    arrived = lax.all_to_all(sent, "step", 0, 0)

    carried = step_width * current + jnp.where(step == 0, current, jnp.zeros_like(current))
    base, total = carried, carried
    bit = 1
    while bit < steps:
        brought = swap(total.astype(jnp.bfloat16), "step", bit).astype(jnp.float32)
        base = base + jnp.where(jnp.bitwise_and(step, bit) != 0, brought, jnp.zeros_like(brought))
        total = total + brought
        bit *= 2
    reached, update = finish(base, arrived)
    return reached[None, None], update[None, None]


def solution(mesh):
    in_specs = (
        P("step", "fsdp", "head", None),
        P("step", None),
        P("fsdp"),
        P("step", None, None),
        P(("step", "fsdp"), "head"),
        P(("step", "fsdp"), "head"),
        P(("step", "fsdp"), "head"),
        P("head", ("step", "fsdp")),
        P("head"),
        P("head"),
    )
    out_specs = (P("step", "fsdp", "head", None), P("step", "fsdp", "head", None))
    return jax.shard_map(body, mesh=mesh, in_specs=in_specs, out_specs=out_specs, check_vma=False)
```

```python
import functools
import math

import jax
import jax.numpy as jnp
from jax import lax
from jax.experimental import pallas as pl
from jax.experimental.pallas import tpu as pltpu
from jax.sharding import PartitionSpec as P

HD = 128
MIB = 1 << 20
SMEM = pl.BlockSpec(memory_space=pltpu.SMEM)
VMEM = pl.BlockSpec(memory_space=pltpu.VMEM)
ANY = pl.BlockSpec(memory_space=pl.ANY)


def swap(x, axis, offset):
    return lax.ppermute(x, axis, [(i, i ^ offset) for i in range(lax.axis_size(axis))])


def spread(x):
    held = [[x]]
    half = x.shape[0] // 2
    for offset in range(1, lax.axis_size("step")):
        low, high = offset & -offset, 1 << (offset.bit_length() - 1)
        if low == high:
            held.append([swap(x, "step", offset)])
            continue
        top, bottom = held[offset ^ low], held[offset ^ high]
        top = top[0][:half] if len(top) == 1 else top[0]
        bottom = bottom[0][half:] if len(bottom) == 1 else bottom[1]
        held.append([swap(top, "step", low), swap(bottom, "step", high)])
    return held


def after(x, *others):
    return lax.optimization_barrier((x,) + others)[0]


def along_line(x, awaited=()):
    size = lax.axis_size("head")
    below, above = [x], [x]
    for hop in range(1, size):
        up, down = below[-1], above[-1]
        if 0 <= hop - 2 < len(awaited):
            up, down = after((up, down), *awaited[hop - 2])
        below.append(lax.ppermute(up, "head", [(i, i + 1) for i in range(hop - 1, size - 1)]))
        above.append(lax.ppermute(down, "head", [(i, i - 1) for i in range(1, size - hop + 1)]))
    return below, above


def params(mib=56):
    return pltpu.CompilerParams(vmem_limit_bytes=mib * MIB)


def cost(flops, moved, raised=0):
    return pl.CostEstimate(flops=int(flops), bytes_accessed=int(moved), transcendentals=int(raised))


def modulate_kernel(steps, place, states, rows, mine, other):
    current = states[...]
    centre = jnp.mean(current, axis=-1, keepdims=True)
    centred = current - centre
    spread_of = jnp.mean(centred * centred, axis=-1, keepdims=True)
    shift, scale = rows[0:1, :], rows[1:2, :]
    modulated = (centred * lax.rsqrt(spread_of + 1e-06) * (1.0 + scale) + shift).astype(jnp.bfloat16)
    core = place[1]
    for block in range(2 * steps):
        width = modulated.shape[1] // (2 * steps)
        piece = modulated[:, block * width : (block + 1) * width]
        at = slice(block // 2 * width, (block // 2 + 1) * width)

        @pl.when(core == block % 2)
        def _(piece=piece, at=at):
            mine[:, at] = piece

        @pl.when(core != block % 2)
        def _(piece=piece, at=at):
            other[:, at] = piece


def modulate(place, states, rows, steps):
    tokens, width = states.shape
    tile = 32
    out = jax.ShapeDtypeStruct((tokens, width // 2), jnp.bfloat16)
    spec = pl.BlockSpec((tile, width // 2), lambda i: (i, 0))
    return pl.pallas_call(
        functools.partial(modulate_kernel, steps),
        grid=(tokens // tile,),
        in_specs=[SMEM, pl.BlockSpec((tile, width), lambda i: (i, 0)), pl.BlockSpec(rows.shape, lambda i: (0, 0))],
        out_specs=[spec, spec],
        out_shape=[out, out],
        compiler_params=params(),
        cost_estimate=cost(10 * tokens * width, 6 * tokens * width),
        name="modulate",
    )(place, states, rows)


def project_kernel(size, parts, layout, place, *refs):
    count = 2 * size - 1
    own, below, above = refs[0], refs[1:size], refs[size:count]
    weights = refs[count : count + len(layout)]
    here, there, x_held, w_held, x_sems, w_sems = refs[count + len(layout) :]
    tokens, depth = own.shape[1:]
    half = depth // 2
    step_at, position = place[0], place[2]
    shift = place[4]
    early = size - 1
    blocks = {"first": range(early), "last": range(early, size), "all": range(size)}[parts]

    def x_copy(ref, clip, part, block):
        row = (clip * len(blocks) + block - blocks[0]) * tokens
        rows, columns = pl.ds(pl.multiple_of(row, tokens), tokens), pl.ds(part * half, half)
        return pltpu.make_async_copy(ref.at[clip, :, columns], x_held.at[rows, columns], x_sems.at[part, clip, block])

    def w_copies(part):
        if len(layout) == 1:
            rows = pl.ds(part * half, half)
            yield pltpu.make_async_copy(weights[0].at[rows], w_held.at[rows], w_sems.at[0, part])
        elif part == 0:
            for index, (ref, (offset, whole, start, rows)) in enumerate(zip(weights, layout)):
                at = jnp.bitwise_xor(step_at, offset) * whole + start
                target = w_held.at[pl.ds(pl.multiple_of(at, rows), rows)]
                yield pltpu.make_async_copy(ref, target, w_sems.at[1, index])

    for part in range(2):
        for copy in w_copies(part):
            copy.start()
        for clip in range(2):
            for away in range(size):
                for sign, held in ((1, above), (-1, below)):
                    if away == 0 and sign < 0:
                        continue
                    source = own if away == 0 else held[away - 1]
                    block_at = position + sign * away
                    block = lax.rem(block_at - shift + size, size)
                    inside = jnp.logical_and(block_at >= 0, block_at < size)
                    inside = jnp.logical_and(inside, jnp.logical_and(block >= blocks[0], block <= blocks[-1]))

                    @pl.when(inside)
                    def _(source=source, block=block, clip=clip, part=part):
                        x_copy(source, clip, part, block).start()

    rows = here.shape[0]
    for part in range(2):
        for copy in w_copies(part):
            copy.wait()
        for clip in range(2):
            for block in blocks:
                x_copy(own, clip, part, block).wait()
        span = slice(part * half, (part + 1) * half)
        product = jnp.dot(x_held[:, span], w_held[span], preferred_element_type=jnp.float32)
        if part == 0:
            here[...] = product[:rows]
            there[...] = product[rows:]
        else:
            here[...] += product[:rows]
            there[...] += product[rows:]


def project(place, line, shards, parts, name):
    size = lax.axis_size("head")
    below, above = line
    operands = [below[0]] + below[1:] + above[1:]
    _, tokens, depth = operands[0].shape
    layout, weights = [], []
    for offset, pieces in enumerate(shards):
        start = 0
        for piece in pieces:
            layout.append((offset, depth // len(shards), start, piece.shape[0]))
            weights.append(piece)
            start += piece.shape[0]
    columns = weights[0].shape[1]
    rows = {"first": size - 1, "last": 1, "all": size}[parts] * tokens
    out = jax.ShapeDtypeStruct((rows, columns), jnp.float32)
    return pl.pallas_call(
        functools.partial(project_kernel, size, parts, tuple(layout)),
        in_specs=[SMEM] + [ANY] * (len(operands) + len(weights)),
        out_specs=[VMEM, VMEM],
        out_shape=[out, out],
        scratch_shapes=[
            pltpu.VMEM((2 * rows, depth), jnp.bfloat16),
            pltpu.VMEM((depth, columns), jnp.bfloat16),
            pltpu.SemaphoreType.DMA((2, 2, size)),
            pltpu.SemaphoreType.DMA((2, max(2, len(layout)))),
        ],
        compiler_params=params(),
        cost_estimate=cost(4 * rows * depth * columns, 2 * depth * (2 * rows + columns) + 8 * rows * columns),
        name=name,
    )(place, *operands, *weights)


def probs_kernel(tokens, place, *refs):
    parts, (q_scale, k_scale, q_gain, k_gain, out) = refs[:8], refs[8:]
    joined = [jnp.concatenate([parts[i][...] + parts[i + 1][...], parts[i + 2][...] + parts[i + 3][...]]) for i in (0, 4)]
    queries = (joined[0] * q_scale[...] * q_gain[...]).astype(jnp.bfloat16)
    keys = (joined[1] * k_scale[...] * k_gain[...]).astype(jnp.bfloat16)
    scores = lax.dot_general(queries, keys, (((1,), (1,)), ((), ())), preferred_element_type=jnp.float32)
    scores = scores * (1.0 / math.sqrt(HD))
    rows = keys.shape[0]
    turned = lax.broadcasted_iota(jnp.int32, (1, rows), 1) + place[4] * tokens
    absolute = jnp.where(turned >= rows, turned - rows, turned)
    scores = jnp.where(absolute < place[3], scores, -jnp.inf)
    highest = jnp.max(scores, axis=-1, keepdims=True)
    raised = jnp.exp(scores - highest)
    out[0] = (raised / jnp.sum(raised, axis=-1, keepdims=True)).astype(jnp.bfloat16)


def probabilities(place, q_parts, k_parts, q_scale, k_scale, q_gain, k_gain):
    columns = q_parts[0].shape[1]
    rows = q_parts[0].shape[0] + q_parts[2].shape[0]
    heads = columns // HD
    by_head = [pl.BlockSpec((part.shape[0], HD), lambda i: (0, i)) for part in q_parts + k_parts]
    gain = pl.BlockSpec((1, HD), lambda i: (0, i))
    per_row = pl.BlockSpec((rows, 1), lambda i: (0, 0))
    return pl.pallas_call(
        functools.partial(probs_kernel, q_parts[2].shape[0]),
        grid=(heads,),
        in_specs=[SMEM] + by_head + [per_row] * 2 + [gain] * 2,
        out_specs=pl.BlockSpec((1, rows, rows), lambda i: (i, 0, 0)),
        out_shape=jax.ShapeDtypeStruct((heads, rows, rows), jnp.bfloat16),
        compiler_params=params(),
        cost_estimate=cost(2 * heads * rows * rows * HD, 16 * rows * columns + 2 * heads * rows * rows, heads * rows * rows),
        name="probs",
    )(place, *q_parts, *k_parts, q_scale, k_scale, q_gain[None], k_gain[None])


def attend_kernel(place, probs, v_a, v_b, out, held):
    values = (v_a[...] + v_b[...]).astype(jnp.bfloat16)
    held[...] = jnp.dot(probs[0], values, preferred_element_type=jnp.float32)
    size, tokens, _ = out.shape
    for block in range(size):
        at = lax.rem(block - place[4] + size, size) * tokens
        out[block] = held[pl.ds(pl.multiple_of(at, tokens), tokens)].astype(jnp.bfloat16)


def attend(place, probs, v_parts, size):
    heads, rows, _ = probs.shape
    tokens = rows // size
    by_head = pl.BlockSpec((rows, HD), lambda i: (0, i))
    return pl.pallas_call(
        attend_kernel,
        grid=(heads,),
        in_specs=[SMEM, pl.BlockSpec((1, rows, rows), lambda i: (i, 0, 0)), by_head, by_head],
        out_specs=pl.BlockSpec((size, tokens, HD), lambda i: (0, 0, i)),
        out_shape=jax.ShapeDtypeStruct((size, tokens, heads * HD), jnp.bfloat16),
        scratch_shapes=[pltpu.VMEM((rows, HD), jnp.float32)],
        compiler_params=params(),
        cost_estimate=cost(2 * heads * rows * rows * HD, 2 * heads * rows * rows + 10 * rows * heads * HD),
        name="attend",
    )(place, probs, *v_parts)


def out_kernel(size, layout, place, widths, *refs):
    pieces, weights = refs[: len(layout)], refs[len(layout) : len(layout) + 2 * size]
    gates, out, a_held, w_held, total, a_sems, w_sems = refs[len(layout) + 2 * size :]
    steps, _, tokens, columns = out.shape
    width = columns // 2
    halves, _, _, span_width = w_held.shape
    joined = halves == 1
    step_at, core, position = place[0], place[1], place[2]

    def a_copies():
        for index, (offset, start, count) in enumerate(layout):
            row = pl.multiple_of(jnp.bitwise_xor(step_at, offset) * tokens, tokens)
            for group in range(count):
                yield pltpu.make_async_copy(
                    pieces[index].at[group], a_held.at[start + group, pl.ds(row, tokens)], a_sems.at[index, group]
                )

    def w_copy(half, away):
        group = lax.rem(position + away, size)
        at = jnp.bitwise_xor(core, half)
        if joined:
            span = pl.ds(pl.multiple_of(at * width, 128), width)
            target = w_held.at[0, group, :, span]
        else:
            target = w_held.at[at, group]
        return pltpu.make_async_copy(weights[half * size + away], target, w_sems.at[half, away])

    for copy in a_copies():
        copy.start()
    for away in range(size):
        for half in range(2):
            w_copy(half, away).start()
    for copy in a_copies():
        copy.wait()
    for away in range(size):
        group = lax.rem(position + away, size)
        for half in range(2):
            w_copy(half, away).wait()
        for half in range(halves):
            part = jnp.dot(a_held[group], w_held[half, group], preferred_element_type=jnp.float32)
            part = part.astype(jnp.bfloat16).astype(jnp.float32)
            if away == 0:
                total[half] = part
            else:
                total[half] += part
    for half in range(halves):
        span = slice(half * span_width, (half + 1) * span_width)
        reached = None
        for step in range(steps):
            branch = total[half, step * tokens : (step + 1) * tokens] * gates[step : step + 1, span]
            out[step, 0, :, span] = branch.astype(jnp.bfloat16)
            drift = branch * widths[step]
            reached = drift if step == 0 else reached + drift
            out[step, 1, :, span] = reached.astype(jnp.bfloat16)


def project_out(place, widths, gathered, weights, gates):
    size = lax.axis_size("head")
    steps = len(gathered)
    _, tokens, inner = gathered[0][0].shape
    width = weights[0][0].shape[1]
    layout, pieces = [], []
    for offset, held in enumerate(gathered):
        start = 0
        for piece in held:
            layout.append((offset, start, piece.shape[0]))
            pieces.append(piece)
            start += piece.shape[0]
    rows = steps * tokens
    halves = 1 if width % 128 == 0 else 2
    operands = pieces + [w for half in weights for w in half]
    return pl.pallas_call(
        functools.partial(out_kernel, size, tuple(layout)),
        in_specs=[SMEM, SMEM] + [ANY] * len(operands) + [VMEM],
        out_specs=VMEM,
        out_shape=jax.ShapeDtypeStruct((steps, 2, tokens, 2 * width), jnp.bfloat16),
        scratch_shapes=[
            pltpu.VMEM((size, rows, inner), jnp.bfloat16),
            pltpu.VMEM((halves, size, inner, 2 * width // halves), jnp.bfloat16),
            pltpu.VMEM((halves, rows, 2 * width // halves), jnp.float32),
            pltpu.SemaphoreType.DMA((len(layout), size)),
            pltpu.SemaphoreType.DMA((2, size)),
        ],
        compiler_params=params(),
        cost_estimate=cost(4 * rows * size * inner * width, 2 * size * inner * (rows + 2 * width) + 8 * rows * width),
        name="project_out",
    )(place, widths, *operands, gates)


def finish_kernel(base, arrived, reached, update):
    reached[...] = base[...] + arrived[0, 1].astype(jnp.float32)
    update[...] = arrived[0, 0]


def finish(base, arrived):
    steps, _, tokens, width = arrived.shape
    by_columns = pl.BlockSpec((tokens, width), lambda i: (0, i))
    return pl.pallas_call(
        finish_kernel,
        grid=(steps,),
        in_specs=[by_columns, pl.BlockSpec((1, 2, tokens, width), lambda i: (i, 0, 0, 0))],
        out_specs=[by_columns, by_columns],
        out_shape=[jax.ShapeDtypeStruct(base.shape, jnp.float32), jax.ShapeDtypeStruct(base.shape, jnp.bfloat16)],
        compiler_params=params(),
        cost_estimate=cost(base.size, 14 * base.size),
        name="finish",
    )(base, arrived)


def body(states, timesteps, lengths, modulation, w_query, w_key, w_value, w_out, q_gain, k_gain):
    steps, size = lax.axis_size("step"), lax.axis_size("head")
    step, core, position = (lax.axis_index(axis) for axis in ("step", "fsdp", "head"))
    current = states[0, 0]
    tokens = current.shape[0]
    shift = (position >= size // 2).astype(jnp.int32)
    place = jnp.stack([step, core, position, lengths[0], shift]).astype(jnp.int32)

    columns = current.shape[1] // steps
    step_width = (timesteps[0, 1] - timesteps[0, 0]).astype(jnp.float32) / 1000.0
    told = jnp.concatenate([modulation[0, 2].reshape(steps, columns), jnp.full((steps, HD), step_width)], axis=1)
    heard = lax.all_to_all(told, "step", 0, 0)
    gates, widths = heard[:, :columns], heard[:, columns]

    q_shards = [[lax.all_gather(w_query, "step", axis=0, tiled=True)]]
    k_shards = spread(w_key)

    mine, other = modulate(place, current, modulation[0], steps)
    direct = [piece for held in k_shards for piece in held if piece.shape == w_key.shape]
    forwarded = [piece for held in k_shards for piece in held if piece.shape != w_key.shape]
    line = along_line(jnp.stack([mine, swap(other, "fsdp", 1)]), (direct + [heard], forwarded))
    v_shards = [[lax.all_gather(w_value, "step", axis=0, tiled=True)]]

    def projected(shards, parts, name):
        here, there = project(place, line, shards, parts, name)
        return [here, swap(there, "fsdp", 1)]

    def early(held):
        return held[: size - 1]

    whole_line, line = line, tuple(early(held) + [held[0]] for held in line)
    q_parts = projected(q_shards, "first", "query")
    k_parts = projected(k_shards, "first", "key")
    line = whole_line
    q_parts = q_parts + projected(q_shards, "last", "query_last")
    k_parts = k_parts + projected(k_shards, "last", "key_last")

    def squares_of(parts):
        return jnp.concatenate([jnp.sum(jnp.square(parts[i] + parts[i + 1]), axis=1) for i in (0, 2)])

    squares = jnp.stack([squares_of(q_parts), squares_of(k_parts)])
    squares = jnp.where(shift == 0, squares, jnp.roll(squares, tokens, axis=1))
    square_sum = jnp.sum(lax.all_to_all(jnp.broadcast_to(squares[None], (size,) + squares.shape), "head", 0, 0), axis=0)
    square_sum = jnp.where(shift == 0, square_sum, jnp.roll(square_sum, -tokens, axis=1))
    full_width = float(w_query.shape[1] * size)
    scales = lax.rsqrt(square_sum / full_width + 1e-06)[..., None]
    probs = probabilities(place, q_parts, k_parts, scales[0], scales[1], q_gain, k_gain)
    v_parts = projected(v_shards, "all", "value")
    attended = attend(place, probs, v_parts, size)

    gathered = spread(lax.all_to_all(attended, "head", 0, 0))

    below, above = along_line(after(w_out, line[0][-1], line[1][-1], q_parts[0], k_parts[0]))
    own_columns = [w_out] + [
        jnp.where(position + away < size, above[away], below[size - away]) for away in range(1, size)
    ]
    out_weights = (own_columns, [swap(w, "fsdp", 1) for w in own_columns])

    sent = project_out(place, widths, gathered, out_weights, gates)
    arrived = lax.all_to_all(sent, "step", 0, 0)

    carried = step_width * current + jnp.where(step == 0, current, jnp.zeros_like(current))
    base, total = carried, carried
    bit = 1
    while bit < steps:
        brought = swap(after(total.astype(jnp.bfloat16), v_shards[0][0]), "step", bit).astype(jnp.float32)
        base = base + jnp.where(jnp.bitwise_and(step, bit) != 0, brought, jnp.zeros_like(brought))
        total = total + brought
        bit *= 2
    reached, update = finish(base, arrived)
    return reached[None, None], update[None, None]


def solution(mesh):
    in_specs = (
        P("step", "fsdp", "head", None),
        P("step", None),
        P("fsdp"),
        P("step", None, None),
        P(("step", "fsdp"), "head"),
        P(("step", "fsdp"), "head"),
        P(("step", "fsdp"), "head"),
        P("head", ("step", "fsdp")),
        P("head"),
        P("head"),
    )
    out_specs = (P("step", "fsdp", "head", None), P("step", "fsdp", "head", None))
    return jax.shard_map(body, mesh=mesh, in_specs=in_specs, out_specs=out_specs, check_vma=False)
```

```python
import functools
import math

import jax
import jax.numpy as jnp
from jax import lax
from jax.experimental import pallas as pl
from jax.experimental.pallas import tpu as pltpu
from jax.sharding import PartitionSpec as P

HD = 128
MIB = 1 << 20
SMEM = pl.BlockSpec(memory_space=pltpu.SMEM)
VMEM = pl.BlockSpec(memory_space=pltpu.VMEM)
ANY = pl.BlockSpec(memory_space=pl.ANY)


def swap(x, axis, offset):
    return lax.ppermute(x, axis, [(i, i ^ offset) for i in range(lax.axis_size(axis))])


def bits_of(axis):
    return [1 << bit for bit in range(lax.axis_size(axis).bit_length() - 1)]


def direct(x):
    return {bit: [swap(x, "step", bit)] for bit in bits_of("step")}


def forwarded(x, near, turn=None):
    held = {0: [x], **near}
    half = x.shape[0] // 2
    for offset in range(1, lax.axis_size("step")):
        low, high = offset & -offset, 1 << (offset.bit_length() - 1)
        if offset in held:
            continue
        if turn is not None:
            last = (low, high)[turn]
            held[offset] = [swap(held[offset ^ last][0], "step", last)]
            continue
        top, bottom = held[offset ^ low], held[offset ^ high]
        top = top[0][:half] if len(top) == 1 else top[0]
        bottom = bottom[0][half:] if len(bottom) == 1 else bottom[1]
        held[offset] = [swap(top, "step", low), swap(bottom, "step", high)]
    return [held[offset] for offset in range(lax.axis_size("step"))]


def listed(held):
    return [piece for pieces in (held.values() if isinstance(held, dict) else held) for piece in pieces]


def after(x, *others):
    return lax.optimization_barrier((x,) + others)[0]


def along_line(x, awaited=()):
    size = lax.axis_size("head")
    below, above = [x], [x]
    for hop in range(1, size):
        up, down = below[-1], above[-1]
        if 0 <= hop - 2 < len(awaited):
            up, down = after((up, down), *awaited[hop - 2])
        below.append(lax.ppermute(up, "head", [(i, i + 1) for i in range(hop - 1, size - 1)]))
        above.append(lax.ppermute(down, "head", [(i, i - 1) for i in range(1, size - hop + 1)]))
    return below, above


def params(mib=56):
    return pltpu.CompilerParams(vmem_limit_bytes=mib * MIB)


def cost(flops, moved, raised=0):
    return pl.CostEstimate(flops=int(flops) // 4, bytes_accessed=int(moved) // 4, transcendentals=int(raised) // 4)


def modulate_kernel(steps, place, states, rows, mine, other):
    current = states[...]
    centre = jnp.mean(current, axis=-1, keepdims=True)
    centred = current - centre
    spread_of = jnp.mean(centred * centred, axis=-1, keepdims=True)
    shift, scale = rows[0:1, :], rows[1:2, :]
    modulated = (centred * lax.rsqrt(spread_of + 1e-06) * (1.0 + scale) + shift).astype(jnp.bfloat16)
    core = place[1]
    for block in range(2 * steps):
        width = modulated.shape[1] // (2 * steps)
        piece = modulated[:, block * width : (block + 1) * width]
        at = slice(block // 2 * width, (block // 2 + 1) * width)

        @pl.when(core == block % 2)
        def _(piece=piece, at=at):
            mine[:, at] = piece

        @pl.when(core != block % 2)
        def _(piece=piece, at=at):
            other[:, at] = piece


def modulate(place, states, rows, steps):
    tokens, width = states.shape
    tile = 32
    out = jax.ShapeDtypeStruct((tokens, width // 2), jnp.bfloat16)
    spec = pl.BlockSpec((tile, width // 2), lambda i: (i, 0))
    return pl.pallas_call(
        functools.partial(modulate_kernel, steps),
        grid=(tokens // tile,),
        in_specs=[SMEM, pl.BlockSpec((tile, width), lambda i: (i, 0)), pl.BlockSpec(rows.shape, lambda i: (0, 0))],
        out_specs=[spec, spec],
        out_shape=[out, out],
        compiler_params=params(),
        cost_estimate=cost(10 * tokens * width, 6 * tokens * width),
        name="modulate",
    )(place, states, rows)


def project_kernel(size, parts, layouts, place, *refs):
    count = 2 * size - 1
    own, below, above = refs[0], refs[1:size], refs[size:count]
    weights = []
    for layout in layouts:
        weights.append(refs[count : count + len(layout)])
        count += len(layout)
    outs = refs[count : count + 2 * len(layouts)]
    x_held, w_held, x_sems, w_sems = refs[count + 2 * len(layouts) :]
    tokens, depth = own.shape[1:]
    step_at, position, shift = place[0], place[2], place[4]
    early = size - 1
    blocks = {"first": range(early), "last": range(early, size), "all": range(size)}[parts]

    def x_copy(ref, clip, block):
        row = (clip * len(blocks) + block - blocks[0]) * tokens
        return pltpu.make_async_copy(
            ref.at[clip], x_held.at[pl.ds(pl.multiple_of(row, tokens), tokens)], x_sems.at[clip, block]
        )

    def w_copies(which):
        for index, (ref, (offset, whole, start, rows)) in enumerate(zip(weights[which], layouts[which])):
            at = jnp.bitwise_xor(step_at, offset) * whole + start
            target = w_held.at[which, pl.ds(pl.multiple_of(at, rows), rows)]
            yield pltpu.make_async_copy(ref, target, w_sems.at[which, index])

    for which in range(len(layouts)):
        for copy in w_copies(which):
            copy.start()
        if which:
            continue
        for clip in range(2):
            for away in range(size):
                for sign, held in ((1, above), (-1, below)):
                    if away == 0 and sign < 0:
                        continue
                    source = own if away == 0 else held[away - 1]
                    block_at = position + sign * away
                    block = lax.rem(block_at - shift + size, size)
                    inside = jnp.logical_and(block_at >= 0, block_at < size)
                    inside = jnp.logical_and(inside, jnp.logical_and(block >= blocks[0], block <= blocks[-1]))

                    @pl.when(inside)
                    def _(source=source, block=block, clip=clip):
                        x_copy(source, clip, block).start()

    rows = outs[0].shape[0]
    for clip in range(2):
        for block in blocks:
            x_copy(own, clip, block).wait()
    for which in range(len(layouts)):
        for copy in w_copies(which):
            copy.wait()
        for clip in range(2):
            span = slice(clip * rows, (clip + 1) * rows)
            outs[2 * which + clip][...] = jnp.dot(x_held[span], w_held[which], preferred_element_type=jnp.float32)


def project(place, line, all_shards, parts, name):
    size = lax.axis_size("head")
    below, above = line
    operands = [below[0]] + below[1:] + above[1:]
    _, tokens, depth = operands[0].shape
    layouts, weights = [], []
    for shards in all_shards:
        layout = []
        for offset, pieces in enumerate(shards):
            start = 0
            for piece in pieces:
                layout.append((offset, depth // len(shards), start, piece.shape[0]))
                weights.append(piece)
                start += piece.shape[0]
        layouts.append(tuple(layout))
    sets = len(layouts)
    columns = weights[0].shape[1]
    rows = {"first": size - 1, "last": 1, "all": size}[parts] * tokens
    out = jax.ShapeDtypeStruct((rows, columns), jnp.float32)
    moved = 2 * depth * (2 * rows + sets * columns) + 8 * sets * rows * columns
    outs = pl.pallas_call(
        functools.partial(project_kernel, size, parts, tuple(layouts)),
        in_specs=[SMEM] + [ANY] * (len(operands) + len(weights)),
        out_specs=[VMEM] * (2 * sets),
        out_shape=[out] * (2 * sets),
        scratch_shapes=[
            pltpu.VMEM((2 * rows, depth), jnp.bfloat16),
            pltpu.VMEM((sets, depth, columns), jnp.bfloat16),
            pltpu.SemaphoreType.DMA((2, size)),
            pltpu.SemaphoreType.DMA((sets, max(len(layout) for layout in layouts))),
        ],
        compiler_params=params(),
        cost_estimate=cost(4 * rows * sets * depth * columns, moved),
        name=name,
    )(place, *operands, *weights)
    return [[outs[2 * which], swap(outs[2 * which + 1], "fsdp", 1)] for which in range(sets)]


def norms_kernel(place, *refs):
    parts, out = refs[:8], refs[8]
    tokens = parts[2].shape[0]
    rows = []
    for at in (0, 4):
        found = []
        for part in (at + 2, at, at + 2):
            total = parts[part][...] + parts[part + 1][...]
            total = total * total
            lanes = total[:, :HD]
            for group in range(1, total.shape[1] // HD):
                lanes = lanes + total[:, group * HD : (group + 1) * HD]
            found.append(jnp.sum(lanes.T, axis=0, keepdims=True))
        wrapped = jnp.concatenate(found[:2], axis=1)
        straight = jnp.concatenate(found[1:], axis=1)
        rows.append(jnp.where(place[4] == 0, straight, wrapped))
    both = jnp.concatenate(rows, axis=0)
    for peer in range(out.shape[0]):
        out[peer] = both


def norms(place, q_parts, k_parts, size):
    rows = q_parts[0].shape[0] + q_parts[2].shape[0]
    operands = q_parts + k_parts
    return pl.pallas_call(
        norms_kernel,
        in_specs=[SMEM] + [VMEM] * 8,
        out_specs=VMEM,
        out_shape=jax.ShapeDtypeStruct((size, 2, rows), jnp.float32),
        compiler_params=params(),
        cost_estimate=cost(8 * rows * q_parts[0].shape[1], 16 * rows * q_parts[0].shape[1]),
        name="norms",
    )(place, *operands)


def probs_kernel(tokens, full_width, place, squares, *refs):
    parts, (q_gain, k_gain, out, scales) = refs[:8], refs[8:]
    rows = scales.shape[1]

    @pl.when(pl.program_id(0) == 0)
    def _():
        total = squares[0]
        for peer in range(1, squares.shape[0]):
            total = total + squares[peer]
        turned = jnp.concatenate([total[:, tokens:], total[:, :tokens]], axis=1)
        total = jnp.where(place[4] == 0, total, turned)
        scale = lax.rsqrt(total / full_width + 1e-06)
        for which in range(2):
            scales[which] = jnp.broadcast_to(scale[which : which + 1], (HD, rows)).T

    column = lax.broadcasted_iota(jnp.int32, (1, rows), 1) + place[4] * tokens
    valid = jnp.where(column >= rows, column - rows, column) < place[3]
    for head in range(out.shape[0]):
        span = slice(head * HD, (head + 1) * HD)

        def normed(at, gain, which):
            joined = [parts[at + i][:, span] + parts[at + i + 1][:, span] for i in (0, 2)]
            return (jnp.concatenate(joined) * scales[which] * gain[:, span]).astype(jnp.bfloat16)

        queries, keys = normed(0, q_gain, 0), normed(4, k_gain, 1)
        scores = lax.dot_general(queries, keys, (((1,), (1,)), ((), ())), preferred_element_type=jnp.float32)
        scores = jnp.where(valid, scores * (1.0 / math.sqrt(HD)), -jnp.inf)
        raised = jnp.exp(scores - jnp.max(scores, axis=-1, keepdims=True))
        out[head] = (raised * (1.0 / jnp.sum(raised, axis=-1, keepdims=True))).astype(jnp.bfloat16)


def at_once(heads):
    return 2 if heads % 2 == 0 else 1


def probabilities(place, squares, q_parts, k_parts, q_gain, k_gain):
    columns = q_parts[0].shape[1]
    rows = q_parts[0].shape[0] + q_parts[2].shape[0]
    heads = columns // HD
    group = at_once(heads)
    by_head = [pl.BlockSpec((part.shape[0], group * HD), lambda i: (0, i)) for part in q_parts + k_parts]
    gain = pl.BlockSpec((1, group * HD), lambda i: (0, i))
    return pl.pallas_call(
        functools.partial(probs_kernel, q_parts[2].shape[0], float(columns * squares.shape[0])),
        grid=(heads // group,),
        in_specs=[SMEM, pl.BlockSpec(squares.shape, lambda i: (0, 0, 0))] + by_head + [gain] * 2,
        out_specs=pl.BlockSpec((group, rows, rows), lambda i: (i, 0, 0)),
        out_shape=jax.ShapeDtypeStruct((heads, rows, rows), jnp.bfloat16),
        scratch_shapes=[pltpu.VMEM((2, rows, HD), jnp.float32)],
        compiler_params=params(),
        cost_estimate=cost(2 * heads * rows * rows * HD, 16 * rows * columns + 2 * heads * rows * rows, heads * rows * rows),
        name="probs",
    )(place, squares, *q_parts, *k_parts, q_gain[None], k_gain[None])


def attend_kernel(place, probs, v_a, v_b, out, held):
    size, tokens, _ = out.shape
    for head in range(probs.shape[0]):
        span = slice(head * HD, (head + 1) * HD)
        values = (v_a[:, span] + v_b[:, span]).astype(jnp.bfloat16)
        held[:, span] = jnp.dot(probs[head], values, preferred_element_type=jnp.float32)
    for block in range(size):
        at = lax.rem(block - place[4] + size, size) * tokens
        out[block] = held[pl.ds(pl.multiple_of(at, tokens), tokens)].astype(jnp.bfloat16)


def attend(place, probs, v_parts, size):
    heads, rows, _ = probs.shape
    tokens = rows // size
    group = at_once(heads)
    by_head = pl.BlockSpec((rows, group * HD), lambda i: (0, i))
    return pl.pallas_call(
        attend_kernel,
        grid=(heads // group,),
        in_specs=[SMEM, pl.BlockSpec((group, rows, rows), lambda i: (i, 0, 0)), by_head, by_head],
        out_specs=pl.BlockSpec((size, tokens, group * HD), lambda i: (0, 0, i)),
        out_shape=jax.ShapeDtypeStruct((size, tokens, heads * HD), jnp.bfloat16),
        scratch_shapes=[pltpu.VMEM((rows, group * HD), jnp.float32)],
        compiler_params=params(),
        cost_estimate=cost(2 * heads * rows * rows * HD, 2 * heads * rows * rows + 10 * rows * heads * HD),
        name="attend",
    )(place, probs, *v_parts)


def out_kernel(size, layout, place, widths, *refs):
    pieces, weights = refs[: len(layout)], refs[len(layout) : len(layout) + 2 * size]
    gates, out, a_held, w_held, total, a_sems, w_sems = refs[len(layout) + 2 * size :]
    steps, _, tokens, columns = out.shape
    width = columns // 2
    halves, _, _, span_width = w_held.shape
    joined = halves == 1
    step_at, core, position = place[0], place[1], place[2]

    def a_copies():
        for index, (offset, start, count) in enumerate(layout):
            row = pl.multiple_of(jnp.bitwise_xor(step_at, offset) * tokens, tokens)
            for group in range(count):
                yield pltpu.make_async_copy(
                    pieces[index].at[group], a_held.at[start + group, pl.ds(row, tokens)], a_sems.at[index, group]
                )

    def w_copy(half, away):
        group = lax.rem(position + away, size)
        at = jnp.bitwise_xor(core, half)
        if joined:
            span = pl.ds(pl.multiple_of(at * width, 128), width)
            target = w_held.at[0, group, :, span]
        else:
            target = w_held.at[at, group]
        return pltpu.make_async_copy(weights[half * size + away], target, w_sems.at[half, away])

    for copy in a_copies():
        copy.start()
    for away in range(size):
        for half in range(2):
            w_copy(half, away).start()
    for copy in a_copies():
        copy.wait()
    for away in range(size):
        group = lax.rem(position + away, size)
        for half in range(2):
            w_copy(half, away).wait()
        for half in range(halves):
            part = jnp.dot(a_held[group], w_held[half, group], preferred_element_type=jnp.float32)
            part = part.astype(jnp.bfloat16).astype(jnp.float32)
            if away == 0:
                total[half] = part
            else:
                total[half] += part
    for half in range(halves):
        span = slice(half * span_width, (half + 1) * span_width)
        reached = None
        for step in range(steps):
            told = jnp.bitwise_xor(step_at, step)
            branch = total[half, step * tokens : (step + 1) * tokens] * gates[pl.ds(told, 1), span]
            out[step, 0, :, span] = branch.astype(jnp.bfloat16)
            drift = branch * widths[told]
            reached = drift if step == 0 else reached + drift
            out[step, 1, :, span] = reached.astype(jnp.bfloat16)


def project_out(place, widths, gathered, weights, gates):
    size = lax.axis_size("head")
    steps = len(gathered)
    _, tokens, inner = gathered[0][0].shape
    width = weights[0][0].shape[1]
    layout, pieces = [], []
    for offset, held in enumerate(gathered):
        start = 0
        for piece in held:
            layout.append((offset, start, piece.shape[0]))
            pieces.append(piece)
            start += piece.shape[0]
    rows = steps * tokens
    halves = 1 if width % 128 == 0 else 2
    operands = pieces + [w for half in weights for w in half]
    return pl.pallas_call(
        functools.partial(out_kernel, size, tuple(layout)),
        in_specs=[SMEM, SMEM] + [ANY] * len(operands) + [VMEM],
        out_specs=VMEM,
        out_shape=jax.ShapeDtypeStruct((steps, 2, tokens, 2 * width), jnp.bfloat16),
        scratch_shapes=[
            pltpu.VMEM((size, rows, inner), jnp.bfloat16),
            pltpu.VMEM((halves, size, inner, 2 * width // halves), jnp.bfloat16),
            pltpu.VMEM((halves, rows, 2 * width // halves), jnp.float32),
            pltpu.SemaphoreType.DMA((len(layout), size)),
            pltpu.SemaphoreType.DMA((2, size)),
        ],
        compiler_params=params(),
        cost_estimate=cost(4 * rows * size * inner * width, 2 * size * inner * (rows + 2 * width) + 8 * rows * width),
        name="project_out",
    )(place, widths, *operands, gates)


def finish_kernel(base, arrived, reached, update):
    reached[...] = base[...] + arrived[0, 1].astype(jnp.float32)
    update[...] = arrived[0, 0]


def finish(base, arrived):
    steps, _, tokens, width = arrived.shape
    by_columns = pl.BlockSpec((tokens, width), lambda i: (0, i))
    return pl.pallas_call(
        finish_kernel,
        grid=(steps,),
        in_specs=[by_columns, pl.BlockSpec((1, 2, tokens, width), lambda i: (i, 0, 0, 0))],
        out_specs=[by_columns, by_columns],
        out_shape=[jax.ShapeDtypeStruct(base.shape, jnp.float32), jax.ShapeDtypeStruct(base.shape, jnp.bfloat16)],
        compiler_params=params(),
        cost_estimate=cost(base.size, 14 * base.size),
        name="finish",
    )(base, arrived)


def body(states, timesteps, lengths, modulation, w_query, w_key, w_value, w_out, q_gain, k_gain):
    steps, size = lax.axis_size("step"), lax.axis_size("head")
    step, core, position = (lax.axis_index(axis) for axis in ("step", "fsdp", "head"))
    current = states[0, 0]
    shift = (position >= size // 2).astype(jnp.int32)
    place = jnp.stack([step, core, position, lengths[0], shift]).astype(jnp.int32)

    q_near = direct(w_query)
    k_near = direct(after(w_key, *listed(q_near)))
    q_near = dict(zip(q_near, [[piece] for piece in after(tuple(listed(q_near)), *listed(k_near))]))
    q_shards = forwarded(w_query, q_near, 0)
    k_shards = forwarded(w_key, k_near, 1)
    v_near = direct(after(w_value, *listed(q_shards), *listed(k_shards)))
    v_shards = forwarded(w_value, v_near)

    mine, other = modulate(place, current, modulation[0], steps)
    line = along_line(jnp.stack([mine, swap(other, "fsdp", 1)]), (listed(q_near), listed(k_near)))
    early = tuple(held[: size - 1] + [held[0]] for held in line)

    q_parts, k_parts = project(place, early, (q_shards, k_shards), "first", "first")
    below, above = along_line(after(w_out, line[0][-1], line[1][-1], q_parts[0], k_parts[0]))
    q_last, k_last = project(place, line, (q_shards, k_shards), "last", "last")
    q_parts, k_parts = q_parts + q_last, k_parts + k_last
    own_squares = norms(place, q_parts, k_parts, size)
    squares = lax.all_to_all(own_squares, "head", 0, 0)
    (v_parts,) = project(after(place, own_squares), line, (v_shards,), "all", "value")
    squares = after(squares, v_parts[0], below[1], above[1])
    probs = probabilities(place, squares, q_parts, k_parts, q_gain, k_gain)

    step_width = (timesteps[0, 1] - timesteps[0, 0]).astype(jnp.float32) / 1000.0
    carried = step_width * current + jnp.where(step == 0, current, jnp.zeros_like(current))
    base, total = carried, carried
    swapped = []
    for bit in bits_of("step"):
        swapped.append(swap(after(total.astype(jnp.bfloat16), *listed(v_shards)), "step", bit))
        brought = swapped[-1].astype(jnp.float32)
        base = base + jnp.where(jnp.bitwise_and(step, bit) != 0, brought, jnp.zeros_like(brought))
        total = total + brought

    columns = current.shape[1] // steps
    told = jnp.concatenate([modulation[0, 2], jnp.full((HD,), step_width)])[None]
    sent_told = after(told, probs)
    heard = jnp.concatenate([told] + [swap(sent_told, "step", offset) for offset in range(1, steps)])
    gates = lax.dynamic_slice(heard, (0, step * columns), (steps, columns))

    attended = attend(place, after(probs, swapped[0]), v_parts, size)
    quarter = after(lax.all_to_all(attended, "head", 0, 0), swapped[-1], below[2], above[2])
    gathered = forwarded(quarter, direct(quarter))

    own_columns = [w_out] + [
        jnp.where(position + away < size, above[away], below[size - away]) for away in range(1, size)
    ]
    out_weights = (own_columns, [swap(w, "fsdp", 1) for w in own_columns])

    sent = project_out(place, heard[:, -1], gathered, out_weights, gates)
    arrived = lax.all_to_all(sent, "step", 0, 0)
    reached, update = finish(base, arrived)
    return reached[None, None], update[None, None]


def solution(mesh):
    in_specs = (
        P("step", "fsdp", "head", None),
        P("step", None),
        P("fsdp"),
        P("step", None, None),
        P(("step", "fsdp"), "head"),
        P(("step", "fsdp"), "head"),
        P(("step", "fsdp"), "head"),
        P("head", ("step", "fsdp")),
        P("head"),
        P("head"),
    )
    out_specs = (P("step", "fsdp", "head", None), P("step", "fsdp", "head", None))
    return jax.shard_map(body, mesh=mesh, in_specs=in_specs, out_specs=out_specs, check_vma=False)
```

```python
import functools
import math

import jax
import jax.numpy as jnp
from jax import lax
from jax.experimental import pallas as pl
from jax.experimental.pallas import tpu as pltpu
from jax.sharding import PartitionSpec as P

HD = 128
MIB = 1 << 20
SMEM = pl.BlockSpec(memory_space=pltpu.SMEM)
VMEM = pl.BlockSpec(memory_space=pltpu.VMEM)
ANY = pl.BlockSpec(memory_space=pl.ANY)


def swap(x, axis, offset):
    return lax.ppermute(x, axis, [(i, i ^ offset) for i in range(lax.axis_size(axis))])


def bits_of(axis):
    return [1 << bit for bit in range(lax.axis_size(axis).bit_length() - 1)]


def direct(x):
    return {bit: [swap(x, "step", bit)] for bit in bits_of("step")}


def forwarded(x, near, *awaited):
    held = {0: [x], **near}
    half = x.shape[0] // 2
    for offset in range(1, lax.axis_size("step")):
        low, high = offset & -offset, 1 << (offset.bit_length() - 1)
        if offset in held:
            continue
        top, bottom = held[offset ^ low], held[offset ^ high]
        top = top[0][:half] if len(top) == 1 else top[0]
        bottom = bottom[0][half:] if len(bottom) == 1 else bottom[1]
        if awaited:
            top, bottom = after((top, bottom), *awaited)
        held[offset] = [swap(top, "step", low), swap(bottom, "step", high)]
    return [held[offset] for offset in range(lax.axis_size("step"))]


def listed(held):
    return [piece for pieces in (held.values() if isinstance(held, dict) else held) for piece in pieces]


def after(x, *others):
    return lax.optimization_barrier((x,) + others)[0]


def along_line(x):
    size = lax.axis_size("head")
    below, above = [x], [x]
    for hop in range(1, size):
        below.append(lax.ppermute(below[-1], "head", [(i, i + 1) for i in range(hop - 1, size - 1)]))
        above.append(lax.ppermute(above[-1], "head", [(i, i - 1) for i in range(1, size - hop + 1)]))
    return below, above


def params(mib=56):
    return pltpu.CompilerParams(vmem_limit_bytes=mib * MIB)


def cost(flops, moved, raised=0):
    return pl.CostEstimate(flops=int(flops) // 4, bytes_accessed=int(moved) // 4, transcendentals=int(raised) // 4)


def modulate_kernel(steps, place, states, rows, mine, other):
    current = states[...]
    centre = jnp.mean(current, axis=-1, keepdims=True)
    centred = current - centre
    spread_of = jnp.mean(centred * centred, axis=-1, keepdims=True)
    shift, scale = rows[0, 0:1, :], rows[0, 1:2, :]
    modulated = (centred * lax.rsqrt(spread_of + 1e-06) * (1.0 + scale) + shift).astype(jnp.bfloat16)
    core = place[1]
    for block in range(2 * steps):
        width = modulated.shape[1] // (2 * steps)
        piece = modulated[:, block * width : (block + 1) * width]
        at = slice(block // 2 * width, (block // 2 + 1) * width)

        @pl.when(core == block % 2)
        def _(piece=piece, at=at):
            mine[:, at] = piece

        @pl.when(core != block % 2)
        def _(piece=piece, at=at):
            other[:, at] = piece


def modulate(place, states, rows, steps):
    tokens, width = states.shape
    tile = 32
    out = jax.ShapeDtypeStruct((tokens, width // 2), jnp.bfloat16)
    spec = pl.BlockSpec((tile, width // 2), lambda i: (i, 0))
    return pl.pallas_call(
        functools.partial(modulate_kernel, steps),
        grid=(tokens // tile,),
        in_specs=[SMEM, pl.BlockSpec((tile, width), lambda i: (i, 0)), pl.BlockSpec(rows.shape, lambda i: (0, 0, 0))],
        out_specs=[spec, spec],
        out_shape=[out, out],
        compiler_params=params(),
        cost_estimate=cost(10 * tokens * width, 6 * tokens * width),
        name="modulate",
    )(place, states, rows)


def project_kernel(size, parts, layout, place, *refs):
    count = 2 * size - 1
    own, below, above = refs[0], refs[1:size], refs[size:count]
    weights = refs[count : count + len(layout)]
    here, there, x_held, w_held, x_sems, w_sems = refs[count + len(layout) :]
    tokens, depth = own.shape[1:]
    step_at, position, shift = place[0], place[2], place[4]
    early = size - 1
    blocks = {"first": range(early), "last": range(early, size), "all": range(size)}[parts]

    def x_copy(ref, clip, block):
        row = (clip * len(blocks) + block - blocks[0]) * tokens
        return pltpu.make_async_copy(
            ref.at[clip], x_held.at[pl.ds(pl.multiple_of(row, tokens), tokens)], x_sems.at[clip, block]
        )

    def w_copies():
        for index, (ref, (offset, whole, start, rows)) in enumerate(zip(weights, layout)):
            at = jnp.bitwise_xor(step_at, offset) * whole + start
            yield pltpu.make_async_copy(ref, w_held.at[pl.ds(pl.multiple_of(at, rows), rows)], w_sems.at[index])

    for copy in w_copies():
        copy.start()
    for clip in range(2):
        for away in range(size):
            for sign, held in ((1, above), (-1, below)):
                if away == 0 and sign < 0:
                    continue
                source = own if away == 0 else held[away - 1]
                block_at = position + sign * away
                block = lax.rem(block_at - shift + size, size)
                inside = jnp.logical_and(block_at >= 0, block_at < size)
                inside = jnp.logical_and(inside, jnp.logical_and(block >= blocks[0], block <= blocks[-1]))

                @pl.when(inside)
                def _(source=source, block=block, clip=clip):
                    x_copy(source, clip, block).start()

    for copy in w_copies():
        copy.wait()
    for clip in range(2):
        for block in blocks:
            x_copy(own, clip, block).wait()
    rows, columns = here.shape
    width = columns if columns % 512 else columns // 2
    for start in range(0, columns, width):
        span = slice(start, start + width)
        product = jnp.dot(x_held[...], w_held[:, span], preferred_element_type=jnp.float32)
        here[:, span] = product[:rows]
        there[:, span] = product[rows:]


def project(place, line, shards, parts, name):
    size = lax.axis_size("head")
    below, above = line
    operands = [below[0]] + below[1:] + above[1:]
    _, tokens, depth = operands[0].shape
    layout, weights = [], []
    for offset, pieces in enumerate(shards):
        start = 0
        for piece in pieces:
            layout.append((offset, depth // len(shards), start, piece.shape[0]))
            weights.append(piece)
            start += piece.shape[0]
    columns = weights[0].shape[1]
    rows = {"first": size - 1, "last": 1, "all": size}[parts] * tokens
    out = jax.ShapeDtypeStruct((rows, columns), jnp.float32)
    moved = 2 * depth * (2 * rows + columns) + 8 * rows * columns
    return pl.pallas_call(
        functools.partial(project_kernel, size, parts, tuple(layout)),
        in_specs=[SMEM] + [ANY] * (len(operands) + len(weights)),
        out_specs=[VMEM, VMEM],
        out_shape=[out, out],
        scratch_shapes=[
            pltpu.VMEM((2 * rows, depth), jnp.bfloat16),
            pltpu.VMEM((depth, columns), jnp.bfloat16),
            pltpu.SemaphoreType.DMA((2, size)),
            pltpu.SemaphoreType.DMA((len(layout),)),
        ],
        compiler_params=params(),
        cost_estimate=cost(4 * rows * depth * columns, moved),
        name=name,
    )(place, *operands, *weights)


def norms_kernel(place, first_a, first_b, last_a, last_b, out):
    width = first_a.shape[1] // 2
    rows = []
    for which in range(2):
        found = []
        for one, other in ((first_a, first_b), (last_a, last_b)):
            lanes = None
            for start in range(which * width, (which + 1) * width, HD):
                total = one[:, start : start + HD] + other[:, start : start + HD]
                lanes = total * total if lanes is None else lanes + total * total
            found.append(jnp.sum(lanes.T, axis=0, keepdims=True))
        straight = jnp.concatenate(found, axis=1)
        wrapped = jnp.concatenate(found[::-1], axis=1)
        rows.append(jnp.where(place[4] == 0, straight, wrapped))
    both = jnp.concatenate(rows, axis=0)
    for peer in range(out.shape[0]):
        out[peer] = both


def norms(place, parts, size):
    rows = parts[0].shape[0] + parts[2].shape[0]
    return pl.pallas_call(
        norms_kernel,
        in_specs=[SMEM] + [VMEM] * 4,
        out_specs=VMEM,
        out_shape=jax.ShapeDtypeStruct((size, 2, rows), jnp.float32),
        compiler_params=params(),
        cost_estimate=cost(4 * rows * parts[0].shape[1], 8 * rows * parts[0].shape[1]),
        name="norms",
    )(place, *parts)


def probs_kernel(tokens, full_width, place, squares, *refs):
    parts, (q_gain, k_gain, out, scales) = refs[:8], refs[8:]
    rows = scales.shape[1]

    @pl.when(pl.program_id(0) == 0)
    def _():
        total = squares[0]
        for peer in range(1, squares.shape[0]):
            total = total + squares[peer]
        turned = jnp.concatenate([total[:, tokens:], total[:, :tokens]], axis=1)
        total = jnp.where(place[4] == 0, total, turned)
        scale = lax.rsqrt(total / full_width + 1e-06)
        for which in range(2):
            scales[which] = jnp.broadcast_to(scale[which : which + 1], (HD, rows)).T

    column = lax.broadcasted_iota(jnp.int32, (1, rows), 1) + place[4] * tokens
    valid = jnp.where(column >= rows, column - rows, column) < place[3]
    for head in range(out.shape[0]):
        span = slice(head * HD, (head + 1) * HD)

        def normed(at, gain, which):
            joined = [parts[at + i][:, span] + parts[at + i + 1][:, span] for i in (0, 2)]
            return (jnp.concatenate(joined) * scales[which] * gain[:, span]).astype(jnp.bfloat16)

        queries, keys = normed(0, q_gain, 0), normed(4, k_gain, 1)
        scores = lax.dot_general(queries, keys, (((1,), (1,)), ((), ())), preferred_element_type=jnp.float32)
        scores = jnp.where(valid, scores * (1.0 / math.sqrt(HD)), -jnp.inf)
        raised = jnp.exp(scores - jnp.max(scores, axis=-1, keepdims=True))
        out[head] = (raised * (1.0 / jnp.sum(raised, axis=-1, keepdims=True))).astype(jnp.bfloat16)


def at_once(heads):
    return 2 if heads % 2 == 0 else 1


def probabilities(place, squares, parts, q_gain, k_gain):
    columns = parts[0].shape[1] // 2
    rows = parts[0].shape[0] + parts[2].shape[0]
    heads = columns // HD
    group = at_once(heads)
    q_blocks = [pl.BlockSpec((part.shape[0], group * HD), lambda i: (0, i)) for part in parts]
    k_blocks = [pl.BlockSpec((part.shape[0], group * HD), lambda i: (0, i + heads // group)) for part in parts]
    gain = pl.BlockSpec((1, group * HD), lambda i: (0, i))
    return pl.pallas_call(
        functools.partial(probs_kernel, parts[2].shape[0], float(columns * squares.shape[0])),
        grid=(heads // group,),
        in_specs=[SMEM, pl.BlockSpec(squares.shape, lambda i: (0, 0, 0))] + q_blocks + k_blocks + [gain] * 2,
        out_specs=pl.BlockSpec((group, rows, rows), lambda i: (i, 0, 0)),
        out_shape=jax.ShapeDtypeStruct((heads, rows, rows), jnp.bfloat16),
        scratch_shapes=[pltpu.VMEM((2, rows, HD), jnp.float32)],
        compiler_params=params(),
        cost_estimate=cost(2 * heads * rows * rows * HD, 16 * rows * columns + 2 * heads * rows * rows, heads * rows * rows),
        name="probs",
    )(place, squares, *parts, *parts, q_gain[None], k_gain[None])


def attend_kernel(place, probs, v_a, v_b, out, held):
    size, tokens, _ = out.shape
    for head in range(probs.shape[0]):
        span = slice(head * HD, (head + 1) * HD)
        values = (v_a[:, span] + v_b[:, span]).astype(jnp.bfloat16)
        held[:, span] = jnp.dot(probs[head], values, preferred_element_type=jnp.float32)
    for block in range(size):
        at = lax.rem(block - place[4] + size, size) * tokens
        out[block] = held[pl.ds(pl.multiple_of(at, tokens), tokens)].astype(jnp.bfloat16)


def attend(place, probs, v_parts, size):
    heads, rows, _ = probs.shape
    tokens = rows // size
    group = at_once(heads)
    by_head = pl.BlockSpec((rows, group * HD), lambda i: (0, i))
    return pl.pallas_call(
        attend_kernel,
        grid=(heads // group,),
        in_specs=[SMEM, pl.BlockSpec((group, rows, rows), lambda i: (i, 0, 0)), by_head, by_head],
        out_specs=pl.BlockSpec((size, tokens, group * HD), lambda i: (0, 0, i)),
        out_shape=jax.ShapeDtypeStruct((size, tokens, heads * HD), jnp.bfloat16),
        scratch_shapes=[pltpu.VMEM((rows, group * HD), jnp.float32)],
        compiler_params=params(),
        cost_estimate=cost(2 * heads * rows * rows * HD, 2 * heads * rows * rows + 10 * rows * heads * HD),
        name="attend",
    )(place, probs, *v_parts)


def out_kernel(size, layout, place, widths, *refs):
    pieces, weights = refs[: len(layout)], refs[len(layout) : len(layout) + 2 * size]
    gates, out, a_held, w_held, total, a_sems, w_sems = refs[len(layout) + 2 * size :]
    steps, _, tokens, columns = out.shape
    width = columns // 2
    halves, _, _, span_width = w_held.shape
    joined = halves == 1
    step_at, core, position = place[0], place[1], place[2]

    def a_copies():
        for index, (offset, start, count) in enumerate(layout):
            row = pl.multiple_of(jnp.bitwise_xor(step_at, offset) * tokens, tokens)
            for group in range(count):
                yield pltpu.make_async_copy(
                    pieces[index].at[group], a_held.at[start + group, pl.ds(row, tokens)], a_sems.at[index, group]
                )

    def w_copy(half, away):
        group = lax.rem(position + away, size)
        at = jnp.bitwise_xor(core, half)
        if joined:
            span = pl.ds(pl.multiple_of(at * width, 128), width)
            target = w_held.at[0, group, :, span]
        else:
            target = w_held.at[at, group]
        return pltpu.make_async_copy(weights[half * size + away], target, w_sems.at[half, away])

    for copy in a_copies():
        copy.start()
    for away in range(size):
        for half in range(2):
            w_copy(half, away).start()
    for copy in a_copies():
        copy.wait()
    for away in range(size):
        group = lax.rem(position + away, size)
        for half in range(2):
            w_copy(half, away).wait()
        for half in range(halves):
            part = jnp.dot(a_held[group], w_held[half, group], preferred_element_type=jnp.float32)
            part = part.astype(jnp.bfloat16).astype(jnp.float32)
            if away == 0:
                total[half] = part
            else:
                total[half] += part
    for half in range(halves):
        span = slice(half * span_width, (half + 1) * span_width)
        reached = None
        for step in range(steps):
            told = jnp.bitwise_xor(step_at, step)
            branch = total[half, step * tokens : (step + 1) * tokens] * gates[pl.ds(told, 1), span]
            out[step, 0, :, span] = branch.astype(jnp.bfloat16)
            drift = branch * widths[told]
            reached = drift if step == 0 else reached + drift
            out[step, 1, :, span] = reached.astype(jnp.bfloat16)


def project_out(place, widths, gathered, weights, gates):
    size = lax.axis_size("head")
    steps = len(gathered)
    _, tokens, inner = gathered[0][0].shape
    width = weights[0][0].shape[1]
    layout, pieces = [], []
    for offset, held in enumerate(gathered):
        start = 0
        for piece in held:
            layout.append((offset, start, piece.shape[0]))
            pieces.append(piece)
            start += piece.shape[0]
    rows = steps * tokens
    halves = 1 if width % 128 == 0 else 2
    operands = pieces + [w for half in weights for w in half]
    return pl.pallas_call(
        functools.partial(out_kernel, size, tuple(layout)),
        in_specs=[SMEM, SMEM] + [ANY] * len(operands) + [VMEM],
        out_specs=VMEM,
        out_shape=jax.ShapeDtypeStruct((steps, 2, tokens, 2 * width), jnp.bfloat16),
        scratch_shapes=[
            pltpu.VMEM((size, rows, inner), jnp.bfloat16),
            pltpu.VMEM((halves, size, inner, 2 * width // halves), jnp.bfloat16),
            pltpu.VMEM((halves, rows, 2 * width // halves), jnp.float32),
            pltpu.SemaphoreType.DMA((len(layout), size)),
            pltpu.SemaphoreType.DMA((2, size)),
        ],
        compiler_params=params(),
        cost_estimate=cost(4 * rows * size * inner * width, 2 * size * inner * (rows + 2 * width) + 8 * rows * width),
        name="project_out",
    )(place, widths, *operands, gates)


def finish_kernel(base, arrived, reached, update):
    reached[...] = base[...] + arrived[0, 1].astype(jnp.float32)
    update[...] = arrived[0, 0]


def finish(base, arrived):
    steps, _, tokens, width = arrived.shape
    by_columns = pl.BlockSpec((tokens, width), lambda i: (0, i))
    return pl.pallas_call(
        finish_kernel,
        grid=(steps,),
        in_specs=[by_columns, pl.BlockSpec((1, 2, tokens, width), lambda i: (i, 0, 0, 0))],
        out_specs=[by_columns, by_columns],
        out_shape=[jax.ShapeDtypeStruct(base.shape, jnp.float32), jax.ShapeDtypeStruct(base.shape, jnp.bfloat16)],
        compiler_params=params(),
        cost_estimate=cost(base.size, 14 * base.size),
        name="finish",
    )(base, arrived)


def body(states, timesteps, lengths, modulation, w_query, w_key, w_value, w_out, q_gain, k_gain):
    steps, size = lax.axis_size("step"), lax.axis_size("head")
    step, core, position = (lax.axis_index(axis) for axis in ("step", "fsdp", "head"))
    current = states[0, 0]
    shift = (position >= size // 2).astype(jnp.int32)
    place = jnp.stack([step, core, position, lengths[0], shift]).astype(jnp.int32)

    mine, other = modulate(place, current, modulation, steps)
    tokens = jnp.stack([mine, swap(other, "fsdp", 1)])
    line = along_line(tokens)
    early = tuple(held[: size - 1] + [held[0]] for held in line)

    w_both = after(jnp.concatenate([w_query, w_key], axis=1), tokens)
    both_shards = forwarded(w_both, direct(w_both), line[0][1], line[1][1])
    first_here, first_there = project(place, early, both_shards, "first", "first")
    v_near = direct(after(w_value, *listed(both_shards)))
    v_shards = forwarded(w_value, v_near, first_here)

    first_there = after(first_there, line[0][-1], line[1][-1])
    parts = [first_here, swap(first_there, "fsdp", 1)]
    last_here, last_there = project(place, line, both_shards, "last", "last")
    parts += [last_here, swap(last_there, "fsdp", 1)]
    own_squares = norms(place, parts, size)
    squares = lax.all_to_all(own_squares, "head", 0, 0)
    v_here, v_there = project(after(place, own_squares), line, v_shards, "all", "value")
    v_parts = [v_here, swap(v_there, "fsdp", 1)]

    below, above = [w_out], [w_out]
    for hop in range(1, size):
        up, down = below[-1], above[-1]
        if hop == 1:
            up, down = after((up, down), line[0][-1], line[1][-1], first_here)
        if hop == size - 1:
            probs = probabilities(place, after(squares, v_here, below[1], above[1]), parts, q_gain, k_gain)
            attended = attend(place, probs, v_parts, size)
            quarter = lax.all_to_all(attended, "head", 0, 0)
            up, down = after((up, down), quarter)
        below.append(lax.ppermute(up, "head", [(i, i + 1) for i in range(hop - 1, size - 1)]))
        above.append(lax.ppermute(down, "head", [(i, i - 1) for i in range(1, size - hop + 1)]))

    step_width = (timesteps[0, 1] - timesteps[0, 0]).astype(jnp.float32) / 1000.0
    carried = step_width * current + jnp.where(step == 0, current, jnp.zeros_like(current))
    base, total = carried, carried
    swapped = []
    for bit in bits_of("step"):
        swapped.append(swap(after(total.astype(jnp.bfloat16), own_squares, *listed(v_shards)), "step", bit))
        brought = swapped[-1].astype(jnp.float32)
        base = base + jnp.where(jnp.bitwise_and(step, bit) != 0, brought, jnp.zeros_like(brought))
        total = total + brought

    columns = current.shape[1] // steps
    told = jnp.concatenate([modulation[0, 2], jnp.full((HD,), step_width)])[None]
    sent_told = after(told, probs)
    heard = jnp.concatenate([told] + [swap(sent_told, "step", offset) for offset in range(1, steps)])
    gates = lax.dynamic_slice(heard, (0, step * columns), (steps, columns))

    quarter = after(quarter, swapped[-1], heard)
    gathered = forwarded(quarter, direct(quarter))

    own_columns = [w_out] + [
        jnp.where(position + away < size, above[away], below[size - away]) for away in range(1, size)
    ]
    out_weights = (own_columns, [swap(w, "fsdp", 1) for w in own_columns])

    sent = project_out(place, heard[:, -1], gathered, out_weights, gates)
    arrived = lax.all_to_all(sent, "step", 0, 0)
    reached, update = finish(base, arrived)
    return reached[None, None], update[None, None]


def solution(mesh):
    in_specs = (
        P("step", "fsdp", "head", None),
        P("step", None),
        P("fsdp"),
        P("step", None, None),
        P(("step", "fsdp"), "head"),
        P(("step", "fsdp"), "head"),
        P(("step", "fsdp"), "head"),
        P("head", ("step", "fsdp")),
        P("head"),
        P("head"),
    )
    out_specs = (P("step", "fsdp", "head", None), P("step", "fsdp", "head", None))
    return jax.shard_map(body, mesh=mesh, in_specs=in_specs, out_specs=out_specs, check_vma=False)
```

```python
import functools
import math

import jax
import jax.numpy as jnp
from jax import lax
from jax.experimental import pallas as pl
from jax.experimental.pallas import tpu as pltpu
from jax.sharding import PartitionSpec as P

HD = 128
MIB = 1 << 20
SMEM = pl.BlockSpec(memory_space=pltpu.SMEM)
VMEM = pl.BlockSpec(memory_space=pltpu.VMEM)
ANY = pl.BlockSpec(memory_space=pl.ANY)


def swap(x, axis, offset):
    return lax.ppermute(x, axis, [(i, i ^ offset) for i in range(lax.axis_size(axis))])


def bits_of(axis):
    return [1 << bit for bit in range(lax.axis_size(axis).bit_length() - 1)]


def direct(x):
    return {bit: [swap(x, "step", bit)] for bit in bits_of("step")}


def forwarded(x, near, *awaited):
    held = {0: [x], **near}
    half = x.shape[0] // 2
    for offset in range(1, lax.axis_size("step")):
        low, high = offset & -offset, 1 << (offset.bit_length() - 1)
        if offset in held:
            continue
        top, bottom = held[offset ^ low], held[offset ^ high]
        top = top[0][:half] if len(top) == 1 else top[0]
        bottom = bottom[0][half:] if len(bottom) == 1 else bottom[1]
        if awaited:
            top, bottom = after((top, bottom), *awaited)
        held[offset] = [swap(top, "step", low), swap(bottom, "step", high)]
    return [held[offset] for offset in range(lax.axis_size("step"))]


def placed(held, column=0):
    found = []
    for offset, pieces in enumerate(held):
        row = 0
        for piece in pieces:
            found.append((piece, offset, row, 0, column, piece.shape[1]))
            row += piece.shape[0]
    return found


def in_rounds(w_both, w_value, line_hops):
    width = w_value.shape[1]
    part = width // 768 * 256
    rest = width - part
    a1, a2 = swap(w_both, "step", 1), swap(w_both, "step", 2)
    hop = line_hops((a1, a2))
    a1, a2 = after((a1, a2), *hop)
    b1 = swap(jnp.concatenate([a2[:, :width], w_value[:, :part]], axis=1), "step", 1)
    b2 = swap(jnp.concatenate([a1[:, width:], w_value[:, :part]], axis=1), "step", 2)
    hop = line_hops((b1, b2))
    e1, e2 = after((b1, b2), *hop)
    middle = width + part // 2
    c1 = swap(jnp.concatenate([w_value[:, part:], e2[:, width:middle]], axis=1), "step", 1)
    c2 = swap(jnp.concatenate([w_value[:, part:], e1[:, middle:]], axis=1), "step", 2)
    both = [
        (w_both, 0, 0, 0, 0, 2 * width),
        (a1, 1, 0, 0, 0, 2 * width),
        (a2, 2, 0, 0, 0, 2 * width),
        (b1, 3, 0, 0, 0, width),
        (b2, 3, 0, 0, width, width),
    ]

    def finished(*awaited):
        f1, f2 = after((c1, c2), *awaited)
        d1 = swap(f2[:, : rest // 2], "step", 1)
        d2 = swap(f1[:, rest // 2 : rest], "step", 2)
        return [
            (w_value, 0, 0, 0, 0, width),
            (b1, 1, 0, width, 0, part),
            (c1, 1, 0, 0, part, rest),
            (b2, 2, 0, width, 0, part),
            (c2, 2, 0, 0, part, rest),
            (c1, 3, 0, rest, 0, part // 2),
            (c2, 3, 0, rest, part // 2, part // 2),
            (d1, 3, 0, 0, part, rest // 2),
            (d2, 3, 0, 0, part + rest // 2, rest // 2),
        ]

    return both, (c1, c2), finished


def after(x, *others):
    return lax.optimization_barrier((x,) + others)[0]


def params(mib=56):
    return pltpu.CompilerParams(vmem_limit_bytes=mib * MIB)


def cost(flops, moved, raised=0):
    return pl.CostEstimate(flops=int(flops) // 4, bytes_accessed=int(moved) // 4, transcendentals=int(raised) // 4)


def modulate_kernel(steps, place, states, rows, mine, other):
    current = states[...]
    centre = jnp.mean(current, axis=-1, keepdims=True)
    centred = current - centre
    spread_of = jnp.mean(centred * centred, axis=-1, keepdims=True)
    shift, scale = rows[0, 0:1, :], rows[0, 1:2, :]
    modulated = (centred * lax.rsqrt(spread_of + 1e-06) * (1.0 + scale) + shift).astype(jnp.bfloat16)
    core = place[1]
    for block in range(2 * steps):
        width = modulated.shape[1] // (2 * steps)
        piece = modulated[:, block * width : (block + 1) * width]
        at = slice(block // 2 * width, (block // 2 + 1) * width)

        @pl.when(core == block % 2)
        def _(piece=piece, at=at):
            mine[:, at] = piece

        @pl.when(core != block % 2)
        def _(piece=piece, at=at):
            other[:, at] = piece


def modulate(place, states, rows, steps):
    tokens, width = states.shape
    tile = 32
    out = jax.ShapeDtypeStruct((tokens, width // 2), jnp.bfloat16)
    spec = pl.BlockSpec((tile, width // 2), lambda i: (i, 0))
    return pl.pallas_call(
        functools.partial(modulate_kernel, steps),
        grid=(tokens // tile,),
        in_specs=[SMEM, pl.BlockSpec((tile, width), lambda i: (i, 0)), pl.BlockSpec(rows.shape, lambda i: (0, 0, 0))],
        out_specs=[spec, spec],
        out_shape=[out, out],
        compiler_params=params(),
        cost_estimate=cost(10 * tokens * width, 6 * tokens * width),
        name="modulate",
    )(place, states, rows)


def project_kernel(size, parts, shard, layout, place, *refs):
    count = 2 * size - 1
    own, below, above = refs[0], refs[1:size], refs[size:count]
    weights = refs[count : count + len(layout)]
    here, there, x_held, w_held, x_sems, w_sems = refs[count + len(layout) :]
    tokens, depth = own.shape[1:]
    step_at, position, shift = place[0], place[2], place[4]
    early = size - 1
    blocks = {"first": range(early), "last": range(early, size), "all": range(size)}[parts]

    def x_copy(ref, clip, block):
        row = (clip * len(blocks) + block - blocks[0]) * tokens
        return pltpu.make_async_copy(
            ref.at[clip], x_held.at[pl.ds(pl.multiple_of(row, tokens), tokens)], x_sems.at[clip, block]
        )

    def w_copies():
        for index, (ref, (offset, row, source, target, count)) in enumerate(zip(weights, layout)):
            at = jnp.bitwise_xor(step_at, offset) * shard + row
            rows = ref.shape[0]
            part = w_held.at[pl.ds(pl.multiple_of(at, rows), rows), pl.ds(target, count)]
            yield pltpu.make_async_copy(ref.at[:, pl.ds(source, count)], part, w_sems.at[index])

    for copy in w_copies():
        copy.start()
    for clip in range(2):
        for away in range(size):
            for sign, held in ((1, above), (-1, below)):
                if away == 0 and sign < 0:
                    continue
                source = own if away == 0 else held[away - 1]
                block_at = position + sign * away
                block = lax.rem(block_at - shift + size, size)
                inside = jnp.logical_and(block_at >= 0, block_at < size)
                inside = jnp.logical_and(inside, jnp.logical_and(block >= blocks[0], block <= blocks[-1]))

                @pl.when(inside)
                def _(source=source, block=block, clip=clip):
                    x_copy(source, clip, block).start()

    for copy in w_copies():
        copy.wait()
    for clip in range(2):
        for block in blocks:
            x_copy(own, clip, block).wait()
    rows, columns = here.shape
    width = columns if columns % 512 else columns // 2
    for start in range(0, columns, width):
        span = slice(start, start + width)
        product = jnp.dot(x_held[...], w_held[:, span], preferred_element_type=jnp.float32)
        here[:, span] = product[:rows]
        there[:, span] = product[rows:]


def project(place, line, shards, parts, name):
    size = lax.axis_size("head")
    below, above = line
    operands = [below[0]] + below[1:] + above[1:]
    _, tokens, depth = operands[0].shape
    weights = [piece[0] for piece in shards]
    layout = [piece[1:] for piece in shards]
    shard, columns = weights[0].shape
    rows = {"first": size - 1, "last": 1, "all": size}[parts] * tokens
    out = jax.ShapeDtypeStruct((rows, columns), jnp.float32)
    moved = 2 * depth * (2 * rows + columns) + 8 * rows * columns
    return pl.pallas_call(
        functools.partial(project_kernel, size, parts, shard, tuple(layout)),
        in_specs=[SMEM] + [ANY] * (len(operands) + len(weights)),
        out_specs=[VMEM, VMEM],
        out_shape=[out, out],
        scratch_shapes=[
            pltpu.VMEM((2 * rows, depth), jnp.bfloat16),
            pltpu.VMEM((depth, columns), jnp.bfloat16),
            pltpu.SemaphoreType.DMA((2, size)),
            pltpu.SemaphoreType.DMA((len(layout),)),
        ],
        compiler_params=params(),
        cost_estimate=cost(4 * rows * depth * columns, moved),
        name=name,
    )(place, *operands, *weights)


def norms_kernel(place, first_a, first_b, last_a, last_b, out):
    width = first_a.shape[1] // 2
    rows = []
    for which in range(2):
        found = []
        for one, other in ((first_a, first_b), (last_a, last_b)):
            lanes = None
            for start in range(which * width, (which + 1) * width, HD):
                total = one[:, start : start + HD] + other[:, start : start + HD]
                lanes = total * total if lanes is None else lanes + total * total
            found.append(jnp.sum(lanes.T, axis=0, keepdims=True))
        straight = jnp.concatenate(found, axis=1)
        wrapped = jnp.concatenate(found[::-1], axis=1)
        rows.append(jnp.where(place[4] == 0, straight, wrapped))
    both = jnp.concatenate(rows, axis=0)
    for peer in range(out.shape[0]):
        out[peer] = both


def norms(place, parts, size):
    rows = parts[0].shape[0] + parts[2].shape[0]
    return pl.pallas_call(
        norms_kernel,
        in_specs=[SMEM] + [VMEM] * 4,
        out_specs=VMEM,
        out_shape=jax.ShapeDtypeStruct((size, 2, rows), jnp.float32),
        compiler_params=params(),
        cost_estimate=cost(4 * rows * parts[0].shape[1], 8 * rows * parts[0].shape[1]),
        name="norms",
    )(place, *parts)


def probs_kernel(tokens, full_width, place, squares, *refs):
    parts, (q_gain, k_gain, out, scales) = refs[:8], refs[8:]
    rows = scales.shape[1]

    @pl.when(pl.program_id(0) == 0)
    def _():
        total = squares[0]
        for peer in range(1, squares.shape[0]):
            total = total + squares[peer]
        turned = jnp.concatenate([total[:, tokens:], total[:, :tokens]], axis=1)
        total = jnp.where(place[4] == 0, total, turned)
        scale = lax.rsqrt(total / full_width + 1e-06)
        for which in range(2):
            scales[which] = jnp.broadcast_to(scale[which : which + 1], (HD, rows)).T

    column = lax.broadcasted_iota(jnp.int32, (1, rows), 1) + place[4] * tokens
    valid = jnp.where(column >= rows, column - rows, column) < place[3]
    for head in range(out.shape[0]):
        span = slice(head * HD, (head + 1) * HD)

        def normed(at, gain, which):
            joined = [parts[at + i][:, span] + parts[at + i + 1][:, span] for i in (0, 2)]
            return (jnp.concatenate(joined) * scales[which] * gain[:, span]).astype(jnp.bfloat16)

        queries, keys = normed(0, q_gain, 0), normed(4, k_gain, 1)
        scores = lax.dot_general(queries, keys, (((1,), (1,)), ((), ())), preferred_element_type=jnp.float32)
        scores = jnp.where(valid, scores * (1.0 / math.sqrt(HD)), -jnp.inf)
        raised = jnp.exp(scores - jnp.max(scores, axis=-1, keepdims=True))
        out[head] = (raised * (1.0 / jnp.sum(raised, axis=-1, keepdims=True))).astype(jnp.bfloat16)


def at_once(heads):
    return 2 if heads % 2 == 0 else 1


def probabilities(place, squares, parts, q_gain, k_gain):
    columns = parts[0].shape[1] // 2
    rows = parts[0].shape[0] + parts[2].shape[0]
    heads = columns // HD
    group = at_once(heads)
    q_blocks = [pl.BlockSpec((part.shape[0], group * HD), lambda i: (0, i)) for part in parts]
    k_blocks = [pl.BlockSpec((part.shape[0], group * HD), lambda i: (0, i + heads // group)) for part in parts]
    gain = pl.BlockSpec((1, group * HD), lambda i: (0, i))
    return pl.pallas_call(
        functools.partial(probs_kernel, parts[2].shape[0], float(columns * squares.shape[0])),
        grid=(heads // group,),
        in_specs=[SMEM, pl.BlockSpec(squares.shape, lambda i: (0, 0, 0))] + q_blocks + k_blocks + [gain] * 2,
        out_specs=pl.BlockSpec((group, rows, rows), lambda i: (i, 0, 0)),
        out_shape=jax.ShapeDtypeStruct((heads, rows, rows), jnp.bfloat16),
        scratch_shapes=[pltpu.VMEM((2, rows, HD), jnp.float32)],
        compiler_params=params(),
        cost_estimate=cost(2 * heads * rows * rows * HD, 16 * rows * columns + 2 * heads * rows * rows, heads * rows * rows),
        name="probs",
    )(place, squares, *parts, *parts, q_gain[None], k_gain[None])


def attend_kernel(place, probs, v_a, v_b, out, held):
    size, tokens, _ = out.shape
    for head in range(probs.shape[0]):
        span = slice(head * HD, (head + 1) * HD)
        values = (v_a[:, span] + v_b[:, span]).astype(jnp.bfloat16)
        held[:, span] = jnp.dot(probs[head], values, preferred_element_type=jnp.float32)
    for block in range(size):
        at = lax.rem(block - place[4] + size, size) * tokens
        out[block] = held[pl.ds(pl.multiple_of(at, tokens), tokens)].astype(jnp.bfloat16)


def attend(place, probs, v_parts, size):
    heads, rows, _ = probs.shape
    tokens = rows // size
    group = at_once(heads)
    by_head = pl.BlockSpec((rows, group * HD), lambda i: (0, i))
    return pl.pallas_call(
        attend_kernel,
        grid=(heads // group,),
        in_specs=[SMEM, pl.BlockSpec((group, rows, rows), lambda i: (i, 0, 0)), by_head, by_head],
        out_specs=pl.BlockSpec((size, tokens, group * HD), lambda i: (0, 0, i)),
        out_shape=jax.ShapeDtypeStruct((size, tokens, heads * HD), jnp.bfloat16),
        scratch_shapes=[pltpu.VMEM((rows, group * HD), jnp.float32)],
        compiler_params=params(),
        cost_estimate=cost(2 * heads * rows * rows * HD, 2 * heads * rows * rows + 10 * rows * heads * HD),
        name="attend",
    )(place, probs, *v_parts)


def out_kernel(size, layout, place, widths, *refs):
    pieces, weights = refs[: len(layout)], refs[len(layout) : len(layout) + 2 * size]
    gates, out, a_held, w_held, total, a_sems, w_sems = refs[len(layout) + 2 * size :]
    steps, _, tokens, columns = out.shape
    width = columns // 2
    halves, _, _, span_width = w_held.shape
    joined = halves == 1
    step_at, core, position = place[0], place[1], place[2]

    def a_copies():
        for index, (offset, start, count) in enumerate(layout):
            row = pl.multiple_of(jnp.bitwise_xor(step_at, offset) * tokens, tokens)
            for group in range(count):
                yield pltpu.make_async_copy(
                    pieces[index].at[group], a_held.at[start + group, pl.ds(row, tokens)], a_sems.at[index, group]
                )

    def w_copy(half, away):
        group = lax.rem(position + away, size)
        at = jnp.bitwise_xor(core, half)
        if joined:
            span = pl.ds(pl.multiple_of(at * width, 128), width)
            target = w_held.at[0, group, :, span]
        else:
            target = w_held.at[at, group]
        return pltpu.make_async_copy(weights[half * size + away], target, w_sems.at[half, away])

    for copy in a_copies():
        copy.start()
    for away in range(size):
        for half in range(2):
            w_copy(half, away).start()
    for copy in a_copies():
        copy.wait()
    for away in range(size):
        group = lax.rem(position + away, size)
        for half in range(2):
            w_copy(half, away).wait()
        for half in range(halves):
            part = jnp.dot(a_held[group], w_held[half, group], preferred_element_type=jnp.float32)
            part = part.astype(jnp.bfloat16).astype(jnp.float32)
            if away == 0:
                total[half] = part
            else:
                total[half] += part
    for half in range(halves):
        span = slice(half * span_width, (half + 1) * span_width)
        reached = None
        for step in range(steps):
            told = jnp.bitwise_xor(step_at, step)
            branch = total[half, step * tokens : (step + 1) * tokens] * gates[pl.ds(told, 1), span]
            out[step, 0, :, span] = branch.astype(jnp.bfloat16)
            drift = branch * widths[told]
            reached = drift if step == 0 else reached + drift
            out[step, 1, :, span] = reached.astype(jnp.bfloat16)


def project_out(place, widths, gathered, weights, gates):
    size = lax.axis_size("head")
    steps = len(gathered)
    _, tokens, inner = gathered[0][0].shape
    width = weights[0][0].shape[1]
    layout, pieces = [], []
    for offset, held in enumerate(gathered):
        start = 0
        for piece in held:
            layout.append((offset, start, piece.shape[0]))
            pieces.append(piece)
            start += piece.shape[0]
    rows = steps * tokens
    halves = 1 if width % 128 == 0 else 2
    operands = pieces + [w for half in weights for w in half]
    return pl.pallas_call(
        functools.partial(out_kernel, size, tuple(layout)),
        in_specs=[SMEM, SMEM] + [ANY] * len(operands) + [VMEM],
        out_specs=VMEM,
        out_shape=jax.ShapeDtypeStruct((steps, 2, tokens, 2 * width), jnp.bfloat16),
        scratch_shapes=[
            pltpu.VMEM((size, rows, inner), jnp.bfloat16),
            pltpu.VMEM((halves, size, inner, 2 * width // halves), jnp.bfloat16),
            pltpu.VMEM((halves, rows, 2 * width // halves), jnp.float32),
            pltpu.SemaphoreType.DMA((len(layout), size)),
            pltpu.SemaphoreType.DMA((2, size)),
        ],
        compiler_params=params(),
        cost_estimate=cost(4 * rows * size * inner * width, 2 * size * inner * (rows + 2 * width) + 8 * rows * width),
        name="project_out",
    )(place, widths, *operands, gates)


def finish_kernel(base, arrived, reached, update):
    reached[...] = base[...] + arrived[0, 1].astype(jnp.float32)
    update[...] = arrived[0, 0]


def finish(base, arrived):
    steps, _, tokens, width = arrived.shape
    by_columns = pl.BlockSpec((tokens, width), lambda i: (0, i))
    return pl.pallas_call(
        finish_kernel,
        grid=(steps,),
        in_specs=[by_columns, pl.BlockSpec((1, 2, tokens, width), lambda i: (i, 0, 0, 0))],
        out_specs=[by_columns, by_columns],
        out_shape=[jax.ShapeDtypeStruct(base.shape, jnp.float32), jax.ShapeDtypeStruct(base.shape, jnp.bfloat16)],
        compiler_params=params(),
        cost_estimate=cost(base.size, 14 * base.size),
        name="finish",
    )(base, arrived)


def body(states, timesteps, lengths, modulation, w_query, w_key, w_value, w_out, q_gain, k_gain):
    steps, size = lax.axis_size("step"), lax.axis_size("head")
    step, core, position = (lax.axis_index(axis) for axis in ("step", "fsdp", "head"))
    current = states[0, 0]
    shift = (position >= size // 2).astype(jnp.int32)
    place = jnp.stack([step, core, position, lengths[0], shift]).astype(jnp.int32)

    mine, other = modulate(place, current, modulation, steps)
    tokens = jnp.stack([mine, swap(other, "fsdp", 1)])
    below, above = [tokens], [tokens]

    def hop(awaited=()):
        count = len(below)
        up, down = below[-1], above[-1]
        if awaited:
            up, down = after((up, down), *awaited)
        below.append(lax.ppermute(up, "head", [(i, i + 1) for i in range(count - 1, size - 1)]))
        above.append(lax.ppermute(down, "head", [(i, i - 1) for i in range(1, size - count + 1)]))
        return below[-1], above[-1]

    w_both = jnp.concatenate([w_query, w_key], axis=1)
    hop()
    if steps == 4 and size > 3 and w_value.shape[1] % 768 == 0:

        def line_hops(awaited):
            arrived = (below[-1], above[-1])
            hop(awaited)
            return arrived

        both_shards, last_round, finished = in_rounds(w_both, w_value, line_hops)
    else:
        both = forwarded(w_both, direct(w_both))
        both_shards = placed(both)
        last_round = tuple(both[-1])

        def finished(*awaited):
            return placed(forwarded(w_value, direct(after(w_value, *awaited))))

    while len(below) < size:
        hop()
    line = below, above
    early = tuple(held[: size - 1] + [held[0]] for held in line)
    first_here, first_there = project(place, early, both_shards, "first", "first")
    ended = (below[-1], above[-1]) + last_round
    first_there = after(first_there, *ended)
    v_shards = finished(*ended, first_here)
    parts = [first_here, swap(first_there, "fsdp", 1)]
    last_here, last_there = project(place, line, both_shards, "last", "last")
    parts += [last_here, swap(after(last_there, v_shards[-1][0], v_shards[-2][0]), "fsdp", 1)]
    own_squares = norms(place, parts, size)
    squares = lax.all_to_all(own_squares, "head", 0, 0)

    below, above = [w_out], [w_out]
    for count in range(1, size):
        up, down = below[-1], above[-1]
        if count == 1:
            up, down = after((up, down), *ended, first_here)
        if count == size - 1:
            up, down = after((up, down), quarter)
        below.append(lax.ppermute(up, "head", [(i, i + 1) for i in range(count - 1, size - 1)]))
        above.append(lax.ppermute(down, "head", [(i, i - 1) for i in range(1, size - count + 1)]))
        if count == 1:
            v_place = after(place, own_squares, below[-1], above[-1])
            v_here, v_there = project(v_place, line, v_shards, "all", "value")
            v_parts = [v_here, swap(v_there, "fsdp", 1)]
            probs = probabilities(place, after(squares, v_here), parts, q_gain, k_gain)
        if count == size - 2:
            attended = attend(place, after(probs, below[-1], above[-1]), v_parts, size)
            quarter = lax.all_to_all(attended, "head", 0, 0)

    step_width = (timesteps[0, 1] - timesteps[0, 0]).astype(jnp.float32) / 1000.0
    carried = step_width * current + jnp.where(step == 0, current, jnp.zeros_like(current))
    base, total = carried, carried
    swapped = []
    for bit in bits_of("step"):
        swapped.append(swap(after(total.astype(jnp.bfloat16), own_squares, v_shards[-1][0], v_shards[-2][0]), "step", bit))
        brought = swapped[-1].astype(jnp.float32)
        base = base + jnp.where(jnp.bitwise_and(step, bit) != 0, brought, jnp.zeros_like(brought))
        total = total + brought

    columns = current.shape[1] // steps
    told = jnp.concatenate([modulation[0, 2], jnp.full((HD,), step_width)])[None]
    sent_told = after(told, probs)
    heard = jnp.concatenate([told] + [swap(sent_told, "step", offset) for offset in range(1, steps)])
    gates = lax.dynamic_slice(heard, (0, step * columns), (steps, columns))

    quarter = after(quarter, swapped[-1], heard)
    gathered = forwarded(quarter, direct(quarter))

    own_columns = [w_out] + [
        jnp.where(position + away < size, above[away], below[size - away]) for away in range(1, size)
    ]
    out_weights = (own_columns, [swap(w, "fsdp", 1) for w in own_columns])

    sent = project_out(place, heard[:, -1], gathered, out_weights, gates)
    arrived = lax.all_to_all(sent, "step", 0, 0)
    reached, update = finish(base, arrived)
    return reached[None, None], update[None, None]


def solution(mesh):
    in_specs = (
        P("step", "fsdp", "head", None),
        P("step", None),
        P("fsdp"),
        P("step", None, None),
        P(("step", "fsdp"), "head"),
        P(("step", "fsdp"), "head"),
        P(("step", "fsdp"), "head"),
        P("head", ("step", "fsdp")),
        P("head"),
        P("head"),
    )
    out_specs = (P("step", "fsdp", "head", None), P("step", "fsdp", "head", None))
    return jax.shard_map(body, mesh=mesh, in_specs=in_specs, out_specs=out_specs, check_vma=False)
```

```python
import functools
import math

import jax
import jax.numpy as jnp
from jax import lax
from jax.experimental import pallas as pl
from jax.experimental.pallas import tpu as pltpu
from jax.sharding import PartitionSpec as P

HD = 128
MIB = 1 << 20
SMEM = pl.BlockSpec(memory_space=pltpu.SMEM)
VMEM = pl.BlockSpec(memory_space=pltpu.VMEM)
ANY = pl.BlockSpec(memory_space=pl.ANY)


def swap(x, axis, offset):
    return lax.ppermute(x, axis, [(i, i ^ offset) for i in range(lax.axis_size(axis))])


def bits_of(axis):
    return [1 << bit for bit in range(lax.axis_size(axis).bit_length() - 1)]


def direct(x):
    return {bit: [swap(x, "step", bit)] for bit in bits_of("step")}


def forwarded(x, near, *awaited):
    held = {0: [x], **near}
    half = x.shape[0] // 2
    for offset in range(1, lax.axis_size("step")):
        low, high = offset & -offset, 1 << (offset.bit_length() - 1)
        if offset in held:
            continue
        top, bottom = held[offset ^ low], held[offset ^ high]
        top = top[0][:half] if len(top) == 1 else top[0]
        bottom = bottom[0][half:] if len(bottom) == 1 else bottom[1]
        if awaited:
            top, bottom = after((top, bottom), *awaited)
        held[offset] = [swap(top, "step", low), swap(bottom, "step", high)]
    return [held[offset] for offset in range(lax.axis_size("step"))]


def placed(held, column=0):
    found = []
    for offset, pieces in enumerate(held):
        row = 0
        for piece in pieces:
            found.append((piece, offset, row, 0, column, piece.shape[1]))
            row += piece.shape[0]
    return found


def in_rounds(w_both, w_value, line_hops):
    width = w_value.shape[1]
    part = width // 768 * 256
    rest = width - part
    a1, a2 = swap(w_both, "step", 1), swap(w_both, "step", 2)
    hop = line_hops((a1, a2))
    a1, a2 = after((a1, a2), *hop)
    b1 = swap(jnp.concatenate([a2[:, :width], w_value[:, :part]], axis=1), "step", 1)
    b2 = swap(jnp.concatenate([a1[:, width:], w_value[:, :part]], axis=1), "step", 2)
    hop = line_hops((b1, b2))
    e1, e2 = after((b1, b2), *hop)
    middle = width + part // 2
    c1 = swap(jnp.concatenate([w_value[:, part:], e2[:, width:middle]], axis=1), "step", 1)
    c2 = swap(jnp.concatenate([w_value[:, part:], e1[:, middle:]], axis=1), "step", 2)
    both = [
        (w_both, 0, 0, 0, 0, 2 * width),
        (a1, 1, 0, 0, 0, 2 * width),
        (a2, 2, 0, 0, 0, 2 * width),
        (b1, 3, 0, 0, 0, width),
        (b2, 3, 0, 0, width, width),
    ]

    def finished(*awaited):
        f1, f2 = after((c1, c2), *awaited)
        d1 = swap(f2[:, : rest // 2], "step", 1)
        d2 = swap(f1[:, rest // 2 : rest], "step", 2)
        return [
            (w_value, 0, 0, 0, 0, width),
            (b1, 1, 0, width, 0, part),
            (c1, 1, 0, 0, part, rest),
            (b2, 2, 0, width, 0, part),
            (c2, 2, 0, 0, part, rest),
            (c1, 3, 0, rest, 0, part // 2),
            (c2, 3, 0, rest, part // 2, part // 2),
            (d1, 3, 0, 0, part, rest // 2),
            (d2, 3, 0, 0, part + rest // 2, rest // 2),
        ]

    return both, (c1, c2), finished


def after(x, *others):
    return lax.optimization_barrier((x,) + others)[0]


def params(mib=56):
    return pltpu.CompilerParams(vmem_limit_bytes=mib * MIB)


def cost(flops, moved, raised=0):
    return pl.CostEstimate(flops=int(flops) // 4, bytes_accessed=int(moved) // 4, transcendentals=int(raised) // 4)


def modulate_kernel(steps, place, states, rows, mine, other):
    current = states[...]
    centre = jnp.mean(current, axis=-1, keepdims=True)
    centred = current - centre
    spread_of = jnp.mean(centred * centred, axis=-1, keepdims=True)
    shift, scale = rows[0, 0:1, :], rows[0, 1:2, :]
    modulated = (centred * lax.rsqrt(spread_of + 1e-06) * (1.0 + scale) + shift).astype(jnp.bfloat16)
    core = place[1]
    for block in range(2 * steps):
        width = modulated.shape[1] // (2 * steps)
        piece = modulated[:, block * width : (block + 1) * width]
        at = slice(block // 2 * width, (block // 2 + 1) * width)

        @pl.when(core == block % 2)
        def _(piece=piece, at=at):
            mine[:, at] = piece

        @pl.when(core != block % 2)
        def _(piece=piece, at=at):
            other[:, at] = piece


def modulate(place, states, rows, steps):
    tokens, width = states.shape
    tile = 32
    out = jax.ShapeDtypeStruct((tokens, width // 2), jnp.bfloat16)
    spec = pl.BlockSpec((tile, width // 2), lambda i: (i, 0))
    return pl.pallas_call(
        functools.partial(modulate_kernel, steps),
        grid=(tokens // tile,),
        in_specs=[SMEM, pl.BlockSpec((tile, width), lambda i: (i, 0)), pl.BlockSpec(rows.shape, lambda i: (0, 0, 0))],
        out_specs=[spec, spec],
        out_shape=[out, out],
        compiler_params=params(),
        cost_estimate=cost(10 * tokens * width, 6 * tokens * width),
        name="modulate",
    )(place, states, rows)


def project_kernel(size, parts, shard, layout, place, *refs):
    count = 2 * size - 1
    own, below, above = refs[0], refs[1:size], refs[size:count]
    weights = refs[count : count + len(layout)]
    here, there, x_held, w_held, x_sems, w_sems = refs[count + len(layout) :]
    tokens, depth = own.shape[1:]
    step_at, position, shift = place[0], place[2], place[4]
    early = size - 1
    blocks = {"first": range(early), "last": range(early, size), "all": range(size)}[parts]

    def x_copy(ref, clip, block):
        row = (clip * len(blocks) + block - blocks[0]) * tokens
        return pltpu.make_async_copy(
            ref.at[clip], x_held.at[pl.ds(pl.multiple_of(row, tokens), tokens)], x_sems.at[clip, block]
        )

    def w_copies():
        for index, (ref, (offset, row, source, target, count)) in enumerate(zip(weights, layout)):
            at = jnp.bitwise_xor(step_at, offset) * shard + row
            rows = ref.shape[0]
            part = w_held.at[pl.ds(pl.multiple_of(at, rows), rows), pl.ds(target, count)]
            yield pltpu.make_async_copy(ref.at[:, pl.ds(source, count)], part, w_sems.at[index])

    for copy in w_copies():
        copy.start()
    for clip in range(2):
        for away in range(size):
            for sign, held in ((1, above), (-1, below)):
                if away == 0 and sign < 0:
                    continue
                source = own if away == 0 else held[away - 1]
                block_at = position + sign * away
                block = lax.rem(block_at - shift + size, size)
                inside = jnp.logical_and(block_at >= 0, block_at < size)
                inside = jnp.logical_and(inside, jnp.logical_and(block >= blocks[0], block <= blocks[-1]))

                @pl.when(inside)
                def _(source=source, block=block, clip=clip):
                    x_copy(source, clip, block).start()

    for copy in w_copies():
        copy.wait()
    for clip in range(2):
        for block in blocks:
            x_copy(own, clip, block).wait()
    rows, columns = here.shape
    width = columns if columns % 512 else columns // 2
    for start in range(0, columns, width):
        span = slice(start, start + width)
        product = jnp.dot(x_held[...], w_held[:, span], preferred_element_type=jnp.float32)
        here[:, span] = product[:rows]
        there[:, span] = product[rows:]


def project(place, line, shards, parts, name):
    size = lax.axis_size("head")
    below, above = line
    operands = [below[0]] + below[1:] + above[1:]
    _, tokens, depth = operands[0].shape
    weights = [piece[0] for piece in shards]
    layout = [piece[1:] for piece in shards]
    shard, columns = weights[0].shape
    rows = {"first": size - 1, "last": 1, "all": size}[parts] * tokens
    out = jax.ShapeDtypeStruct((rows, columns), jnp.float32)
    moved = 2 * depth * (2 * rows + columns) + 8 * rows * columns
    return pl.pallas_call(
        functools.partial(project_kernel, size, parts, shard, tuple(layout)),
        in_specs=[SMEM] + [ANY] * (len(operands) + len(weights)),
        out_specs=[VMEM, VMEM],
        out_shape=[out, out],
        scratch_shapes=[
            pltpu.VMEM((2 * rows, depth), jnp.bfloat16),
            pltpu.VMEM((depth, columns), jnp.bfloat16),
            pltpu.SemaphoreType.DMA((2, size)),
            pltpu.SemaphoreType.DMA((len(layout),)),
        ],
        compiler_params=params(),
        cost_estimate=cost(4 * rows * depth * columns, moved),
        name=name,
    )(place, *operands, *weights)


def norms_kernel(place, first_a, first_b, last_a, last_b, out):
    width = first_a.shape[1] // 2
    rows = []
    for which in range(2):
        found = []
        for one, other in ((first_a, first_b), (last_a, last_b)):
            lanes = None
            for start in range(which * width, (which + 1) * width, HD):
                total = one[:, start : start + HD] + other[:, start : start + HD]
                lanes = total * total if lanes is None else lanes + total * total
            found.append(jnp.sum(lanes.T, axis=0, keepdims=True))
        straight = jnp.concatenate(found, axis=1)
        wrapped = jnp.concatenate(found[::-1], axis=1)
        rows.append(jnp.where(place[4] == 0, straight, wrapped))
    both = jnp.concatenate(rows, axis=0)
    for peer in range(out.shape[0]):
        out[peer] = both


def norms(place, parts, size):
    rows = parts[0].shape[0] + parts[2].shape[0]
    return pl.pallas_call(
        norms_kernel,
        in_specs=[SMEM] + [VMEM] * 4,
        out_specs=VMEM,
        out_shape=jax.ShapeDtypeStruct((size, 2, rows), jnp.float32),
        compiler_params=params(),
        cost_estimate=cost(4 * rows * parts[0].shape[1], 8 * rows * parts[0].shape[1]),
        name="norms",
    )(place, *parts)


def probs_kernel(tokens, full_width, place, squares, *refs):
    parts, (q_gain, k_gain, out, scales) = refs[:8], refs[8:]
    rows = scales.shape[1]

    @pl.when(pl.program_id(0) == 0)
    def _():
        total = squares[0]
        for peer in range(1, squares.shape[0]):
            total = total + squares[peer]
        turned = jnp.concatenate([total[:, tokens:], total[:, :tokens]], axis=1)
        total = jnp.where(place[4] == 0, total, turned)
        scale = lax.rsqrt(total / full_width + 1e-06)
        for which in range(2):
            scales[which] = jnp.broadcast_to(scale[which : which + 1], (HD, rows)).T

    column = lax.broadcasted_iota(jnp.int32, (1, rows), 1) + place[4] * tokens
    valid = jnp.where(column >= rows, column - rows, column) < place[3]
    for head in range(out.shape[0]):
        span = slice(head * HD, (head + 1) * HD)

        def normed(at, gain, which):
            joined = [parts[at + i][:, span] + parts[at + i + 1][:, span] for i in (0, 2)]
            return (jnp.concatenate(joined) * scales[which] * gain[:, span]).astype(jnp.bfloat16)

        queries, keys = normed(0, q_gain, 0), normed(4, k_gain, 1)
        scores = lax.dot_general(queries, keys, (((1,), (1,)), ((), ())), preferred_element_type=jnp.float32)
        scores = jnp.where(valid, scores * (1.0 / math.sqrt(HD)), -jnp.inf)
        raised = jnp.exp(scores - jnp.max(scores, axis=-1, keepdims=True))
        out[head] = (raised * (1.0 / jnp.sum(raised, axis=-1, keepdims=True))).astype(jnp.bfloat16)


def at_once(heads):
    return 2 if heads % 2 == 0 else 1


def probabilities(place, squares, parts, q_gain, k_gain):
    columns = parts[0].shape[1] // 2
    rows = parts[0].shape[0] + parts[2].shape[0]
    heads = columns // HD
    group = at_once(heads)
    q_blocks = [pl.BlockSpec((part.shape[0], group * HD), lambda i: (0, i)) for part in parts]
    k_blocks = [pl.BlockSpec((part.shape[0], group * HD), lambda i: (0, i + heads // group)) for part in parts]
    gain = pl.BlockSpec((1, group * HD), lambda i: (0, i))
    return pl.pallas_call(
        functools.partial(probs_kernel, parts[2].shape[0], float(columns * squares.shape[0])),
        grid=(heads // group,),
        in_specs=[SMEM, pl.BlockSpec(squares.shape, lambda i: (0, 0, 0))] + q_blocks + k_blocks + [gain] * 2,
        out_specs=pl.BlockSpec((group, rows, rows), lambda i: (i, 0, 0)),
        out_shape=jax.ShapeDtypeStruct((heads, rows, rows), jnp.bfloat16),
        scratch_shapes=[pltpu.VMEM((2, rows, HD), jnp.float32)],
        compiler_params=params(),
        cost_estimate=cost(2 * heads * rows * rows * HD, 16 * rows * columns + 2 * heads * rows * rows, heads * rows * rows),
        name="probs",
    )(place, squares, *parts, *parts, q_gain[None], k_gain[None])


def attend_kernel(place, probs, v_a, v_b, out, held):
    size, tokens, _ = out.shape
    for head in range(probs.shape[0]):
        span = slice(head * HD, (head + 1) * HD)
        values = (v_a[:, span] + v_b[:, span]).astype(jnp.bfloat16)
        held[:, span] = jnp.dot(probs[head], values, preferred_element_type=jnp.float32)
    for block in range(size):
        at = lax.rem(block - place[4] + size, size) * tokens
        out[block] = held[pl.ds(pl.multiple_of(at, tokens), tokens)].astype(jnp.bfloat16)


def attend(place, probs, v_parts, size):
    heads, rows, _ = probs.shape
    tokens = rows // size
    group = at_once(heads)
    by_head = pl.BlockSpec((rows, group * HD), lambda i: (0, i))
    return pl.pallas_call(
        attend_kernel,
        grid=(heads // group,),
        in_specs=[SMEM, pl.BlockSpec((group, rows, rows), lambda i: (i, 0, 0)), by_head, by_head],
        out_specs=pl.BlockSpec((size, tokens, group * HD), lambda i: (0, 0, i)),
        out_shape=jax.ShapeDtypeStruct((size, tokens, heads * HD), jnp.bfloat16),
        scratch_shapes=[pltpu.VMEM((rows, group * HD), jnp.float32)],
        compiler_params=params(),
        cost_estimate=cost(2 * heads * rows * rows * HD, 2 * heads * rows * rows + 10 * rows * heads * HD),
        name="attend",
    )(place, probs, *v_parts)


def out_kernel(size, layout, place, widths, *refs):
    count = 2 * size - 1
    pieces, weights = refs[: len(layout)], refs[len(layout) : len(layout) + 2 * count]
    gates, out, a_held, w_held, total, a_sems, w_sems = refs[len(layout) + 2 * count :]
    steps, _, tokens, columns = out.shape
    width = columns // 2
    halves, _, _, span_width = w_held.shape
    joined = halves == 1
    step_at, core, position = place[0], place[1], place[2]

    def a_copies():
        for index, (offset, start, groups) in enumerate(layout):
            row = pl.multiple_of(jnp.bitwise_xor(step_at, offset) * tokens, tokens)
            for group in range(groups):
                yield pltpu.make_async_copy(
                    pieces[index].at[group], a_held.at[start + group, pl.ds(row, tokens)], a_sems.at[index, group]
                )

    def w_copy(half, away, slot):
        group = lax.rem(position + away, size)
        at = jnp.bitwise_xor(core, half)
        if joined:
            span = pl.ds(pl.multiple_of(at * width, 128), width)
            target = w_held.at[0, group, :, span]
        else:
            target = w_held.at[at, group]
        return pltpu.make_async_copy(weights[half * count + slot], target, w_sems.at[half, away])

    for copy in a_copies():
        copy.start()
    for away in range(size):
        for half in range(2):
            if away == 0:
                w_copy(half, 0, 0).start()
                continue

            @pl.when(position + away < size)
            def _(half=half, away=away):
                w_copy(half, away, size - 1 + away).start()

            @pl.when(position + away >= size)
            def _(half=half, away=away):
                w_copy(half, away, size - away).start()

    for copy in a_copies():
        copy.wait()
    for away in range(size):
        group = lax.rem(position + away, size)
        for half in range(2):
            w_copy(half, away, 0).wait()
        for half in range(halves):
            part = jnp.dot(a_held[group], w_held[half, group], preferred_element_type=jnp.float32)
            part = part.astype(jnp.bfloat16).astype(jnp.float32)
            if away == 0:
                total[half] = part
            else:
                total[half] += part
    for half in range(halves):
        span = slice(half * span_width, (half + 1) * span_width)
        reached = None
        for step in range(steps):
            told = jnp.bitwise_xor(step_at, step)
            branch = total[half, step * tokens : (step + 1) * tokens] * gates[pl.ds(told, 1), span]
            out[step, 0, :, span] = branch.astype(jnp.bfloat16)
            drift = branch * widths[told]
            reached = drift if step == 0 else reached + drift
            out[step, 1, :, span] = reached.astype(jnp.bfloat16)


def project_out(place, widths, gathered, weights, gates):
    size = lax.axis_size("head")
    steps = len(gathered)
    _, tokens, inner = gathered[0][0].shape
    width = weights[0][0].shape[1]
    layout, pieces = [], []
    for offset, held in enumerate(gathered):
        start = 0
        for piece in held:
            layout.append((offset, start, piece.shape[0]))
            pieces.append(piece)
            start += piece.shape[0]
    rows = steps * tokens
    halves = 1 if width % 128 == 0 else 2
    operands = pieces + [w for half in weights for w in half]
    return pl.pallas_call(
        functools.partial(out_kernel, size, tuple(layout)),
        in_specs=[SMEM, SMEM] + [ANY] * len(operands) + [VMEM],
        out_specs=VMEM,
        out_shape=jax.ShapeDtypeStruct((steps, 2, tokens, 2 * width), jnp.bfloat16),
        scratch_shapes=[
            pltpu.VMEM((size, rows, inner), jnp.bfloat16),
            pltpu.VMEM((halves, size, inner, 2 * width // halves), jnp.bfloat16),
            pltpu.VMEM((halves, rows, 2 * width // halves), jnp.float32),
            pltpu.SemaphoreType.DMA((len(layout), size)),
            pltpu.SemaphoreType.DMA((2, size)),
        ],
        compiler_params=params(),
        cost_estimate=cost(4 * rows * size * inner * width, 2 * size * inner * (rows + 2 * width) + 8 * rows * width),
        name="project_out",
    )(place, widths, *operands, gates)


def finish_kernel(base, arrived, reached, update):
    reached[...] = base[...] + arrived[0, 1].astype(jnp.float32)
    update[...] = arrived[0, 0]


def finish(base, arrived):
    steps, _, tokens, width = arrived.shape
    by_columns = pl.BlockSpec((tokens, width), lambda i: (0, i))
    return pl.pallas_call(
        finish_kernel,
        grid=(steps,),
        in_specs=[by_columns, pl.BlockSpec((1, 2, tokens, width), lambda i: (i, 0, 0, 0))],
        out_specs=[by_columns, by_columns],
        out_shape=[jax.ShapeDtypeStruct(base.shape, jnp.float32), jax.ShapeDtypeStruct(base.shape, jnp.bfloat16)],
        compiler_params=params(),
        cost_estimate=cost(base.size, 14 * base.size),
        name="finish",
    )(base, arrived)


def body(states, timesteps, lengths, modulation, w_query, w_key, w_value, w_out, q_gain, k_gain):
    steps, size = lax.axis_size("step"), lax.axis_size("head")
    step, core, position = (lax.axis_index(axis) for axis in ("step", "fsdp", "head"))
    current = states[0, 0]
    shift = (position >= size // 2).astype(jnp.int32)
    place = jnp.stack([step, core, position, lengths[0], shift]).astype(jnp.int32)

    w_both = jnp.concatenate([w_query, w_key], axis=1)
    mine, other = modulate(place, after(current, w_both), modulation, steps)
    tokens = jnp.stack([mine, swap(other, "fsdp", 1)])
    below, above = [tokens], [tokens]

    def hop(awaited=()):
        count = len(below)
        up, down = below[-1], above[-1]
        if awaited:
            up, down = after((up, down), *awaited)
        below.append(lax.ppermute(up, "head", [(i, i + 1) for i in range(count - 1, size - 1)]))
        above.append(lax.ppermute(down, "head", [(i, i - 1) for i in range(1, size - count + 1)]))
        return below[-1], above[-1]

    hop()
    if steps == 4 and size > 3 and w_value.shape[1] % 768 == 0:

        def line_hops(awaited):
            arrived = (below[-1], above[-1])
            hop(awaited)
            return arrived

        both_shards, last_round, finished = in_rounds(w_both, w_value, line_hops)
    else:
        both = forwarded(w_both, direct(w_both))
        both_shards = placed(both)
        last_round = tuple(both[-1])

        def finished(*awaited):
            return placed(forwarded(w_value, direct(after(w_value, *awaited))))

    while len(below) < size:
        hop()
    line = below, above
    early = tuple(held[: size - 1] + [held[0]] for held in line)
    first_here, first_there = project(place, early, both_shards, "first", "first")

    step_width = (timesteps[0, 1] - timesteps[0, 0]).astype(jnp.float32) / 1000.0
    carried = step_width * current + jnp.where(step == 0, current, jnp.zeros_like(current))
    base, total = carried, carried
    swapped = []

    def add_states(base, total, bit, awaited):
        swapped.append(swap(after(total.astype(jnp.bfloat16), *awaited), "step", bit))
        brought = swapped[-1].astype(jnp.float32)
        return base + jnp.where(jnp.bitwise_and(step, bit) != 0, brought, jnp.zeros_like(brought)), total + brought

    awaited = (early[0][-2], early[1][-2], both_shards[-1][0], both_shards[-2][0])
    base, total = add_states(base, total, 1, awaited)
    ended = (below[-1], above[-1]) + last_round
    first_there = after(first_there, *ended)
    v_shards = finished(*ended, first_here)
    for bit in bits_of("step")[1:]:
        base, total = add_states(base, total, bit, (v_shards[-1][0], v_shards[-2][0]))
    parts = [first_here, swap(first_there, "fsdp", 1)]
    last_here, last_there = project(place, line, both_shards, "last", "last")
    parts += [last_here, swap(after(last_there, v_shards[-1][0], v_shards[-2][0]), "fsdp", 1)]
    own_squares = norms(place, parts, size)
    squares = lax.all_to_all(own_squares, "head", 0, 0)

    columns = current.shape[1] // steps
    told = jnp.concatenate([modulation[0, 2], jnp.full((HD,), step_width)])[None]
    sent_told = after(told, own_squares)
    heard = jnp.concatenate([told] + [swap(sent_told, "step", offset) for offset in range(1, steps)])
    gates = lax.dynamic_slice(heard, (0, step * columns), (steps, columns))

    below, above = [w_out], [w_out]
    for count in range(1, size):
        up, down = below[-1], above[-1]
        if count == 1:
            up, down = after((up, down), *ended, first_here)
        if count == size - 1:
            up, down = after((up, down), quarter)
        below.append(lax.ppermute(up, "head", [(i, i + 1) for i in range(count - 1, size - 1)]))
        above.append(lax.ppermute(down, "head", [(i, i - 1) for i in range(1, size - count + 1)]))
        if count == 1:
            v_place = after(place, squares, below[-1], above[-1], heard, swapped[-1])
            v_here, v_there = project(v_place, line, v_shards, "all", "value")
            v_parts = [v_here, swap(v_there, "fsdp", 1)]
            probs = probabilities(place, squares, parts, q_gain, k_gain)
        if count == size - 2:
            attended = attend(place, probs, v_parts, size)
            quarter = lax.all_to_all(attended, "head", 0, 0)

    gathered = forwarded(quarter, direct(quarter))

    raw = [w_out] + below[1:] + above[1:]
    out_weights = (raw, [swap(w, "fsdp", 1) for w in raw])

    sent = project_out(place, heard[:, -1], gathered, out_weights, gates)
    arrived = lax.all_to_all(sent, "step", 0, 0)
    reached, update = finish(base, arrived)
    return reached[None, None], update[None, None]


def solution(mesh):
    in_specs = (
        P("step", "fsdp", "head", None),
        P("step", None),
        P("fsdp"),
        P("step", None, None),
        P(("step", "fsdp"), "head"),
        P(("step", "fsdp"), "head"),
        P(("step", "fsdp"), "head"),
        P("head", ("step", "fsdp")),
        P("head"),
        P("head"),
    )
    out_specs = (P("step", "fsdp", "head", None), P("step", "fsdp", "head", None))
    return jax.shard_map(body, mesh=mesh, in_specs=in_specs, out_specs=out_specs, check_vma=False)
```

```python
import functools
import math

import jax
import jax.numpy as jnp
from jax import lax
from jax.experimental import pallas as pl
from jax.experimental.pallas import tpu as pltpu
from jax.sharding import PartitionSpec as P

HD = 128
MIB = 1 << 20
SMEM = pl.BlockSpec(memory_space=pltpu.SMEM)
VMEM = pl.BlockSpec(memory_space=pltpu.VMEM)
ANY = pl.BlockSpec(memory_space=pl.ANY)


def swap(x, axis, offset):
    return lax.ppermute(x, axis, [(i, i ^ offset) for i in range(lax.axis_size(axis))])


def bits_of(axis):
    return [1 << bit for bit in range(lax.axis_size(axis).bit_length() - 1)]


def direct(x):
    return {bit: [swap(x, "step", bit)] for bit in bits_of("step")}


def forwarded(x, near, *awaited):
    held = {0: [x], **near}
    half = x.shape[0] // 2
    for offset in range(1, lax.axis_size("step")):
        low, high = offset & -offset, 1 << (offset.bit_length() - 1)
        if offset in held:
            continue
        top, bottom = held[offset ^ low], held[offset ^ high]
        top = top[0][:half] if len(top) == 1 else top[0]
        bottom = bottom[0][half:] if len(bottom) == 1 else bottom[1]
        if awaited:
            top, bottom = after((top, bottom), *awaited)
        held[offset] = [swap(top, "step", low), swap(bottom, "step", high)]
    return [held[offset] for offset in range(lax.axis_size("step"))]


def placed(held, column=0):
    found = []
    for offset, pieces in enumerate(held):
        row = 0
        for piece in pieces:
            found.append((piece, offset, row, 0, column, piece.shape[1]))
            row += piece.shape[0]
    return found


def in_rounds(w_both, w_value, hop):
    width = w_value.shape[1]
    a1, a2 = swap(w_both, "step", 1), swap(w_both, "step", 2)
    e1, e2 = after((a1, a2), *hop())
    b1, b2 = swap(e2[:, :width], "step", 1), swap(e1[:, width:], "step", 2)
    v1, v2 = after((w_value, w_value), b1, b2, *hop(b1, b2))
    c1, c2 = swap(v1, "step", 1), swap(v2, "step", 2)
    both = [
        (w_both, 0, 0, 0, 0, 2 * width),
        (a1, 1, 0, 0, 0, 2 * width),
        (a2, 2, 0, 0, 0, 2 * width),
        (b1, 3, 0, 0, 0, width),
        (b2, 3, 0, 0, width, width),
    ]

    def finished(*awaited):
        f1, f2 = after((c1, c2), *awaited)
        d1, d2 = swap(f2[:, : width // 2], "step", 1), swap(f1[:, width // 2 :], "step", 2)
        whole = [(w_value, 0, 0, 0, 0, width), (c1, 1, 0, 0, 0, width), (c2, 2, 0, 0, 0, width)]
        return whole + [(d1, 3, 0, 0, 0, width // 2), (d2, 3, 0, 0, width // 2, width // 2)]

    return both, (c1, c2), finished


def after(x, *others):
    return lax.optimization_barrier((x,) + others)[0]


def params(mib=56):
    return pltpu.CompilerParams(vmem_limit_bytes=mib * MIB)


def cost(flops, moved, raised=0):
    return pl.CostEstimate(flops=int(flops) // 4, bytes_accessed=int(moved) // 4, transcendentals=int(raised) // 4)


def modulate_kernel(steps, place, states, rows, mine, other):
    current = states[...]
    centre = jnp.mean(current, axis=-1, keepdims=True)
    centred = current - centre
    spread_of = jnp.mean(centred * centred, axis=-1, keepdims=True)
    shift, scale = rows[0, 0:1, :], rows[0, 1:2, :]
    modulated = (centred * lax.rsqrt(spread_of + 1e-06) * (1.0 + scale) + shift).astype(jnp.bfloat16)
    core = place[1]
    for block in range(2 * steps):
        width = modulated.shape[1] // (2 * steps)
        piece = modulated[:, block * width : (block + 1) * width]
        at = slice(block // 2 * width, (block // 2 + 1) * width)

        @pl.when(core == block % 2)
        def _(piece=piece, at=at):
            mine[:, at] = piece

        @pl.when(core != block % 2)
        def _(piece=piece, at=at):
            other[:, at] = piece


def modulate(place, states, rows, steps):
    tokens, width = states.shape
    tile = 32
    out = jax.ShapeDtypeStruct((tokens, width // 2), jnp.bfloat16)
    spec = pl.BlockSpec((tile, width // 2), lambda i: (i, 0))
    return pl.pallas_call(
        functools.partial(modulate_kernel, steps),
        grid=(tokens // tile,),
        in_specs=[SMEM, pl.BlockSpec((tile, width), lambda i: (i, 0)), pl.BlockSpec(rows.shape, lambda i: (0, 0, 0))],
        out_specs=[spec, spec],
        out_shape=[out, out],
        compiler_params=params(),
        cost_estimate=cost(10 * tokens * width, 6 * tokens * width),
        name="modulate",
    )(place, states, rows)


def terms(x):
    high = x.astype(jnp.bfloat16).astype(jnp.float32)
    middle = (x - high).astype(jnp.bfloat16).astype(jnp.float32)
    return [high, middle, x - high - middle]


def tell_kernel(place, step_width, states, rows, out):
    current = states[...]
    tokens, columns = current.shape
    width = step_width[0]
    anchor = jnp.where(place[0] == 0, 1.0, 0.0)
    out[0, :tokens] = (width * current + anchor * current).astype(jnp.bfloat16)
    told = terms(rows[0, 2:3, :]) + terms(jnp.full((1, columns), width, jnp.float32))
    told.append(jnp.zeros((10, columns), jnp.float32))
    out[0, tokens:] = jnp.concatenate(told).astype(jnp.bfloat16)


def tell(place, step_width, states, rows, steps):
    tokens, width = states.shape
    columns = width // steps
    return pl.pallas_call(
        tell_kernel,
        grid=(steps,),
        in_specs=[
            SMEM,
            SMEM,
            pl.BlockSpec((tokens, columns), lambda i: (0, i)),
            pl.BlockSpec((1, rows.shape[1], columns), lambda i: (0, 0, i)),
        ],
        out_specs=pl.BlockSpec((1, tokens + 16, columns), lambda i: (i, 0, 0)),
        out_shape=jax.ShapeDtypeStruct((steps, tokens + 16, columns), jnp.bfloat16),
        compiler_params=params(),
        cost_estimate=cost(4 * tokens * width, 6 * tokens * width),
        name="tell",
    )(place, step_width, states, rows)


def project_kernel(size, parts, shard, layout, place, *refs):
    count = 2 * size - 1
    own, below, above = refs[0], refs[1:size], refs[size:count]
    weights = refs[count : count + len(layout)]
    here, there, x_held, w_held, x_sems, w_sems = refs[count + len(layout) :]
    tokens, depth = own.shape[1:]
    step_at, position, shift = place[0], place[2], place[4]
    early = size - 1
    blocks = {"first": range(early), "last": range(early, size), "all": range(size)}[parts]

    def x_copy(ref, clip, block):
        row = (clip * len(blocks) + block - blocks[0]) * tokens
        return pltpu.make_async_copy(
            ref.at[clip], x_held.at[pl.ds(pl.multiple_of(row, tokens), tokens)], x_sems.at[clip, block]
        )

    def w_copies():
        for index, (ref, (offset, row, source, target, count)) in enumerate(zip(weights, layout)):
            at = jnp.bitwise_xor(step_at, offset) * shard + row
            rows = ref.shape[0]
            part = w_held.at[pl.ds(pl.multiple_of(at, rows), rows), pl.ds(target, count)]
            yield pltpu.make_async_copy(ref.at[:, pl.ds(source, count)], part, w_sems.at[index])

    for copy in w_copies():
        copy.start()
    for clip in range(2):
        for away in range(size):
            for sign, held in ((1, above), (-1, below)):
                if away == 0 and sign < 0:
                    continue
                source = own if away == 0 else held[away - 1]
                block_at = position + sign * away
                block = lax.rem(block_at - shift + size, size)
                inside = jnp.logical_and(block_at >= 0, block_at < size)
                inside = jnp.logical_and(inside, jnp.logical_and(block >= blocks[0], block <= blocks[-1]))

                @pl.when(inside)
                def _(source=source, block=block, clip=clip):
                    x_copy(source, clip, block).start()

    for copy in w_copies():
        copy.wait()
    for clip in range(2):
        for block in blocks:
            x_copy(own, clip, block).wait()
    rows, columns = here.shape
    width = columns if columns % 512 else columns // 2
    for start in range(0, columns, width):
        span = slice(start, start + width)
        product = jnp.dot(x_held[...], w_held[:, span], preferred_element_type=jnp.float32)
        here[:, span] = product[:rows]
        there[:, span] = product[rows:]


def project(place, line, shards, parts, name):
    size = lax.axis_size("head")
    below, above = line
    operands = [below[0]] + below[1:] + above[1:]
    _, tokens, depth = operands[0].shape
    weights = [piece[0] for piece in shards]
    layout = [piece[1:] for piece in shards]
    shard, columns = weights[0].shape
    rows = {"first": size - 1, "last": 1, "all": size}[parts] * tokens
    out = jax.ShapeDtypeStruct((rows, columns), jnp.float32)
    moved = 2 * depth * (2 * rows + columns) + 8 * rows * columns
    return pl.pallas_call(
        functools.partial(project_kernel, size, parts, shard, tuple(layout)),
        in_specs=[SMEM] + [ANY] * (len(operands) + len(weights)),
        out_specs=[VMEM, VMEM],
        out_shape=[out, out],
        scratch_shapes=[
            pltpu.VMEM((2 * rows, depth), jnp.bfloat16),
            pltpu.VMEM((depth, columns), jnp.bfloat16),
            pltpu.SemaphoreType.DMA((2, size)),
            pltpu.SemaphoreType.DMA((len(layout),)),
        ],
        compiler_params=params(),
        cost_estimate=cost(4 * rows * depth * columns, moved),
        name=name,
    )(place, *operands, *weights)


def norms_kernel(place, first_a, first_b, last_a, last_b, out):
    width = first_a.shape[1] // 2
    rows = []
    for which in range(2):
        found = []
        for one, other in ((first_a, first_b), (last_a, last_b)):
            lanes = None
            for start in range(which * width, (which + 1) * width, HD):
                total = one[:, start : start + HD] + other[:, start : start + HD]
                lanes = total * total if lanes is None else lanes + total * total
            found.append(jnp.sum(lanes.T, axis=0, keepdims=True))
        straight = jnp.concatenate(found, axis=1)
        wrapped = jnp.concatenate(found[::-1], axis=1)
        rows.append(jnp.where(place[4] == 0, straight, wrapped))
    both = jnp.concatenate(rows, axis=0)
    for peer in range(out.shape[0]):
        out[peer] = both


def norms(place, parts, size):
    rows = parts[0].shape[0] + parts[2].shape[0]
    return pl.pallas_call(
        norms_kernel,
        in_specs=[SMEM] + [VMEM] * 4,
        out_specs=VMEM,
        out_shape=jax.ShapeDtypeStruct((size, 2, rows), jnp.float32),
        compiler_params=params(),
        cost_estimate=cost(4 * rows * parts[0].shape[1], 8 * rows * parts[0].shape[1]),
        name="norms",
    )(place, *parts)


def probs_kernel(tokens, full_width, place, squares, *refs):
    parts, (q_gain, k_gain, out, scales) = refs[:8], refs[8:]
    rows = scales.shape[1]

    @pl.when(pl.program_id(0) == 0)
    def _():
        total = squares[0]
        for peer in range(1, squares.shape[0]):
            total = total + squares[peer]
        turned = jnp.concatenate([total[:, tokens:], total[:, :tokens]], axis=1)
        total = jnp.where(place[4] == 0, total, turned)
        scale = lax.rsqrt(total / full_width + 1e-06)
        for which in range(2):
            scales[which] = jnp.broadcast_to(scale[which : which + 1], (HD, rows)).T

    column = lax.broadcasted_iota(jnp.int32, (1, rows), 1) + place[4] * tokens
    valid = jnp.where(column >= rows, column - rows, column) < place[3]
    for head in range(out.shape[0]):
        span = slice(head * HD, (head + 1) * HD)

        def normed(at, gain, which):
            joined = [parts[at + i][:, span] + parts[at + i + 1][:, span] for i in (0, 2)]
            return (jnp.concatenate(joined) * scales[which] * gain[:, span]).astype(jnp.bfloat16)

        queries, keys = normed(0, q_gain, 0), normed(4, k_gain, 1)
        scores = lax.dot_general(queries, keys, (((1,), (1,)), ((), ())), preferred_element_type=jnp.float32)
        scores = jnp.where(valid, scores * (1.0 / math.sqrt(HD)), -jnp.inf)
        raised = jnp.exp(scores - jnp.max(scores, axis=-1, keepdims=True))
        out[head] = (raised * (1.0 / jnp.sum(raised, axis=-1, keepdims=True))).astype(jnp.bfloat16)


def at_once(heads):
    return 2 if heads % 2 == 0 else 1


def probabilities(place, squares, parts, q_gain, k_gain):
    columns = parts[0].shape[1] // 2
    rows = parts[0].shape[0] + parts[2].shape[0]
    heads = columns // HD
    group = at_once(heads)
    q_blocks = [pl.BlockSpec((part.shape[0], group * HD), lambda i: (0, i)) for part in parts]
    k_blocks = [pl.BlockSpec((part.shape[0], group * HD), lambda i: (0, i + heads // group)) for part in parts]
    gain = pl.BlockSpec((1, group * HD), lambda i: (0, i))
    return pl.pallas_call(
        functools.partial(probs_kernel, parts[2].shape[0], float(columns * squares.shape[0])),
        grid=(heads // group,),
        in_specs=[SMEM, pl.BlockSpec(squares.shape, lambda i: (0, 0, 0))] + q_blocks + k_blocks + [gain] * 2,
        out_specs=pl.BlockSpec((group, rows, rows), lambda i: (i, 0, 0)),
        out_shape=jax.ShapeDtypeStruct((heads, rows, rows), jnp.bfloat16),
        scratch_shapes=[pltpu.VMEM((2, rows, HD), jnp.float32)],
        compiler_params=params(),
        cost_estimate=cost(2 * heads * rows * rows * HD, 16 * rows * columns + 2 * heads * rows * rows, heads * rows * rows),
        name="probs",
    )(place, squares, *parts, *parts, q_gain[None], k_gain[None])


def attend_kernel(place, probs, v_a, v_b, out, held):
    size, tokens, _ = out.shape
    for head in range(probs.shape[0]):
        span = slice(head * HD, (head + 1) * HD)
        values = (v_a[:, span] + v_b[:, span]).astype(jnp.bfloat16)
        held[:, span] = jnp.dot(probs[head], values, preferred_element_type=jnp.float32)
    for block in range(size):
        at = lax.rem(block - place[4] + size, size) * tokens
        out[block] = held[pl.ds(pl.multiple_of(at, tokens), tokens)].astype(jnp.bfloat16)


def attend(place, probs, v_parts, size):
    heads, rows, _ = probs.shape
    tokens = rows // size
    group = at_once(heads)
    by_head = pl.BlockSpec((rows, group * HD), lambda i: (0, i))
    return pl.pallas_call(
        attend_kernel,
        grid=(heads // group,),
        in_specs=[SMEM, pl.BlockSpec((group, rows, rows), lambda i: (i, 0, 0)), by_head, by_head],
        out_specs=pl.BlockSpec((size, tokens, group * HD), lambda i: (0, 0, i)),
        out_shape=jax.ShapeDtypeStruct((size, tokens, heads * HD), jnp.bfloat16),
        scratch_shapes=[pltpu.VMEM((rows, group * HD), jnp.float32)],
        compiler_params=params(),
        cost_estimate=cost(2 * heads * rows * rows * HD, 2 * heads * rows * rows + 10 * rows * heads * HD),
        name="attend",
    )(place, probs, *v_parts)


def out_kernel(size, layout, place, *refs):
    count = 2 * size - 1
    pieces, weights = refs[: len(layout)], refs[len(layout) : len(layout) + 2 * count]
    heard, out, a_held, w_held, total, a_sems, w_sems = refs[len(layout) + 2 * count :]
    steps, _, tokens, columns = out.shape
    width = columns // 2
    halves, _, _, span_width = w_held.shape
    joined = halves == 1
    step_at, core, position = place[0], place[1], place[2]

    def a_copies():
        for index, (offset, start, groups) in enumerate(layout):
            row = pl.multiple_of(jnp.bitwise_xor(step_at, offset) * tokens, tokens)
            for group in range(groups):
                yield pltpu.make_async_copy(
                    pieces[index].at[group], a_held.at[start + group, pl.ds(row, tokens)], a_sems.at[index, group]
                )

    def w_copy(half, away, slot):
        group = lax.rem(position + away, size)
        at = jnp.bitwise_xor(core, half)
        if joined:
            span = pl.ds(pl.multiple_of(at * width, 128), width)
            target = w_held.at[0, group, :, span]
        else:
            target = w_held.at[at, group]
        return pltpu.make_async_copy(weights[half * count + slot], target, w_sems.at[half, away])

    for copy in a_copies():
        copy.start()
    for away in range(size):
        for half in range(2):
            if away == 0:
                w_copy(half, 0, 0).start()
                continue

            @pl.when(position + away < size)
            def _(half=half, away=away):
                w_copy(half, away, size - 1 + away).start()

            @pl.when(position + away >= size)
            def _(half=half, away=away):
                w_copy(half, away, size - away).start()

    for copy in a_copies():
        copy.wait()
    for away in range(size):
        group = lax.rem(position + away, size)
        for half in range(2):
            w_copy(half, away, 0).wait()
        for half in range(halves):
            part = jnp.dot(a_held[group], w_held[half, group], preferred_element_type=jnp.float32)
            part = part.astype(jnp.bfloat16).astype(jnp.float32)
            if away == 0:
                total[half] = part
            else:
                total[half] += part
    for half in range(halves):
        span = slice(half * span_width, (half + 1) * span_width)
        reached = jnp.zeros((tokens, span_width), jnp.float32)
        for step in range(steps):
            told = heard[step, tokens : tokens + 16, span].astype(jnp.float32)
            gate = told[0:1] + told[1:2] + told[2:3]
            step_width = told[3:4] + told[4:5] + told[5:6]
            branch = total[half, step * tokens : (step + 1) * tokens] * gate
            out[step, 0, :, span] = branch.astype(jnp.bfloat16)
            reached += branch * step_width
            out[step, 1, :, span] = reached.astype(jnp.bfloat16)
            reached += heard[step, :tokens, span].astype(jnp.float32)


def project_out(place, heard, gathered, weights):
    size = lax.axis_size("head")
    steps = len(gathered)
    _, tokens, inner = gathered[0][0].shape
    width = weights[0][0].shape[1]
    layout, pieces = [], []
    for offset, held in enumerate(gathered):
        start = 0
        for piece in held:
            layout.append((offset, start, piece.shape[0]))
            pieces.append(piece)
            start += piece.shape[0]
    rows = steps * tokens
    halves = 1 if width % 128 == 0 else 2
    operands = pieces + [w for half in weights for w in half]
    return pl.pallas_call(
        functools.partial(out_kernel, size, tuple(layout)),
        in_specs=[SMEM] + [ANY] * len(operands) + [VMEM],
        out_specs=VMEM,
        out_shape=jax.ShapeDtypeStruct((steps, 2, tokens, 2 * width), jnp.bfloat16),
        scratch_shapes=[
            pltpu.VMEM((size, rows, inner), jnp.bfloat16),
            pltpu.VMEM((halves, size, inner, 2 * width // halves), jnp.bfloat16),
            pltpu.VMEM((halves, rows, 2 * width // halves), jnp.float32),
            pltpu.SemaphoreType.DMA((len(layout), size)),
            pltpu.SemaphoreType.DMA((2, size)),
        ],
        compiler_params=params(),
        cost_estimate=cost(4 * rows * size * inner * width, 2 * size * inner * (rows + 2 * width) + 8 * rows * width),
        name="project_out",
    )(place, *operands, heard)


def finish_kernel(base, arrived, reached, update):
    reached[...] = base[...] + arrived[0, 1].astype(jnp.float32)
    update[...] = arrived[0, 0]


def finish(base, arrived):
    steps, _, tokens, width = arrived.shape
    by_columns = pl.BlockSpec((tokens, width), lambda i: (0, i))
    return pl.pallas_call(
        finish_kernel,
        grid=(steps,),
        in_specs=[by_columns, pl.BlockSpec((1, 2, tokens, width), lambda i: (i, 0, 0, 0))],
        out_specs=[by_columns, by_columns],
        out_shape=[jax.ShapeDtypeStruct(base.shape, jnp.float32), jax.ShapeDtypeStruct(base.shape, jnp.bfloat16)],
        compiler_params=params(),
        cost_estimate=cost(base.size, 14 * base.size),
        name="finish",
    )(base, arrived)


def body(states, timesteps, lengths, modulation, w_query, w_key, w_value, w_out, q_gain, k_gain):
    steps, size = lax.axis_size("step"), lax.axis_size("head")
    step, core, position = (lax.axis_index(axis) for axis in ("step", "fsdp", "head"))
    current = states[0, 0]
    shift = (position >= size // 2).astype(jnp.int32)
    place = jnp.stack([step, core, position, lengths[0], shift]).astype(jnp.int32)

    w_both = jnp.concatenate([w_query, w_key], axis=1)
    mine, other = modulate(place, after(current, w_both), modulation, steps)
    tokens = jnp.stack([mine, swap(other, "fsdp", 1)])
    below, above = [tokens], [tokens]

    def hop(*awaited):
        count = len(below)
        arrived = (below[-1], above[-1])
        up, down = after(arrived, *awaited) if awaited else arrived
        below.append(lax.ppermute(up, "head", [(i, i + 1) for i in range(count - 1, size - 1)]))
        above.append(lax.ppermute(down, "head", [(i, i - 1) for i in range(1, size - count + 1)]))
        return arrived

    hop()
    if steps == 4 and size > 3 and w_value.shape[1] % 256 == 0:
        both_shards, last_round, finished = in_rounds(w_both, w_value, hop)
    else:
        both = forwarded(w_both, direct(w_both))
        both_shards = placed(both)
        last_round = tuple(both[-1])

        def finished(*awaited):
            return placed(forwarded(w_value, direct(after(w_value, *awaited))))

    while len(below) < size:
        hop()
    line = below, above
    early = tuple(held[: size - 1] + [held[0]] for held in line)
    step_width = (timesteps[0, 1] - timesteps[0, 0]).astype(jnp.float32) / 1000.0
    told = tell(place, step_width[None], current, modulation, steps)
    partner_below, partner_above = [swap(after(w_out, below[1], above[1]), "fsdp", 1)], []
    first_here, first_there = project(after(place, told, *partner_below), early, both_shards, "first", "first")
    ended = (below[-1], above[-1]) + last_round
    first_there = after(first_there, *ended)
    v_shards = finished(*ended, first_here)
    v_last = (v_shards[-1][0], v_shards[-2][0])
    parts = [first_here, swap(first_there, "fsdp", 1)]
    last_here, last_there = project(place, line, both_shards, "last", "last")
    parts += [last_here, swap(after(last_there, *v_last), "fsdp", 1)]
    v_here, v_there = project(after(place, last_here), line, v_shards, "all", "value")
    v_parts = [v_here, swap(v_there, "fsdp", 1)]
    heard = lax.all_to_all(after(told, *v_last), "step", 0, 0)

    below, above = [w_out], [w_out]
    for count in range(1, size):
        up, down = below[-1], above[-1]
        if count == 1:
            up, down = after((up, down), *ended, first_here)
        if count == 2:
            up, down = after((up, down), squares)
        if count == size - 1:
            up, down = after((up, down), quarter)
        below.append(lax.ppermute(up, "head", [(i, i + 1) for i in range(count - 1, size - 1)]))
        above.append(lax.ppermute(down, "head", [(i, i - 1) for i in range(1, size - count + 1)]))
        partner_below.append(swap(below[-1], "fsdp", 1))
        partner_above.append(swap(above[-1], "fsdp", 1))
        if count == 1:
            own_squares = norms(after(place, below[-1], above[-1], v_here, heard), parts, size)
            squares = lax.all_to_all(own_squares, "head", 0, 0)
            ready = after(squares, *partner_below, *partner_above)
            probs = probabilities(place, ready, parts, q_gain, k_gain)
        if count == size - 2:
            attended = after(attend(place, probs, v_parts, size), below[-1], above[-1])
            quarter = after(lax.all_to_all(attended, "head", 0, 0), partner_below[-1], partner_above[-1])

    gathered = forwarded(quarter, direct(quarter))

    raw = [w_out] + below[1:] + above[1:]
    out_weights = (raw, partner_below + partner_above)
    carried = step_width * current + jnp.where(step == 0, current, jnp.zeros_like(current))

    sent = project_out(place, heard, gathered, out_weights)
    arrived = lax.all_to_all(sent, "step", 0, 0)
    reached, update = finish(carried, arrived)
    return reached[None, None], update[None, None]


def solution(mesh):
    in_specs = (
        P("step", "fsdp", "head", None),
        P("step", None),
        P("fsdp"),
        P("step", None, None),
        P(("step", "fsdp"), "head"),
        P(("step", "fsdp"), "head"),
        P(("step", "fsdp"), "head"),
        P("head", ("step", "fsdp")),
        P("head"),
        P("head"),
    )
    out_specs = (P("step", "fsdp", "head", None), P("step", "fsdp", "head", None))
    return jax.shard_map(body, mesh=mesh, in_specs=in_specs, out_specs=out_specs, check_vma=False)
```

```python
import functools
import math

import jax
import jax.numpy as jnp
from jax import lax
from jax.experimental import pallas as pl
from jax.experimental.pallas import tpu as pltpu
from jax.sharding import PartitionSpec as P

HD = 128
MIB = 1 << 20
SMEM = pl.BlockSpec(memory_space=pltpu.SMEM)
VMEM = pl.BlockSpec(memory_space=pltpu.VMEM)
ANY = pl.BlockSpec(memory_space=pl.ANY)


def swap(x, axis, offset):
    return lax.ppermute(x, axis, [(i, i ^ offset) for i in range(lax.axis_size(axis))])


def bits_of(axis):
    return [1 << bit for bit in range(lax.axis_size(axis).bit_length() - 1)]


def direct(x):
    return {bit: [swap(x, "step", bit)] for bit in bits_of("step")}


def forwarded(x, near, *awaited):
    held = {0: [x], **near}
    half = x.shape[0] // 2
    for offset in range(1, lax.axis_size("step")):
        low, high = offset & -offset, 1 << (offset.bit_length() - 1)
        if offset in held:
            continue
        top, bottom = held[offset ^ low], held[offset ^ high]
        top = top[0][:half] if len(top) == 1 else top[0]
        bottom = bottom[0][half:] if len(bottom) == 1 else bottom[1]
        if awaited:
            top, bottom = after((top, bottom), *awaited)
        held[offset] = [swap(top, "step", low), swap(bottom, "step", high)]
    return [held[offset] for offset in range(lax.axis_size("step"))]


def placed(held, column=0):
    found = []
    for offset, pieces in enumerate(held):
        row = 0
        for piece in pieces:
            found.append((piece, offset, row, 0, column, piece.shape[1]))
            row += piece.shape[0]
    return found


def in_rounds(w_both, w_value, hop):
    width = w_value.shape[1]
    a1, a2 = swap(w_both, "step", 1), swap(w_both, "step", 2)
    e1, e2 = after((a1, a2), *hop())
    b1, b2 = swap(e2[:, :width], "step", 1), swap(e1[:, width:], "step", 2)
    v1, v2 = after((w_value, w_value), b1, b2, *hop(b1, b2))
    c1, c2 = swap(v1, "step", 1), swap(v2, "step", 2)
    both = [
        (w_both, 0, 0, 0, 0, 2 * width),
        (a1, 1, 0, 0, 0, 2 * width),
        (a2, 2, 0, 0, 0, 2 * width),
        (b1, 3, 0, 0, 0, width),
        (b2, 3, 0, 0, width, width),
    ]

    def finished(*awaited):
        f1, f2 = after((c1, c2), *awaited)
        d1, d2 = swap(f2[:, : width // 2], "step", 1), swap(f1[:, width // 2 :], "step", 2)
        whole = [(w_value, 0, 0, 0, 0, width), (c1, 1, 0, 0, 0, width), (c2, 2, 0, 0, 0, width)]
        return whole + [(d1, 3, 0, 0, 0, width // 2), (d2, 3, 0, 0, width // 2, width // 2)]

    return both, (c1, c2), finished


def after(x, *others):
    return lax.optimization_barrier((x,) + others)[0]


def params(mib=56):
    return pltpu.CompilerParams(vmem_limit_bytes=mib * MIB)


def cost(flops, moved, raised=0):
    return pl.CostEstimate(flops=int(flops) // 4, bytes_accessed=int(moved) // 4, transcendentals=int(raised) // 4)


def modulate_kernel(steps, place, states, rows, mine, other):
    current = states[...]
    centre = jnp.mean(current, axis=-1, keepdims=True)
    centred = current - centre
    spread_of = jnp.mean(centred * centred, axis=-1, keepdims=True)
    shift, scale = rows[0, 0:1, :], rows[0, 1:2, :]
    modulated = (centred * lax.rsqrt(spread_of + 1e-06) * (1.0 + scale) + shift).astype(jnp.bfloat16)
    core = place[1]
    for block in range(2 * steps):
        width = modulated.shape[1] // (2 * steps)
        piece = modulated[:, block * width : (block + 1) * width]
        at = slice(block // 2 * width, (block // 2 + 1) * width)

        @pl.when(core == block % 2)
        def _(piece=piece, at=at):
            mine[:, at] = piece

        @pl.when(core != block % 2)
        def _(piece=piece, at=at):
            other[:, at] = piece


def modulate(place, states, rows, steps):
    tokens, width = states.shape
    tile = 32
    out = jax.ShapeDtypeStruct((tokens, width // 2), jnp.bfloat16)
    spec = pl.BlockSpec((tile, width // 2), lambda i: (i, 0))
    return pl.pallas_call(
        functools.partial(modulate_kernel, steps),
        grid=(tokens // tile,),
        in_specs=[SMEM, pl.BlockSpec((tile, width), lambda i: (i, 0)), pl.BlockSpec(rows.shape, lambda i: (0, 0, 0))],
        out_specs=[spec, spec],
        out_shape=[out, out],
        compiler_params=params(),
        cost_estimate=cost(10 * tokens * width, 6 * tokens * width),
        name="modulate",
    )(place, states, rows)


def terms(x):
    high = x.astype(jnp.bfloat16).astype(jnp.float32)
    middle = (x - high).astype(jnp.bfloat16).astype(jnp.float32)
    return [high, middle, x - high - middle]


def tell_kernel(place, step_width, states, rows, out):
    current = states[...]
    tokens, columns = current.shape
    width = step_width[0]
    anchor = jnp.where(place[0] == 0, 1.0, 0.0)
    out[0, :tokens] = (width * current + anchor * current).astype(jnp.bfloat16)
    told = terms(rows[0, 2:3, :]) + terms(jnp.full((1, columns), width, jnp.float32))
    told.append(jnp.zeros((10, columns), jnp.float32))
    out[0, tokens:] = jnp.concatenate(told).astype(jnp.bfloat16)


def tell(place, step_width, states, rows, steps):
    tokens, width = states.shape
    columns = width // steps
    return pl.pallas_call(
        tell_kernel,
        grid=(steps,),
        in_specs=[
            SMEM,
            SMEM,
            pl.BlockSpec((tokens, columns), lambda i: (0, i)),
            pl.BlockSpec((1, rows.shape[1], columns), lambda i: (0, 0, i)),
        ],
        out_specs=pl.BlockSpec((1, tokens + 16, columns), lambda i: (i, 0, 0)),
        out_shape=jax.ShapeDtypeStruct((steps, tokens + 16, columns), jnp.bfloat16),
        compiler_params=params(),
        cost_estimate=cost(4 * tokens * width, 6 * tokens * width),
        name="tell",
    )(place, step_width, states, rows)


def project_kernel(size, parts, shard, layout, place, *refs):
    count = 2 * size - 1
    own, below, above = refs[0], refs[1:size], refs[size:count]
    weights = refs[count : count + len(layout)]
    here, there, x_held, w_held, x_sems, w_sems = refs[count + len(layout) :]
    tokens, depth = own.shape[1:]
    step_at, position, shift = place[0], place[2], place[4]
    early = size - 1
    blocks = {"first": range(early), "last": range(early, size), "all": range(size)}[parts]

    def x_copy(ref, clip, block):
        row = (clip * len(blocks) + block - blocks[0]) * tokens
        return pltpu.make_async_copy(
            ref.at[clip], x_held.at[pl.ds(pl.multiple_of(row, tokens), tokens)], x_sems.at[clip, block]
        )

    def w_copies():
        for index, (ref, (offset, row, source, target, count)) in enumerate(zip(weights, layout)):
            at = jnp.bitwise_xor(step_at, offset) * shard + row
            rows = ref.shape[0]
            part = w_held.at[pl.ds(pl.multiple_of(at, rows), rows), pl.ds(target, count)]
            yield pltpu.make_async_copy(ref.at[:, pl.ds(source, count)], part, w_sems.at[index])

    for copy in w_copies():
        copy.start()
    for clip in range(2):
        for away in range(size):
            for sign, held in ((1, above), (-1, below)):
                if away == 0 and sign < 0:
                    continue
                source = own if away == 0 else held[away - 1]
                block_at = position + sign * away
                block = lax.rem(block_at - shift + size, size)
                inside = jnp.logical_and(block_at >= 0, block_at < size)
                inside = jnp.logical_and(inside, jnp.logical_and(block >= blocks[0], block <= blocks[-1]))

                @pl.when(inside)
                def _(source=source, block=block, clip=clip):
                    x_copy(source, clip, block).start()

    for copy in w_copies():
        copy.wait()
    for clip in range(2):
        for block in blocks:
            x_copy(own, clip, block).wait()
    rows, columns = here.shape
    width = columns if columns % 512 else columns // 2
    for start in range(0, columns, width):
        span = slice(start, start + width)
        product = jnp.dot(x_held[...], w_held[:, span], preferred_element_type=jnp.float32)
        here[:, span] = product[:rows]
        there[:, span] = product[rows:]


def project(place, line, shards, parts, name):
    size = lax.axis_size("head")
    below, above = line
    operands = [below[0]] + below[1:] + above[1:]
    _, tokens, depth = operands[0].shape
    weights = [piece[0] for piece in shards]
    layout = [piece[1:] for piece in shards]
    shard, columns = weights[0].shape
    rows = {"first": size - 1, "last": 1, "all": size}[parts] * tokens
    out = jax.ShapeDtypeStruct((rows, columns), jnp.float32)
    moved = 2 * depth * (2 * rows + columns) + 8 * rows * columns
    return pl.pallas_call(
        functools.partial(project_kernel, size, parts, shard, tuple(layout)),
        in_specs=[SMEM] + [ANY] * (len(operands) + len(weights)),
        out_specs=[VMEM, VMEM],
        out_shape=[out, out],
        scratch_shapes=[
            pltpu.VMEM((2 * rows, depth), jnp.bfloat16),
            pltpu.VMEM((depth, columns), jnp.bfloat16),
            pltpu.SemaphoreType.DMA((2, size)),
            pltpu.SemaphoreType.DMA((len(layout),)),
        ],
        compiler_params=params(),
        cost_estimate=cost(4 * rows * depth * columns, moved),
        name=name,
    )(place, *operands, *weights)


def norms_kernel(place, first_a, first_b, last_a, last_b, out):
    width = first_a.shape[1] // 2
    rows = []
    for which in range(2):
        found = []
        for one, other in ((first_a, first_b), (last_a, last_b)):
            lanes = None
            for start in range(which * width, (which + 1) * width, HD):
                total = one[:, start : start + HD] + other[:, start : start + HD]
                lanes = total * total if lanes is None else lanes + total * total
            found.append(jnp.sum(lanes.T, axis=0, keepdims=True))
        straight = jnp.concatenate(found, axis=1)
        wrapped = jnp.concatenate(found[::-1], axis=1)
        rows.append(jnp.where(place[4] == 0, straight, wrapped))
    both = jnp.concatenate(rows, axis=0)
    for peer in range(out.shape[0]):
        out[peer] = both


def norms(place, parts, size):
    rows = parts[0].shape[0] + parts[2].shape[0]
    return pl.pallas_call(
        norms_kernel,
        in_specs=[SMEM] + [VMEM] * 4,
        out_specs=VMEM,
        out_shape=jax.ShapeDtypeStruct((size, 2, rows), jnp.float32),
        compiler_params=params(),
        cost_estimate=cost(4 * rows * parts[0].shape[1], 8 * rows * parts[0].shape[1]),
        name="norms",
    )(place, *parts)


def probs_kernel(tokens, full_width, place, squares, *refs):
    parts, (q_gain, k_gain, out, scales) = refs[:8], refs[8:]
    rows = scales.shape[1]

    @pl.when(pl.program_id(0) == 0)
    def _():
        total = squares[0]
        for peer in range(1, squares.shape[0]):
            total = total + squares[peer]
        turned = jnp.concatenate([total[:, tokens:], total[:, :tokens]], axis=1)
        total = jnp.where(place[4] == 0, total, turned)
        scale = lax.rsqrt(total / full_width + 1e-06)
        for which in range(2):
            scales[which] = jnp.broadcast_to(scale[which : which + 1], (HD, rows)).T

    column = lax.broadcasted_iota(jnp.int32, (1, rows), 1) + place[4] * tokens
    valid = jnp.where(column >= rows, column - rows, column) < place[3]
    for head in range(out.shape[0]):
        span = slice(head * HD, (head + 1) * HD)

        def normed(at, gain, which):
            joined = [parts[at + i][:, span] + parts[at + i + 1][:, span] for i in (0, 2)]
            return (jnp.concatenate(joined) * scales[which] * gain[:, span]).astype(jnp.bfloat16)

        queries, keys = normed(0, q_gain, 0), normed(4, k_gain, 1)
        scores = lax.dot_general(queries, keys, (((1,), (1,)), ((), ())), preferred_element_type=jnp.float32)
        scores = jnp.where(valid, scores * (1.0 / math.sqrt(HD)), -jnp.inf)
        raised = jnp.exp(scores - jnp.max(scores, axis=-1, keepdims=True))
        out[head] = (raised * (1.0 / jnp.sum(raised, axis=-1, keepdims=True))).astype(jnp.bfloat16)


def at_once(heads):
    return 2 if heads % 2 == 0 else 1


def probabilities(place, squares, parts, q_gain, k_gain):
    columns = parts[0].shape[1] // 2
    rows = parts[0].shape[0] + parts[2].shape[0]
    heads = columns // HD
    group = at_once(heads)
    q_blocks = [pl.BlockSpec((part.shape[0], group * HD), lambda i: (0, i)) for part in parts]
    k_blocks = [pl.BlockSpec((part.shape[0], group * HD), lambda i: (0, i + heads // group)) for part in parts]
    gain = pl.BlockSpec((1, group * HD), lambda i: (0, i))
    return pl.pallas_call(
        functools.partial(probs_kernel, parts[2].shape[0], float(columns * squares.shape[0])),
        grid=(heads // group,),
        in_specs=[SMEM, pl.BlockSpec(squares.shape, lambda i: (0, 0, 0))] + q_blocks + k_blocks + [gain] * 2,
        out_specs=pl.BlockSpec((group, rows, rows), lambda i: (i, 0, 0)),
        out_shape=jax.ShapeDtypeStruct((heads, rows, rows), jnp.bfloat16),
        scratch_shapes=[pltpu.VMEM((2, rows, HD), jnp.float32)],
        compiler_params=params(),
        cost_estimate=cost(2 * heads * rows * rows * HD, 16 * rows * columns + 2 * heads * rows * rows, heads * rows * rows),
        name="probs",
    )(place, squares, *parts, *parts, q_gain[None], k_gain[None])


def attend_kernel(place, probs, v_a, v_b, out, held):
    size, tokens, _ = out.shape
    for head in range(probs.shape[0]):
        span = slice(head * HD, (head + 1) * HD)
        values = (v_a[:, span] + v_b[:, span]).astype(jnp.bfloat16)
        held[:, span] = jnp.dot(probs[head], values, preferred_element_type=jnp.float32)
    for block in range(size):
        at = lax.rem(block - place[4] + size, size) * tokens
        out[block] = held[pl.ds(pl.multiple_of(at, tokens), tokens)].astype(jnp.bfloat16)


def attend(place, probs, v_parts, size):
    heads, rows, _ = probs.shape
    tokens = rows // size
    group = at_once(heads)
    by_head = pl.BlockSpec((rows, group * HD), lambda i: (0, i))
    return pl.pallas_call(
        attend_kernel,
        grid=(heads // group,),
        in_specs=[SMEM, pl.BlockSpec((group, rows, rows), lambda i: (i, 0, 0)), by_head, by_head],
        out_specs=pl.BlockSpec((size, tokens, group * HD), lambda i: (0, 0, i)),
        out_shape=jax.ShapeDtypeStruct((size, tokens, heads * HD), jnp.bfloat16),
        scratch_shapes=[pltpu.VMEM((rows, group * HD), jnp.float32)],
        compiler_params=params(),
        cost_estimate=cost(2 * heads * rows * rows * HD, 2 * heads * rows * rows + 10 * rows * heads * HD),
        name="attend",
    )(place, probs, *v_parts)


def out_kernel(size, layout, first, place, *refs):
    count = 2 * size - 1
    pieces, weights = refs[: len(layout)], refs[len(layout) : len(layout) + 2 * count]
    heard, out, a_held, w_held, total, a_sems, w_sems = refs[len(layout) + 2 * count :]
    steps, _, tokens, columns = out.shape
    width = columns // 2
    halves, _, _, span_width = w_held.shape
    joined = halves == 1
    step_at, core, position = place[0], place[1], place[2]

    def a_copies():
        for index, (offset, start, groups) in enumerate(layout):
            row = pl.multiple_of(jnp.bitwise_xor(step_at, offset) * tokens, tokens)
            for group in range(groups):
                yield pltpu.make_async_copy(
                    pieces[index].at[group, pl.ds(first, tokens)],
                    a_held.at[start + group, pl.ds(row, tokens)],
                    a_sems.at[index, group],
                )

    def w_copy(half, away, slot):
        group = lax.rem(position + away, size)
        at = jnp.bitwise_xor(core, half)
        if joined:
            span = pl.ds(pl.multiple_of(at * width, 128), width)
            target = w_held.at[0, group, :, span]
        else:
            target = w_held.at[at, group]
        return pltpu.make_async_copy(weights[half * count + slot], target, w_sems.at[half, away])

    for copy in a_copies():
        copy.start()
    for away in range(size):
        for half in range(2):
            if away == 0:
                w_copy(half, 0, 0).start()
                continue

            @pl.when(position + away < size)
            def _(half=half, away=away):
                w_copy(half, away, size - 1 + away).start()

            @pl.when(position + away >= size)
            def _(half=half, away=away):
                w_copy(half, away, size - away).start()

    for copy in a_copies():
        copy.wait()
    for away in range(size):
        group = lax.rem(position + away, size)
        for half in range(2):
            w_copy(half, away, 0).wait()
        for half in range(halves):
            part = jnp.dot(a_held[group], w_held[half, group], preferred_element_type=jnp.float32)
            part = part.astype(jnp.bfloat16).astype(jnp.float32)
            if away == 0:
                total[half] = part
            else:
                total[half] += part
    for half in range(halves):
        span = slice(half * span_width, (half + 1) * span_width)
        reached = jnp.zeros((tokens, span_width), jnp.float32)
        for step in range(steps):
            told = heard[step, -16:, span].astype(jnp.float32)
            gate = told[0:1] + told[1:2] + told[2:3]
            step_width = told[3:4] + told[4:5] + told[5:6]
            branch = total[half, step * tokens : (step + 1) * tokens] * gate
            out[step, 0, :, span] = branch.astype(jnp.bfloat16)
            reached += branch * step_width
            out[step, 1, :, span] = reached.astype(jnp.bfloat16)
            reached += heard[step, first : first + tokens, span].astype(jnp.float32)


def project_out(place, heard, gathered, weights, part, parts):
    size = lax.axis_size("head")
    steps = len(gathered)
    _, tokens, inner = gathered[0][0].shape
    tokens = tokens // parts
    width = weights[0][0].shape[1]
    layout, pieces = [], []
    for offset, held in enumerate(gathered):
        start = 0
        for piece in held:
            layout.append((offset, start, piece.shape[0]))
            pieces.append(piece)
            start += piece.shape[0]
    rows = steps * tokens
    halves = 1 if width % 128 == 0 else 2
    operands = pieces + [w for half in weights for w in half]
    return pl.pallas_call(
        functools.partial(out_kernel, size, tuple(layout), part * tokens),
        in_specs=[SMEM] + [ANY] * len(operands) + [VMEM],
        out_specs=VMEM,
        out_shape=jax.ShapeDtypeStruct((steps, 2, tokens, 2 * width), jnp.bfloat16),
        scratch_shapes=[
            pltpu.VMEM((size, rows, inner), jnp.bfloat16),
            pltpu.VMEM((halves, size, inner, 2 * width // halves), jnp.bfloat16),
            pltpu.VMEM((halves, rows, 2 * width // halves), jnp.float32),
            pltpu.SemaphoreType.DMA((len(layout), size)),
            pltpu.SemaphoreType.DMA((2, size)),
        ],
        compiler_params=params(),
        cost_estimate=cost(4 * rows * size * inner * width, 2 * size * inner * (rows + 2 * width) + 8 * rows * width),
        name="project_out",
    )(place, *operands, heard)


def finish_kernel(base, arrived, *refs):
    reached, update = refs[-2:]
    reached[...] = base[...] + arrived[0, 1].astype(jnp.float32)
    update[...] = arrived[0, 0]


def finish(base, arrived, part, started):
    steps, _, tokens, width = arrived.shape
    by_columns = pl.BlockSpec((tokens, width), lambda i: (part, i))
    return pl.pallas_call(
        finish_kernel,
        grid=(steps,),
        in_specs=[by_columns, pl.BlockSpec((1, 2, tokens, width), lambda i: (i, 0, 0, 0))] + [ANY] * len(started),
        out_specs=[by_columns, by_columns],
        out_shape=[jax.ShapeDtypeStruct(base.shape, jnp.float32), jax.ShapeDtypeStruct(base.shape, jnp.bfloat16)],
        input_output_aliases={2 + i: i for i in range(len(started))},
        compiler_params=params(),
        cost_estimate=cost(arrived.size // 2, 7 * arrived.size),
        name="finish",
    )(base, arrived, *started)


def body(states, timesteps, lengths, modulation, w_query, w_key, w_value, w_out, q_gain, k_gain):
    steps, size = lax.axis_size("step"), lax.axis_size("head")
    step, core, position = (lax.axis_index(axis) for axis in ("step", "fsdp", "head"))
    current = states[0, 0]
    shift = (position >= size // 2).astype(jnp.int32)
    place = jnp.stack([step, core, position, lengths[0], shift]).astype(jnp.int32)

    w_both = jnp.concatenate([w_query, w_key], axis=1)
    mine, other = modulate(place, current, modulation, steps)
    tokens = jnp.stack([mine, swap(other, "fsdp", 1)])
    below, above = [tokens], [tokens]

    def hop(*awaited):
        count = len(below)
        arrived = (below[-1], above[-1])
        up, down = after(arrived, *awaited) if awaited else arrived
        below.append(lax.ppermute(up, "head", [(i, i + 1) for i in range(count - 1, size - 1)]))
        above.append(lax.ppermute(down, "head", [(i, i - 1) for i in range(1, size - count + 1)]))
        return arrived

    hop()
    if steps == 4 and size > 3 and w_value.shape[1] % 256 == 0:
        both_shards, last_round, finished = in_rounds(w_both, w_value, hop)
    else:
        both = forwarded(w_both, direct(w_both))
        both_shards = placed(both)
        last_round = tuple(both[-1])

        def finished(*awaited):
            return placed(forwarded(w_value, direct(after(w_value, *awaited))))

    while len(below) < size:
        hop()
    line = below, above
    early = tuple(held[: size - 1] + [held[0]] for held in line)
    step_width = (timesteps[0, 1] - timesteps[0, 0]).astype(jnp.float32) / 1000.0
    told = tell(place, step_width[None], current, modulation, steps)
    partner_below, partner_above = [swap(after(w_out, below[1], above[1]), "fsdp", 1)], []
    first_here, first_there = project(after(place, told, *partner_below), early, both_shards, "first", "first")
    ended = (below[-1], above[-1]) + last_round
    first_there = after(first_there, *ended)
    v_shards = finished(*ended, first_here)
    v_last = (v_shards[-1][0], v_shards[-2][0])
    parts = [first_here, swap(first_there, "fsdp", 1)]
    last_here, last_there = project(place, line, both_shards, "last", "last")
    parts += [last_here, swap(after(last_there, *v_last), "fsdp", 1)]
    v_here, v_there = project(after(place, last_here), line, v_shards, "all", "value")
    v_parts = [v_here, swap(v_there, "fsdp", 1)]
    heard = lax.all_to_all(after(told, last_here, *v_last), "step", 0, 0)

    below, above = [w_out], [w_out]
    for count in range(1, size):
        up, down = below[-1], above[-1]
        if count == 1:
            up, down = after((up, down), *ended, first_here)
        if count == 2:
            up, down = after((up, down), v_here)
        if count == size - 1:
            up, down = after((up, down), quarter)
        below.append(lax.ppermute(up, "head", [(i, i + 1) for i in range(count - 1, size - 1)]))
        above.append(lax.ppermute(down, "head", [(i, i - 1) for i in range(1, size - count + 1)]))
        partner_below.append(swap(below[-1], "fsdp", 1))
        partner_above.append(swap(above[-1], "fsdp", 1))
        if count == 1:
            own_squares = norms(after(place, below[-1], above[-1], v_here, heard), parts, size)
            squares = lax.all_to_all(own_squares, "head", 0, 0)
        if count == size - 2:
            ready = after(squares, *partner_below[:-1], *partner_above[:-1], below[-1], above[-1])
            probs = probabilities(place, ready, parts, q_gain, k_gain)
            attended = attend(place, probs, v_parts, size)
            quarter = after(lax.all_to_all(attended, "head", 0, 0), partner_below[-1], partner_above[-1])

    gathered = forwarded(quarter, direct(quarter))

    raw = [w_out] + below[1:] + above[1:]
    out_weights = (raw, partner_below + partner_above)
    carried = step_width * current + jnp.where(step == 0, current, jnp.zeros_like(current))

    outputs, parts_of = (), 2
    sent = [project_out(place, heard, gathered, out_weights, part, parts_of) for part in range(parts_of)]
    for part in range(parts_of):
        outputs = finish(carried, lax.all_to_all(sent[part], "step", 0, 0), part, outputs)
    reached, update = outputs
    return reached[None, None], update[None, None]


def solution(mesh):
    in_specs = (
        P("step", "fsdp", "head", None),
        P("step", None),
        P("fsdp"),
        P("step", None, None),
        P(("step", "fsdp"), "head"),
        P(("step", "fsdp"), "head"),
        P(("step", "fsdp"), "head"),
        P("head", ("step", "fsdp")),
        P("head"),
        P("head"),
    )
    out_specs = (P("step", "fsdp", "head", None), P("step", "fsdp", "head", None))
    return jax.shard_map(body, mesh=mesh, in_specs=in_specs, out_specs=out_specs, check_vma=False)
```

```python
import functools
import math

import jax
import jax.numpy as jnp
from jax import lax
from jax.experimental import pallas as pl
from jax.experimental.pallas import tpu as pltpu
from jax.sharding import PartitionSpec as P

HD = 128
MIB = 1 << 20
SMEM = pl.BlockSpec(memory_space=pltpu.SMEM)
VMEM = pl.BlockSpec(memory_space=pltpu.VMEM)
ANY = pl.BlockSpec(memory_space=pl.ANY)


def swap(x, axis, offset):
    return lax.ppermute(x, axis, [(i, i ^ offset) for i in range(lax.axis_size(axis))])


def bits_of(axis):
    return [1 << bit for bit in range(lax.axis_size(axis).bit_length() - 1)]


def direct(x):
    return {bit: [swap(x, "step", bit)] for bit in bits_of("step")}


def forwarded(x, near, *awaited):
    held = {0: [x], **near}
    half = x.shape[0] // 2
    for offset in range(1, lax.axis_size("step")):
        low, high = offset & -offset, 1 << (offset.bit_length() - 1)
        if offset in held:
            continue
        top, bottom = held[offset ^ low], held[offset ^ high]
        top = top[0][:half] if len(top) == 1 else top[0]
        bottom = bottom[0][half:] if len(bottom) == 1 else bottom[1]
        if awaited:
            top, bottom = after((top, bottom), *awaited)
        held[offset] = [swap(top, "step", low), swap(bottom, "step", high)]
    return [held[offset] for offset in range(lax.axis_size("step"))]


def placed(held, column=0):
    found = []
    for offset, pieces in enumerate(held):
        row = 0
        for piece in pieces:
            found.append((piece, offset, row, 0, column, piece.shape[1]))
            row += piece.shape[0]
    return found


def in_rounds(w_both, w_value, hop):
    width = w_value.shape[1]
    a1, a2 = swap(w_both, "step", 1), swap(w_both, "step", 2)
    e1, e2 = after((a1, a2), *hop())
    b1, b2 = swap(e2[:, :width], "step", 1), swap(e1[:, width:], "step", 2)
    v1, v2 = after((w_value, w_value), b1, b2, *hop(b1, b2))
    c1, c2 = swap(v1, "step", 1), swap(v2, "step", 2)
    both = [
        (w_both, 0, 0, 0, 0, 2 * width),
        (a1, 1, 0, 0, 0, 2 * width),
        (a2, 2, 0, 0, 0, 2 * width),
        (b1, 3, 0, 0, 0, width),
        (b2, 3, 0, 0, width, width),
    ]

    def finished(*awaited):
        f1, f2 = after((c1, c2), *awaited)
        d1, d2 = swap(f2[:, : width // 2], "step", 1), swap(f1[:, width // 2 :], "step", 2)
        whole = [(w_value, 0, 0, 0, 0, width), (c1, 1, 0, 0, 0, width), (c2, 2, 0, 0, 0, width)]
        return whole + [(d1, 3, 0, 0, 0, width // 2), (d2, 3, 0, 0, width // 2, width // 2)]

    return both, (c1, c2), finished


def after(x, *others):
    return lax.optimization_barrier((x,) + others)[0]


def params(mib=56):
    return pltpu.CompilerParams(vmem_limit_bytes=mib * MIB)


def cost(flops, moved, raised=0):
    return pl.CostEstimate(flops=int(flops) // 4, bytes_accessed=int(moved) // 4, transcendentals=int(raised) // 4)


def modulate_kernel(steps, place, states, rows, mine, other):
    current = states[...]
    centre = jnp.mean(current, axis=-1, keepdims=True)
    centred = current - centre
    spread_of = jnp.mean(centred * centred, axis=-1, keepdims=True)
    shift, scale = rows[0, 0:1, :], rows[0, 1:2, :]
    modulated = (centred * lax.rsqrt(spread_of + 1e-06) * (1.0 + scale) + shift).astype(jnp.bfloat16)
    core = place[1]
    for block in range(2 * steps):
        width = modulated.shape[1] // (2 * steps)
        piece = modulated[:, block * width : (block + 1) * width]
        at = slice(block // 2 * width, (block // 2 + 1) * width)

        @pl.when(core == block % 2)
        def _(piece=piece, at=at):
            mine[:, at] = piece

        @pl.when(core != block % 2)
        def _(piece=piece, at=at):
            other[:, at] = piece


def modulate(place, states, rows, steps):
    tokens, width = states.shape
    tile = 32
    out = jax.ShapeDtypeStruct((tokens, width // 2), jnp.bfloat16)
    spec = pl.BlockSpec((tile, width // 2), lambda i: (i, 0))
    return pl.pallas_call(
        functools.partial(modulate_kernel, steps),
        grid=(tokens // tile,),
        in_specs=[SMEM, pl.BlockSpec((tile, width), lambda i: (i, 0)), pl.BlockSpec(rows.shape, lambda i: (0, 0, 0))],
        out_specs=[spec, spec],
        out_shape=[out, out],
        compiler_params=params(),
        cost_estimate=cost(10 * tokens * width, 6 * tokens * width),
        name="modulate",
    )(place, states, rows)


def terms(x):
    high = x.astype(jnp.bfloat16).astype(jnp.float32)
    middle = (x - high).astype(jnp.bfloat16).astype(jnp.float32)
    return [high, middle, x - high - middle]


def tell_kernel(place, step_width, states, rows, out):
    current = states[...]
    tokens, columns = current.shape
    width = step_width[0]
    anchor = jnp.where(place[0] == 0, 1.0, 0.0)
    out[0, :tokens] = (width * current + anchor * current).astype(jnp.bfloat16)
    told = terms(rows[0, 2:3, :]) + terms(jnp.full((1, columns), width, jnp.float32))
    told.append(jnp.zeros((10, columns), jnp.float32))
    out[0, tokens:] = jnp.concatenate(told).astype(jnp.bfloat16)


def tell(place, step_width, states, rows, steps):
    tokens, width = states.shape
    columns = width // steps
    return pl.pallas_call(
        tell_kernel,
        grid=(steps,),
        in_specs=[
            SMEM,
            SMEM,
            pl.BlockSpec((tokens, columns), lambda i: (0, i)),
            pl.BlockSpec((1, rows.shape[1], columns), lambda i: (0, 0, i)),
        ],
        out_specs=pl.BlockSpec((1, tokens + 16, columns), lambda i: (i, 0, 0)),
        out_shape=jax.ShapeDtypeStruct((steps, tokens + 16, columns), jnp.bfloat16),
        compiler_params=params(),
        cost_estimate=cost(4 * tokens * width, 6 * tokens * width),
        name="tell",
    )(place, step_width, states, rows)


def project_kernel(size, parts, shard, layout, place, *refs):
    count = 2 * size - 1
    own, below, above = refs[0], refs[1:size], refs[size:count]
    weights = refs[count : count + len(layout)]
    here, there, x_held, w_held, x_sems, w_sems = refs[count + len(layout) :]
    tokens, depth = own.shape[1:]
    step_at, position, shift = place[0], place[2], place[4]
    early = size - 1
    blocks = {"first": range(early), "last": range(early, size), "all": range(size)}[parts]

    def x_copy(ref, clip, block):
        row = (clip * len(blocks) + block - blocks[0]) * tokens
        return pltpu.make_async_copy(
            ref.at[clip], x_held.at[pl.ds(pl.multiple_of(row, tokens), tokens)], x_sems.at[clip, block]
        )

    def w_copies():
        for index, (ref, (offset, row, source, target, count)) in enumerate(zip(weights, layout)):
            at = jnp.bitwise_xor(step_at, offset) * shard + row
            rows = ref.shape[0]
            part = w_held.at[pl.ds(pl.multiple_of(at, rows), rows), pl.ds(target, count)]
            yield pltpu.make_async_copy(ref.at[:, pl.ds(source, count)], part, w_sems.at[index])

    for copy in w_copies():
        copy.start()
    for clip in range(2):
        for away in range(size):
            for sign, held in ((1, above), (-1, below)):
                if away == 0 and sign < 0:
                    continue
                source = own if away == 0 else held[away - 1]
                block_at = position + sign * away
                block = lax.rem(block_at - shift + size, size)
                inside = jnp.logical_and(block_at >= 0, block_at < size)
                inside = jnp.logical_and(inside, jnp.logical_and(block >= blocks[0], block <= blocks[-1]))

                @pl.when(inside)
                def _(source=source, block=block, clip=clip):
                    x_copy(source, clip, block).start()

    for copy in w_copies():
        copy.wait()
    for clip in range(2):
        for block in blocks:
            x_copy(own, clip, block).wait()
    rows, columns = here.shape
    width = columns if columns % 512 else columns // 2
    for start in range(0, columns, width):
        span = slice(start, start + width)
        product = jnp.dot(x_held[...], w_held[:, span], preferred_element_type=jnp.float32)
        here[:, span] = product[:rows]
        there[:, span] = product[rows:]


def project(place, line, shards, parts, name):
    size = lax.axis_size("head")
    below, above = line
    operands = [below[0]] + below[1:] + above[1:]
    _, tokens, depth = operands[0].shape
    weights = [piece[0] for piece in shards]
    layout = [piece[1:] for piece in shards]
    shard, columns = weights[0].shape
    rows = {"first": size - 1, "last": 1, "all": size}[parts] * tokens
    out = jax.ShapeDtypeStruct((rows, columns), jnp.float32)
    moved = 2 * depth * (2 * rows + columns) + 8 * rows * columns
    return pl.pallas_call(
        functools.partial(project_kernel, size, parts, shard, tuple(layout)),
        in_specs=[SMEM] + [ANY] * (len(operands) + len(weights)),
        out_specs=[VMEM, VMEM],
        out_shape=[out, out],
        scratch_shapes=[
            pltpu.VMEM((2 * rows, depth), jnp.bfloat16),
            pltpu.VMEM((depth, columns), jnp.bfloat16),
            pltpu.SemaphoreType.DMA((2, size)),
            pltpu.SemaphoreType.DMA((len(layout),)),
        ],
        compiler_params=params(),
        cost_estimate=cost(4 * rows * depth * columns, moved),
        name=name,
    )(place, *operands, *weights)


def norms_kernel(place, first_a, first_b, last_a, last_b, out):
    width = first_a.shape[1] // 2
    rows = []
    for which in range(2):
        found = []
        for one, other in ((first_a, first_b), (last_a, last_b)):
            lanes = None
            for start in range(which * width, (which + 1) * width, HD):
                total = one[:, start : start + HD] + other[:, start : start + HD]
                lanes = total * total if lanes is None else lanes + total * total
            found.append(jnp.sum(lanes.T, axis=0, keepdims=True))
        straight = jnp.concatenate(found, axis=1)
        wrapped = jnp.concatenate(found[::-1], axis=1)
        rows.append(jnp.where(place[4] == 0, straight, wrapped))
    both = jnp.concatenate(rows, axis=0)
    for peer in range(out.shape[0]):
        out[peer] = both


def norms(place, parts, size):
    rows = parts[0].shape[0] + parts[2].shape[0]
    return pl.pallas_call(
        norms_kernel,
        in_specs=[SMEM] + [VMEM] * 4,
        out_specs=VMEM,
        out_shape=jax.ShapeDtypeStruct((size, 2, rows), jnp.float32),
        compiler_params=params(),
        cost_estimate=cost(4 * rows * parts[0].shape[1], 8 * rows * parts[0].shape[1]),
        name="norms",
    )(place, *parts)


def probs_kernel(tokens, full_width, place, squares, *refs):
    parts, (q_gain, k_gain, out, scales) = refs[:8], refs[8:]
    rows = scales.shape[1]

    @pl.when(pl.program_id(0) == 0)
    def _():
        total = squares[0]
        for peer in range(1, squares.shape[0]):
            total = total + squares[peer]
        turned = jnp.concatenate([total[:, tokens:], total[:, :tokens]], axis=1)
        total = jnp.where(place[4] == 0, total, turned)
        scale = lax.rsqrt(total / full_width + 1e-06)
        for which in range(2):
            scales[which] = jnp.broadcast_to(scale[which : which + 1], (HD, rows)).T

    column = lax.broadcasted_iota(jnp.int32, (1, rows), 1) + place[4] * tokens
    valid = jnp.where(column >= rows, column - rows, column) < place[3]
    for head in range(out.shape[0]):
        span = slice(head * HD, (head + 1) * HD)

        def normed(at, gain, which):
            joined = [parts[at + i][:, span] + parts[at + i + 1][:, span] for i in (0, 2)]
            return (jnp.concatenate(joined) * scales[which] * gain[:, span]).astype(jnp.bfloat16)

        queries, keys = normed(0, q_gain, 0), normed(4, k_gain, 1)
        scores = lax.dot_general(queries, keys, (((1,), (1,)), ((), ())), preferred_element_type=jnp.float32)
        scores = jnp.where(valid, scores * (1.0 / math.sqrt(HD)), -jnp.inf)
        raised = jnp.exp(scores - jnp.max(scores, axis=-1, keepdims=True))
        out[head] = (raised * (1.0 / jnp.sum(raised, axis=-1, keepdims=True))).astype(jnp.bfloat16)


def at_once(heads):
    return 2 if heads % 2 == 0 else 1


def probabilities(place, squares, parts, q_gain, k_gain):
    columns = parts[0].shape[1] // 2
    rows = parts[0].shape[0] + parts[2].shape[0]
    heads = columns // HD
    group = at_once(heads)
    q_blocks = [pl.BlockSpec((part.shape[0], group * HD), lambda i: (0, i)) for part in parts]
    k_blocks = [pl.BlockSpec((part.shape[0], group * HD), lambda i: (0, i + heads // group)) for part in parts]
    gain = pl.BlockSpec((1, group * HD), lambda i: (0, i))
    return pl.pallas_call(
        functools.partial(probs_kernel, parts[2].shape[0], float(columns * squares.shape[0])),
        grid=(heads // group,),
        in_specs=[SMEM, pl.BlockSpec(squares.shape, lambda i: (0, 0, 0))] + q_blocks + k_blocks + [gain] * 2,
        out_specs=pl.BlockSpec((group, rows, rows), lambda i: (i, 0, 0)),
        out_shape=jax.ShapeDtypeStruct((heads, rows, rows), jnp.bfloat16),
        scratch_shapes=[pltpu.VMEM((2, rows, HD), jnp.float32)],
        compiler_params=params(),
        cost_estimate=cost(2 * heads * rows * rows * HD, 16 * rows * columns + 2 * heads * rows * rows, heads * rows * rows),
        name="probs",
    )(place, squares, *parts, *parts, q_gain[None], k_gain[None])


def attend_kernel(place, probs, v_a, v_b, out, held):
    size, tokens, _ = out.shape
    for head in range(probs.shape[0]):
        span = slice(head * HD, (head + 1) * HD)
        values = (v_a[:, span] + v_b[:, span]).astype(jnp.bfloat16)
        held[:, span] = jnp.dot(probs[head], values, preferred_element_type=jnp.float32)
    for block in range(size):
        at = lax.rem(block - place[4] + size, size) * tokens
        out[block] = held[pl.ds(pl.multiple_of(at, tokens), tokens)].astype(jnp.bfloat16)


def attend(place, probs, v_parts, size):
    heads, rows, _ = probs.shape
    tokens = rows // size
    group = at_once(heads)
    by_head = pl.BlockSpec((rows, group * HD), lambda i: (0, i))
    return pl.pallas_call(
        attend_kernel,
        grid=(heads // group,),
        in_specs=[SMEM, pl.BlockSpec((group, rows, rows), lambda i: (i, 0, 0)), by_head, by_head],
        out_specs=pl.BlockSpec((size, tokens, group * HD), lambda i: (0, 0, i)),
        out_shape=jax.ShapeDtypeStruct((size, tokens, heads * HD), jnp.bfloat16),
        scratch_shapes=[pltpu.VMEM((rows, group * HD), jnp.float32)],
        compiler_params=params(),
        cost_estimate=cost(2 * heads * rows * rows * HD, 2 * heads * rows * rows + 10 * rows * heads * HD),
        name="attend",
    )(place, probs, *v_parts)


def out_kernel(size, layout, first, place, *refs):
    count = 2 * size - 1
    pieces, weights = refs[: len(layout)], refs[len(layout) : len(layout) + 2 * count]
    heard, out, a_held, w_held, total, a_sems, w_sems = refs[len(layout) + 2 * count :]
    steps, _, tokens, columns = out.shape
    width = columns // 2
    halves, _, _, span_width = w_held.shape
    joined = halves == 1
    step_at, core, position = place[0], place[1], place[2]

    def a_copies():
        for index, (offset, start, groups) in enumerate(layout):
            row = pl.multiple_of(jnp.bitwise_xor(step_at, offset) * tokens, tokens)
            for group in range(groups):
                yield pltpu.make_async_copy(
                    pieces[index].at[group, pl.ds(first, tokens)],
                    a_held.at[start + group, pl.ds(row, tokens)],
                    a_sems.at[index, group],
                )

    def w_copy(half, away, slot):
        group = lax.rem(position + away, size)
        at = jnp.bitwise_xor(core, half)
        if joined:
            span = pl.ds(pl.multiple_of(at * width, 128), width)
            target = w_held.at[0, group, :, span]
        else:
            target = w_held.at[at, group]
        return pltpu.make_async_copy(weights[half * count + slot], target, w_sems.at[half, away])

    for copy in a_copies():
        copy.start()
    for away in range(size):
        for half in range(2):
            if away == 0:
                w_copy(half, 0, 0).start()
                continue

            @pl.when(position + away < size)
            def _(half=half, away=away):
                w_copy(half, away, size - 1 + away).start()

            @pl.when(position + away >= size)
            def _(half=half, away=away):
                w_copy(half, away, size - away).start()

    for copy in a_copies():
        copy.wait()
    for away in range(size):
        group = lax.rem(position + away, size)
        for half in range(2):
            w_copy(half, away, 0).wait()
        for half in range(halves):
            part = jnp.dot(a_held[group], w_held[half, group], preferred_element_type=jnp.float32)
            part = part.astype(jnp.bfloat16).astype(jnp.float32)
            if away == 0:
                total[half] = part
            else:
                total[half] += part
    for half in range(halves):
        span = slice(half * span_width, (half + 1) * span_width)
        reached = jnp.zeros((tokens, span_width), jnp.float32)
        for step in range(steps):
            told = heard[step, -16:, span].astype(jnp.float32)
            gate = told[0:1] + told[1:2] + told[2:3]
            step_width = told[3:4] + told[4:5] + told[5:6]
            branch = total[half, step * tokens : (step + 1) * tokens] * gate
            out[step, 0, :, span] = branch.astype(jnp.bfloat16)
            reached += branch * step_width
            out[step, 1, :, span] = reached.astype(jnp.bfloat16)
            reached += heard[step, first : first + tokens, span].astype(jnp.float32)


def project_out(place, heard, gathered, weights, part, parts):
    size = lax.axis_size("head")
    steps = len(gathered)
    _, tokens, inner = gathered[0][0].shape
    tokens = tokens // parts
    width = weights[0][0].shape[1]
    layout, pieces = [], []
    for offset, held in enumerate(gathered):
        start = 0
        for piece in held:
            layout.append((offset, start, piece.shape[0]))
            pieces.append(piece)
            start += piece.shape[0]
    rows = steps * tokens
    halves = 1 if width % 128 == 0 else 2
    operands = pieces + [w for half in weights for w in half]
    return pl.pallas_call(
        functools.partial(out_kernel, size, tuple(layout), part * tokens),
        in_specs=[SMEM] + [ANY] * len(operands) + [VMEM],
        out_specs=VMEM,
        out_shape=jax.ShapeDtypeStruct((steps, 2, tokens, 2 * width), jnp.bfloat16),
        scratch_shapes=[
            pltpu.VMEM((size, rows, inner), jnp.bfloat16),
            pltpu.VMEM((halves, size, inner, 2 * width // halves), jnp.bfloat16),
            pltpu.VMEM((halves, rows, 2 * width // halves), jnp.float32),
            pltpu.SemaphoreType.DMA((len(layout), size)),
            pltpu.SemaphoreType.DMA((2, size)),
        ],
        compiler_params=params(),
        cost_estimate=cost(4 * rows * size * inner * width, 2 * size * inner * (rows + 2 * width) + 8 * rows * width),
        name="project_out",
    )(place, *operands, heard)


def finish_kernel(base, *refs):
    reached, update = refs[-2:]
    for part, arrived in enumerate(refs[:-2]):
        tokens = arrived.shape[2]
        rows = slice(part * tokens, (part + 1) * tokens)
        reached[rows] = base[rows] + arrived[0, 1].astype(jnp.float32)
        update[rows] = arrived[0, 0]


def finish(base, parts):
    steps, _, tokens, width = parts[0].shape
    by_columns = pl.BlockSpec((base.shape[0], width), lambda i: (0, i))
    return pl.pallas_call(
        finish_kernel,
        grid=(steps,),
        in_specs=[by_columns] + [pl.BlockSpec((1, 2, tokens, width), lambda i: (i, 0, 0, 0))] * len(parts),
        out_specs=[by_columns, by_columns],
        out_shape=[jax.ShapeDtypeStruct(base.shape, jnp.float32), jax.ShapeDtypeStruct(base.shape, jnp.bfloat16)],
        compiler_params=params(),
        cost_estimate=cost(base.size, 14 * base.size),
        name="finish",
    )(base, *parts)


def body(states, timesteps, lengths, modulation, w_query, w_key, w_value, w_out, q_gain, k_gain):
    steps, size = lax.axis_size("step"), lax.axis_size("head")
    step, core, position = (lax.axis_index(axis) for axis in ("step", "fsdp", "head"))
    current = states[0, 0]
    shift = (position >= size // 2).astype(jnp.int32)
    place = jnp.stack([step, core, position, lengths[0], shift]).astype(jnp.int32)

    w_both = jnp.concatenate([w_query, w_key], axis=1)
    mine, other = modulate(place, current, modulation, steps)
    tokens = jnp.stack([mine, swap(other, "fsdp", 1)])
    below, above = [tokens], [tokens]

    def hop(*awaited):
        count = len(below)
        arrived = (below[-1], above[-1])
        up, down = after(arrived, *awaited) if awaited else arrived
        below.append(lax.ppermute(up, "head", [(i, i + 1) for i in range(count - 1, size - 1)]))
        above.append(lax.ppermute(down, "head", [(i, i - 1) for i in range(1, size - count + 1)]))
        return arrived

    hop()
    if steps == 4 and size > 3 and w_value.shape[1] % 256 == 0:
        both_shards, last_round, finished = in_rounds(w_both, w_value, hop)
    else:
        both = forwarded(w_both, direct(w_both))
        both_shards = placed(both)
        last_round = tuple(both[-1])

        def finished(*awaited):
            return placed(forwarded(w_value, direct(after(w_value, *awaited))))

    while len(below) < size:
        hop()
    line = below, above
    early = tuple(held[: size - 1] + [held[0]] for held in line)
    step_width = (timesteps[0, 1] - timesteps[0, 0]).astype(jnp.float32) / 1000.0
    told = tell(place, step_width[None], current, modulation, steps)
    partner_below, partner_above = [swap(after(w_out, below[1], above[1]), "fsdp", 1)], []
    first_here, first_there = project(after(place, told, *partner_below), early, both_shards, "first", "first")
    ended = (below[-1], above[-1]) + last_round
    first_there = after(first_there, *ended)
    v_shards = finished(*ended, first_here)
    v_last = (v_shards[-1][0], v_shards[-2][0])
    parts = [first_here, swap(first_there, "fsdp", 1)]
    last_here, last_there = project(place, line, both_shards, "last", "last")
    parts += [last_here, swap(after(last_there, *v_last), "fsdp", 1)]
    v_here, v_there = project(after(place, last_here), line, v_shards, "all", "value")
    v_parts = [v_here, swap(v_there, "fsdp", 1)]
    heard = lax.all_to_all(after(told, last_here, *v_last), "step", 0, 0)

    below, above = [w_out], [w_out]
    for count in range(1, size):
        up, down = below[-1], above[-1]
        if count == 1:
            up, down = after((up, down), *ended, first_here)
        if count == 2:
            up, down = after((up, down), v_here)
        if count == size - 1:
            up, down = after((up, down), quarter)
        below.append(lax.ppermute(up, "head", [(i, i + 1) for i in range(count - 1, size - 1)]))
        above.append(lax.ppermute(down, "head", [(i, i - 1) for i in range(1, size - count + 1)]))
        arrived = (below[-1], above[-1])
        if count == size - 1:
            near = direct(quarter)
            gathered = forwarded(quarter, near)
            arrived = after(arrived, *[piece for pieces in near.values() for piece in pieces])
        partner_below.append(swap(arrived[0], "fsdp", 1))
        partner_above.append(swap(arrived[1], "fsdp", 1))
        if count == 1:
            own_squares = norms(after(place, below[-1], above[-1], v_here), parts, size)
            squares = lax.all_to_all(own_squares, "head", 0, 0)
        if count == size - 2:
            ready = after(squares, *partner_below[:-1], *partner_above[:-1], below[-1], above[-1], heard)
            probs = probabilities(place, ready, parts, q_gain, k_gain)
            attended = attend(place, probs, v_parts, size)
            quarter = after(lax.all_to_all(attended, "head", 0, 0), partner_below[-1], partner_above[-1])

    raw = [w_out] + below[1:] + above[1:]
    out_weights = (raw, partner_below + partner_above)
    carried = step_width * current + jnp.where(step == 0, current, jnp.zeros_like(current))

    halves = 2
    sent = [project_out(place, heard, gathered, out_weights, part, halves) for part in range(halves)]
    arrived = after(tuple(lax.all_to_all(part, "step", 0, 0) for part in sent), carried)
    reached, update = finish(carried, arrived)
    return reached[None, None], update[None, None]


def solution(mesh):
    in_specs = (
        P("step", "fsdp", "head", None),
        P("step", None),
        P("fsdp"),
        P("step", None, None),
        P(("step", "fsdp"), "head"),
        P(("step", "fsdp"), "head"),
        P(("step", "fsdp"), "head"),
        P("head", ("step", "fsdp")),
        P("head"),
        P("head"),
    )
    out_specs = (P("step", "fsdp", "head", None), P("step", "fsdp", "head", None))
    return jax.shard_map(body, mesh=mesh, in_specs=in_specs, out_specs=out_specs, check_vma=False)
```

```python
import functools
import math

import jax
import jax.numpy as jnp
from jax import lax
from jax.experimental import pallas as pl
from jax.experimental.pallas import tpu as pltpu
from jax.sharding import PartitionSpec as P

HD = 128
MIB = 1 << 20
SMEM = pl.BlockSpec(memory_space=pltpu.SMEM)
VMEM = pl.BlockSpec(memory_space=pltpu.VMEM)
ANY = pl.BlockSpec(memory_space=pl.ANY)


def swap(x, axis, offset):
    return lax.ppermute(x, axis, [(i, i ^ offset) for i in range(lax.axis_size(axis))])


def bits_of(axis):
    return [1 << bit for bit in range(lax.axis_size(axis).bit_length() - 1)]


def direct(x):
    return {bit: [swap(x, "step", bit)] for bit in bits_of("step")}


def forwarded(x, near, *awaited):
    held = {0: [x], **near}
    half = x.shape[0] // 2
    for offset in range(1, lax.axis_size("step")):
        low, high = offset & -offset, 1 << (offset.bit_length() - 1)
        if offset in held:
            continue
        top, bottom = held[offset ^ low], held[offset ^ high]
        top = top[0][:half] if len(top) == 1 else top[0]
        bottom = bottom[0][half:] if len(bottom) == 1 else bottom[1]
        if awaited:
            top, bottom = after((top, bottom), *awaited)
        held[offset] = [swap(top, "step", low), swap(bottom, "step", high)]
    return [held[offset] for offset in range(lax.axis_size("step"))]


def placed(held, column=0):
    found = []
    for offset, pieces in enumerate(held):
        row = 0
        for piece in pieces:
            found.append((piece, offset, row, 0, column, piece.shape[1]))
            row += piece.shape[0]
    return found


def in_rounds(w_both, w_value, hop):
    width = w_value.shape[1]
    a1, a2 = swap(w_both, "step", 1), swap(w_both, "step", 2)
    e1, e2 = after((a1, a2), *hop())
    b1, b2 = swap(e2[:, :width], "step", 1), swap(e1[:, width:], "step", 2)
    v1, v2 = after((w_value, w_value), b1, b2, *hop(b1, b2))
    c1, c2 = swap(v1, "step", 1), swap(v2, "step", 2)
    both = [
        (w_both, 0, 0, 0, 0, 2 * width),
        (a1, 1, 0, 0, 0, 2 * width),
        (a2, 2, 0, 0, 0, 2 * width),
        (b1, 3, 0, 0, 0, width),
        (b2, 3, 0, 0, width, width),
    ]

    def finished(*awaited):
        f1, f2 = after((c1, c2), *awaited)
        d1, d2 = swap(f2[:, : width // 2], "step", 1), swap(f1[:, width // 2 :], "step", 2)
        whole = [(w_value, 0, 0, 0, 0, width), (c1, 1, 0, 0, 0, width), (c2, 2, 0, 0, 0, width)]
        return whole + [(d1, 3, 0, 0, 0, width // 2), (d2, 3, 0, 0, width // 2, width // 2)]

    return both, (c1, c2), finished


def after(x, *others):
    return lax.optimization_barrier((x,) + others)[0]


def params(mib=56):
    return pltpu.CompilerParams(vmem_limit_bytes=mib * MIB)


def cost(flops, moved, raised=0):
    return pl.CostEstimate(flops=int(flops) // 4, bytes_accessed=int(moved) // 4, transcendentals=int(raised) // 4)


def modulate_kernel(steps, place, states, rows, mine, other):
    current = states[...]
    centre = jnp.mean(current, axis=-1, keepdims=True)
    centred = current - centre
    spread_of = jnp.mean(centred * centred, axis=-1, keepdims=True)
    shift, scale = rows[0, 0:1, :], rows[0, 1:2, :]
    modulated = (centred * lax.rsqrt(spread_of + 1e-06) * (1.0 + scale) + shift).astype(jnp.bfloat16)
    core = place[1]
    for block in range(2 * steps):
        width = modulated.shape[1] // (2 * steps)
        piece = modulated[:, block * width : (block + 1) * width]
        at = slice(block // 2 * width, (block // 2 + 1) * width)

        @pl.when(core == block % 2)
        def _(piece=piece, at=at):
            mine[:, at] = piece

        @pl.when(core != block % 2)
        def _(piece=piece, at=at):
            other[:, at] = piece


def modulate(place, states, rows, steps):
    tokens, width = states.shape
    tile = 32
    out = jax.ShapeDtypeStruct((tokens, width // 2), jnp.bfloat16)
    spec = pl.BlockSpec((tile, width // 2), lambda i: (i, 0))
    return pl.pallas_call(
        functools.partial(modulate_kernel, steps),
        grid=(tokens // tile,),
        in_specs=[SMEM, pl.BlockSpec((tile, width), lambda i: (i, 0)), pl.BlockSpec(rows.shape, lambda i: (0, 0, 0))],
        out_specs=[spec, spec],
        out_shape=[out, out],
        compiler_params=params(),
        cost_estimate=cost(10 * tokens * width, 6 * tokens * width),
        name="modulate",
    )(place, states, rows)


def terms(x):
    high = x.astype(jnp.bfloat16).astype(jnp.float32)
    middle = (x - high).astype(jnp.bfloat16).astype(jnp.float32)
    return [high, middle, x - high - middle]


def tell_kernel(place, step_width, states, rows, out):
    current = states[...]
    tokens, columns = current.shape
    width = step_width[0]
    anchor = jnp.where(place[0] == 0, 1.0, 0.0)
    out[0, :tokens] = (width * current + anchor * current).astype(jnp.bfloat16)
    told = terms(rows[0, 2:3, :]) + terms(jnp.full((1, columns), width, jnp.float32))
    told.append(jnp.zeros((10, columns), jnp.float32))
    out[0, tokens:] = jnp.concatenate(told).astype(jnp.bfloat16)


def tell(place, step_width, states, rows, steps):
    tokens, width = states.shape
    columns = width // steps
    return pl.pallas_call(
        tell_kernel,
        grid=(steps,),
        in_specs=[
            SMEM,
            SMEM,
            pl.BlockSpec((tokens, columns), lambda i: (0, i)),
            pl.BlockSpec((1, rows.shape[1], columns), lambda i: (0, 0, i)),
        ],
        out_specs=pl.BlockSpec((1, tokens + 16, columns), lambda i: (i, 0, 0)),
        out_shape=jax.ShapeDtypeStruct((steps, tokens + 16, columns), jnp.bfloat16),
        compiler_params=params(),
        cost_estimate=cost(4 * tokens * width, 6 * tokens * width),
        name="tell",
    )(place, step_width, states, rows)


def project_kernel(size, parts, shard, layout, place, *refs):
    count = 2 * size - 1
    own, below, above = refs[0], refs[1:size], refs[size:count]
    weights = refs[count : count + len(layout)]
    here, there, x_held, w_held, x_sems, w_sems = refs[count + len(layout) :]
    tokens, depth = own.shape[1:]
    step_at, position, shift = place[0], place[2], place[4]
    early = size - 1
    blocks = {"first": range(early), "last": range(early, size), "all": range(size)}[parts]

    def x_copy(ref, clip, block):
        row = (clip * len(blocks) + block - blocks[0]) * tokens
        return pltpu.make_async_copy(
            ref.at[clip], x_held.at[pl.ds(pl.multiple_of(row, tokens), tokens)], x_sems.at[clip, block]
        )

    def w_copies():
        for index, (ref, (offset, row, source, target, count)) in enumerate(zip(weights, layout)):
            at = jnp.bitwise_xor(step_at, offset) * shard + row
            rows = ref.shape[0]
            part = w_held.at[pl.ds(pl.multiple_of(at, rows), rows), pl.ds(target, count)]
            yield pltpu.make_async_copy(ref.at[:, pl.ds(source, count)], part, w_sems.at[index])

    for copy in w_copies():
        copy.start()
    for clip in range(2):
        for away in range(size):
            for sign, held in ((1, above), (-1, below)):
                if away == 0 and sign < 0:
                    continue
                source = own if away == 0 else held[away - 1]
                block_at = position + sign * away
                block = lax.rem(block_at - shift + size, size)
                inside = jnp.logical_and(block_at >= 0, block_at < size)
                inside = jnp.logical_and(inside, jnp.logical_and(block >= blocks[0], block <= blocks[-1]))

                @pl.when(inside)
                def _(source=source, block=block, clip=clip):
                    x_copy(source, clip, block).start()

    for copy in w_copies():
        copy.wait()
    for clip in range(2):
        for block in blocks:
            x_copy(own, clip, block).wait()
    rows, columns = here.shape
    width = columns if columns % 512 else columns // 2
    for start in range(0, columns, width):
        span = slice(start, start + width)
        product = jnp.dot(x_held[...], w_held[:, span], preferred_element_type=jnp.float32)
        here[:, span] = product[:rows]
        there[:, span] = product[rows:]


def project(place, line, shards, parts, name):
    size = lax.axis_size("head")
    below, above = line
    operands = [below[0]] + below[1:] + above[1:]
    _, tokens, depth = operands[0].shape
    weights = [piece[0] for piece in shards]
    layout = [piece[1:] for piece in shards]
    shard, columns = weights[0].shape
    rows = {"first": size - 1, "last": 1, "all": size}[parts] * tokens
    out = jax.ShapeDtypeStruct((rows, columns), jnp.float32)
    moved = 2 * depth * (2 * rows + columns) + 8 * rows * columns
    return pl.pallas_call(
        functools.partial(project_kernel, size, parts, shard, tuple(layout)),
        in_specs=[SMEM] + [ANY] * (len(operands) + len(weights)),
        out_specs=[VMEM, VMEM],
        out_shape=[out, out],
        scratch_shapes=[
            pltpu.VMEM((2 * rows, depth), jnp.bfloat16),
            pltpu.VMEM((depth, columns), jnp.bfloat16),
            pltpu.SemaphoreType.DMA((2, size)),
            pltpu.SemaphoreType.DMA((len(layout),)),
        ],
        compiler_params=params(),
        cost_estimate=cost(4 * rows * depth * columns, moved),
        name=name,
    )(place, *operands, *weights)


def norms_kernel(place, first_a, first_b, last_a, last_b, out):
    width = first_a.shape[1] // 2
    rows = []
    for which in range(2):
        found = []
        for one, other in ((first_a, first_b), (last_a, last_b)):
            lanes = None
            for start in range(which * width, (which + 1) * width, HD):
                total = one[:, start : start + HD] + other[:, start : start + HD]
                lanes = total * total if lanes is None else lanes + total * total
            found.append(jnp.sum(lanes.T, axis=0, keepdims=True))
        straight = jnp.concatenate(found, axis=1)
        wrapped = jnp.concatenate(found[::-1], axis=1)
        rows.append(jnp.where(place[4] == 0, straight, wrapped))
    both = jnp.concatenate(rows, axis=0)
    for peer in range(out.shape[0]):
        out[peer] = both


def norms(place, parts, size):
    rows = parts[0].shape[0] + parts[2].shape[0]
    return pl.pallas_call(
        norms_kernel,
        in_specs=[SMEM] + [VMEM] * 4,
        out_specs=VMEM,
        out_shape=jax.ShapeDtypeStruct((size, 2, rows), jnp.float32),
        compiler_params=params(),
        cost_estimate=cost(4 * rows * parts[0].shape[1], 8 * rows * parts[0].shape[1]),
        name="norms",
    )(place, *parts)


def probs_kernel(tokens, full_width, place, squares, *refs):
    parts, (q_gain, k_gain, out, scales) = refs[:8], refs[8:]
    rows = scales.shape[1]

    @pl.when(pl.program_id(0) == 0)
    def _():
        total = squares[0]
        for peer in range(1, squares.shape[0]):
            total = total + squares[peer]
        turned = jnp.concatenate([total[:, tokens:], total[:, :tokens]], axis=1)
        total = jnp.where(place[4] == 0, total, turned)
        scale = lax.rsqrt(total / full_width + 1e-06)
        for which in range(2):
            scales[which] = jnp.broadcast_to(scale[which : which + 1], (HD, rows)).T

    column = lax.broadcasted_iota(jnp.int32, (1, rows), 1) + place[4] * tokens
    valid = jnp.where(column >= rows, column - rows, column) < place[3]
    for head in range(out.shape[0]):
        span = slice(head * HD, (head + 1) * HD)

        def normed(at, gain, which):
            joined = [parts[at + i][:, span] + parts[at + i + 1][:, span] for i in (0, 2)]
            return (jnp.concatenate(joined) * scales[which] * gain[:, span]).astype(jnp.bfloat16)

        queries, keys = normed(0, q_gain, 0), normed(4, k_gain, 1)
        scores = lax.dot_general(queries, keys, (((1,), (1,)), ((), ())), preferred_element_type=jnp.float32)
        scores = jnp.where(valid, scores * (1.0 / math.sqrt(HD)), -jnp.inf)
        raised = jnp.exp(scores - jnp.max(scores, axis=-1, keepdims=True))
        out[head] = (raised * (1.0 / jnp.sum(raised, axis=-1, keepdims=True))).astype(jnp.bfloat16)


def at_once(heads):
    return 2 if heads % 2 == 0 else 1


def probabilities(place, squares, parts, q_gain, k_gain):
    columns = parts[0].shape[1] // 2
    rows = parts[0].shape[0] + parts[2].shape[0]
    heads = columns // HD
    group = at_once(heads)
    q_blocks = [pl.BlockSpec((part.shape[0], group * HD), lambda i: (0, i)) for part in parts]
    k_blocks = [pl.BlockSpec((part.shape[0], group * HD), lambda i: (0, i + heads // group)) for part in parts]
    gain = pl.BlockSpec((1, group * HD), lambda i: (0, i))
    return pl.pallas_call(
        functools.partial(probs_kernel, parts[2].shape[0], float(columns * squares.shape[0])),
        grid=(heads // group,),
        in_specs=[SMEM, pl.BlockSpec(squares.shape, lambda i: (0, 0, 0))] + q_blocks + k_blocks + [gain] * 2,
        out_specs=pl.BlockSpec((group, rows, rows), lambda i: (i, 0, 0)),
        out_shape=jax.ShapeDtypeStruct((heads, rows, rows), jnp.bfloat16),
        scratch_shapes=[pltpu.VMEM((2, rows, HD), jnp.float32)],
        compiler_params=params(),
        cost_estimate=cost(2 * heads * rows * rows * HD, 16 * rows * columns + 2 * heads * rows * rows, heads * rows * rows),
        name="probs",
    )(place, squares, *parts, *parts, q_gain[None], k_gain[None])


def attend_kernel(place, probs, v_a, v_b, out, held):
    size, tokens, _ = out.shape
    for head in range(probs.shape[0]):
        span = slice(head * HD, (head + 1) * HD)
        values = (v_a[:, span] + v_b[:, span]).astype(jnp.bfloat16)
        held[:, span] = jnp.dot(probs[head], values, preferred_element_type=jnp.float32)
    for block in range(size):
        at = lax.rem(block - place[4] + size, size) * tokens
        out[block] = held[pl.ds(pl.multiple_of(at, tokens), tokens)].astype(jnp.bfloat16)


def attend(place, probs, v_parts, size):
    heads, rows, _ = probs.shape
    tokens = rows // size
    group = at_once(heads)
    by_head = pl.BlockSpec((rows, group * HD), lambda i: (0, i))
    return pl.pallas_call(
        attend_kernel,
        grid=(heads // group,),
        in_specs=[SMEM, pl.BlockSpec((group, rows, rows), lambda i: (i, 0, 0)), by_head, by_head],
        out_specs=pl.BlockSpec((size, tokens, group * HD), lambda i: (0, 0, i)),
        out_shape=jax.ShapeDtypeStruct((size, tokens, heads * HD), jnp.bfloat16),
        scratch_shapes=[pltpu.VMEM((rows, group * HD), jnp.float32)],
        compiler_params=params(),
        cost_estimate=cost(2 * heads * rows * rows * HD, 2 * heads * rows * rows + 10 * rows * heads * HD),
        name="attend",
    )(place, probs, *v_parts)


def out_kernel(size, layout, first, place, *refs):
    count = 2 * size - 1
    pieces, weights = refs[: len(layout)], refs[len(layout) : len(layout) + 2 * count]
    heard, out, a_held, w_held, total, a_sems, w_sems = refs[len(layout) + 2 * count :]
    steps, _, tokens, columns = out.shape
    width = columns // 2
    halves, _, _, span_width = w_held.shape
    joined = halves == 1
    step_at, core, position = place[0], place[1], place[2]

    def a_copies():
        for index, (offset, start, groups) in enumerate(layout):
            row = pl.multiple_of(jnp.bitwise_xor(step_at, offset) * tokens, tokens)
            for group in range(groups):
                yield pltpu.make_async_copy(
                    pieces[index].at[group, pl.ds(first, tokens)],
                    a_held.at[start + group, pl.ds(row, tokens)],
                    a_sems.at[index, group],
                )

    def w_copy(half, away, slot):
        group = lax.rem(position + away, size)
        at = jnp.bitwise_xor(core, half)
        if joined:
            span = pl.ds(pl.multiple_of(at * width, 128), width)
            target = w_held.at[0, group, :, span]
        else:
            target = w_held.at[at, group]
        return pltpu.make_async_copy(weights[half * count + slot], target, w_sems.at[half, away])

    for copy in a_copies():
        copy.start()
    for away in range(size):
        for half in range(2):
            if away == 0:
                w_copy(half, 0, 0).start()
                continue

            @pl.when(position + away < size)
            def _(half=half, away=away):
                w_copy(half, away, size - 1 + away).start()

            @pl.when(position + away >= size)
            def _(half=half, away=away):
                w_copy(half, away, size - away).start()

    for copy in a_copies():
        copy.wait()
    for away in range(size):
        group = lax.rem(position + away, size)
        for half in range(2):
            w_copy(half, away, 0).wait()
        for half in range(halves):
            part = jnp.dot(a_held[group], w_held[half, group], preferred_element_type=jnp.float32)
            part = part.astype(jnp.bfloat16).astype(jnp.float32)
            if away == 0:
                total[half] = part
            else:
                total[half] += part
    for half in range(halves):
        span = slice(half * span_width, (half + 1) * span_width)
        reached = jnp.zeros((tokens, span_width), jnp.float32)
        for step in range(steps):
            told = heard[step, -16:, span].astype(jnp.float32)
            gate = told[0:1] + told[1:2] + told[2:3]
            step_width = told[3:4] + told[4:5] + told[5:6]
            branch = total[half, step * tokens : (step + 1) * tokens] * gate
            out[step, 0, :, span] = branch.astype(jnp.bfloat16)
            reached += branch * step_width
            out[step, 1, :, span] = reached.astype(jnp.bfloat16)
            reached += heard[step, first : first + tokens, span].astype(jnp.float32)


def project_out(place, heard, gathered, weights, part, parts):
    size = lax.axis_size("head")
    steps = len(gathered)
    _, tokens, inner = gathered[0][0].shape
    tokens = tokens // parts
    width = weights[0][0].shape[1]
    layout, pieces = [], []
    for offset, held in enumerate(gathered):
        start = 0
        for piece in held:
            layout.append((offset, start, piece.shape[0]))
            pieces.append(piece)
            start += piece.shape[0]
    rows = steps * tokens
    halves = 1 if width % 128 == 0 else 2
    operands = pieces + [w for half in weights for w in half]
    return pl.pallas_call(
        functools.partial(out_kernel, size, tuple(layout), part * tokens),
        in_specs=[SMEM] + [ANY] * len(operands) + [VMEM],
        out_specs=VMEM,
        out_shape=jax.ShapeDtypeStruct((steps, 2, tokens, 2 * width), jnp.bfloat16),
        scratch_shapes=[
            pltpu.VMEM((size, rows, inner), jnp.bfloat16),
            pltpu.VMEM((halves, size, inner, 2 * width // halves), jnp.bfloat16),
            pltpu.VMEM((halves, rows, 2 * width // halves), jnp.float32),
            pltpu.SemaphoreType.DMA((len(layout), size)),
            pltpu.SemaphoreType.DMA((2, size)),
        ],
        compiler_params=params(),
        cost_estimate=cost(4 * rows * size * inner * width, 2 * size * inner * (rows + 2 * width) + 8 * rows * width),
        name="project_out",
    )(place, *operands, heard)


def finish_kernel(base, *refs):
    reached, update = refs[-2:]
    for part, arrived in enumerate(refs[:-2]):
        tokens = arrived.shape[2]
        rows = slice(part * tokens, (part + 1) * tokens)
        reached[rows] = base[rows] + arrived[0, 1].astype(jnp.float32)
        update[rows] = arrived[0, 0]


def finish(base, parts):
    steps, _, tokens, width = parts[0].shape
    by_columns = pl.BlockSpec((base.shape[0], width), lambda i: (0, i))
    return pl.pallas_call(
        finish_kernel,
        grid=(steps,),
        in_specs=[by_columns] + [pl.BlockSpec((1, 2, tokens, width), lambda i: (i, 0, 0, 0))] * len(parts),
        out_specs=[by_columns, by_columns],
        out_shape=[jax.ShapeDtypeStruct(base.shape, jnp.float32), jax.ShapeDtypeStruct(base.shape, jnp.bfloat16)],
        compiler_params=params(),
        cost_estimate=cost(base.size, 14 * base.size),
        name="finish",
    )(base, *parts)


def body(states, timesteps, lengths, modulation, w_query, w_key, w_value, w_out, q_gain, k_gain):
    steps, size = lax.axis_size("step"), lax.axis_size("head")
    step, core, position = (lax.axis_index(axis) for axis in ("step", "fsdp", "head"))
    current = states[0, 0]
    shift = (position >= size // 2).astype(jnp.int32)
    place = jnp.stack([step, core, position, lengths[0], shift]).astype(jnp.int32)

    w_both = jnp.concatenate([w_query, w_key], axis=1)
    mine, other = modulate(place, current, modulation, steps)
    tokens = jnp.stack([mine, swap(other, "fsdp", 1)])
    below, above = [tokens], [tokens]

    def hop(*awaited):
        count = len(below)
        arrived = (below[-1], above[-1])
        up, down = after(arrived, *awaited) if awaited else arrived
        below.append(lax.ppermute(up, "head", [(i, i + 1) for i in range(count - 1, size - 1)]))
        above.append(lax.ppermute(down, "head", [(i, i - 1) for i in range(1, size - count + 1)]))
        return arrived

    hop()
    if steps == 4 and size > 3 and w_value.shape[1] % 256 == 0:
        both_shards, last_round, finished = in_rounds(w_both, w_value, hop)
    else:
        both = forwarded(w_both, direct(w_both))
        both_shards = placed(both)
        last_round = tuple(both[-1])

        def finished(*awaited):
            return placed(forwarded(w_value, direct(after(w_value, *awaited))))

    while len(below) < size:
        hop()
    line = below, above
    early = tuple(held[: size - 1] + [held[0]] for held in line)
    step_width = (timesteps[0, 1] - timesteps[0, 0]).astype(jnp.float32) / 1000.0
    told = tell(place, step_width[None], current, modulation, steps)
    partner_below, partner_above = [swap(after(w_out, below[1], above[1]), "fsdp", 1)], []
    first_here, first_there = project(after(place, told, *partner_below), early, both_shards, "first", "first")
    ended = (below[-1], above[-1]) + last_round
    second_round = (both_shards[-1][0], both_shards[-2][0], early[0][-2], early[1][-2])
    heard = lax.all_to_all(after(told, *second_round), "step", 0, 0)
    first_there = after(first_there, heard, *ended)
    v_shards = finished(*ended, first_here)
    v_last = (v_shards[-1][0], v_shards[-2][0])
    parts = [first_here, swap(first_there, "fsdp", 1)]
    last_here, last_there = project(after(place, heard), line, both_shards, "last", "last")
    parts += [last_here, swap(after(last_there, *v_last), "fsdp", 1)]
    v_here, v_there = project(after(place, last_here), line, v_shards, "all", "value")
    v_parts = [v_here, swap(v_there, "fsdp", 1)]

    below, above = [w_out], [w_out]
    for count in range(1, size):
        up, down = below[-1], above[-1]
        if count == 1:
            up, down = after((up, down), line[0][-1], line[1][-1], first_here)
        if count == 2:
            up, down = after((up, down), v_here)
        if count == size - 1:
            up, down = after((up, down), quarter)
        below.append(lax.ppermute(up, "head", [(i, i + 1) for i in range(count - 1, size - 1)]))
        above.append(lax.ppermute(down, "head", [(i, i - 1) for i in range(1, size - count + 1)]))
        arrived = (below[-1], above[-1])
        if count == size - 1:
            near = direct(quarter)
            gathered = forwarded(quarter, near)
            arrived = after(arrived, *[piece for pieces in near.values() for piece in pieces])
        partner_below.append(swap(arrived[0], "fsdp", 1))
        partner_above.append(swap(arrived[1], "fsdp", 1))
        if count == 1:
            own_squares = norms(after(place, below[-1], above[-1], v_here), parts, size)
            squares = lax.all_to_all(own_squares, "head", 0, 0)
        if count == size - 2:
            ready = after(squares, *partner_below[:-1], *partner_above[:-1], below[-1], above[-1])
            probs = probabilities(place, ready, parts, q_gain, k_gain)
            attended = attend(place, probs, v_parts, size)
            quarter = after(lax.all_to_all(attended, "head", 0, 0), partner_below[-1], partner_above[-1])

    raw = [w_out] + below[1:] + above[1:]
    out_weights = (raw, partner_below + partner_above)
    carried = step_width * current + jnp.where(step == 0, current, jnp.zeros_like(current))

    halves = 1
    sent = [project_out(place, heard, gathered, out_weights, part, halves) for part in range(halves)]
    arrived = after(tuple(lax.all_to_all(part, "step", 0, 0) for part in sent), carried)
    reached, update = finish(carried, arrived)
    return reached[None, None], update[None, None]


def solution(mesh):
    in_specs = (
        P("step", "fsdp", "head", None),
        P("step", None),
        P("fsdp"),
        P("step", None, None),
        P(("step", "fsdp"), "head"),
        P(("step", "fsdp"), "head"),
        P(("step", "fsdp"), "head"),
        P("head", ("step", "fsdp")),
        P("head"),
        P("head"),
    )
    out_specs = (P("step", "fsdp", "head", None), P("step", "fsdp", "head", None))
    return jax.shard_map(body, mesh=mesh, in_specs=in_specs, out_specs=out_specs, check_vma=False)
```

```python
import functools
import math

import jax
import jax.numpy as jnp
from jax import lax
from jax.experimental import pallas as pl
from jax.experimental.pallas import tpu as pltpu
from jax.sharding import PartitionSpec as P

HD = 128
MIB = 1 << 20
SMEM = pl.BlockSpec(memory_space=pltpu.SMEM)
VMEM = pl.BlockSpec(memory_space=pltpu.VMEM)
ANY = pl.BlockSpec(memory_space=pl.ANY)


def swap(x, axis, offset):
    return lax.ppermute(x, axis, [(i, i ^ offset) for i in range(lax.axis_size(axis))])


def bits_of(axis):
    return [1 << bit for bit in range(lax.axis_size(axis).bit_length() - 1)]


def direct(x):
    return {bit: [swap(x, "step", bit)] for bit in bits_of("step")}


def forwarded(x, near, *awaited):
    held = {0: [x], **near}
    half = x.shape[0] // 2
    for offset in range(1, lax.axis_size("step")):
        low, high = offset & -offset, 1 << (offset.bit_length() - 1)
        if offset in held:
            continue
        top, bottom = held[offset ^ low], held[offset ^ high]
        top = top[0][:half] if len(top) == 1 else top[0]
        bottom = bottom[0][half:] if len(bottom) == 1 else bottom[1]
        if awaited:
            top, bottom = after((top, bottom), *awaited)
        held[offset] = [swap(top, "step", low), swap(bottom, "step", high)]
    return [held[offset] for offset in range(lax.axis_size("step"))]


def placed(held, column=0):
    found = []
    for offset, pieces in enumerate(held):
        row = 0
        for piece in pieces:
            found.append((piece, offset, row, 0, column, piece.shape[1]))
            row += piece.shape[0]
    return found


def in_rounds(w_both, w_value, hop):
    width = w_value.shape[1]
    a1, a2 = swap(w_both, "step", 1), swap(w_both, "step", 2)
    e1, e2 = after((a1, a2), *hop())
    b1, b2 = swap(e2[:, :width], "step", 1), swap(e1[:, width:], "step", 2)
    v1, v2 = after((w_value, w_value), b1, b2, *hop(b1, b2))
    c1, c2 = swap(v1, "step", 1), swap(v2, "step", 2)
    both = [
        (w_both, 0, 0, 0, 0, 2 * width),
        (a1, 1, 0, 0, 0, 2 * width),
        (a2, 2, 0, 0, 0, 2 * width),
        (b1, 3, 0, 0, 0, width),
        (b2, 3, 0, 0, width, width),
    ]

    def finished(*awaited):
        f1, f2 = after((c1, c2), *awaited)
        d1, d2 = swap(f2[:, : width // 2], "step", 1), swap(f1[:, width // 2 :], "step", 2)
        whole = [(w_value, 0, 0, 0, 0, width), (c1, 1, 0, 0, 0, width), (c2, 2, 0, 0, 0, width)]
        return whole + [(d1, 3, 0, 0, 0, width // 2), (d2, 3, 0, 0, width // 2, width // 2)]

    return both, (c1, c2), finished


def after(x, *others):
    return lax.optimization_barrier((x,) + others)[0]


def params(mib=56):
    return pltpu.CompilerParams(vmem_limit_bytes=mib * MIB)


def cost(flops, moved, raised=0):
    return pl.CostEstimate(flops=int(flops) // 4, bytes_accessed=int(moved) // 4, transcendentals=int(raised) // 4)


def modulate_kernel(steps, place, states, rows, mine, other):
    current = states[...]
    centre = jnp.mean(current, axis=-1, keepdims=True)
    centred = current - centre
    spread_of = jnp.mean(centred * centred, axis=-1, keepdims=True)
    shift, scale = rows[0, 0:1, :], rows[0, 1:2, :]
    modulated = (centred * lax.rsqrt(spread_of + 1e-06) * (1.0 + scale) + shift).astype(jnp.bfloat16)
    core = place[1]
    for block in range(2 * steps):
        width = modulated.shape[1] // (2 * steps)
        piece = modulated[:, block * width : (block + 1) * width]
        at = slice(block // 2 * width, (block // 2 + 1) * width)

        @pl.when(core == block % 2)
        def _(piece=piece, at=at):
            mine[:, at] = piece

        @pl.when(core != block % 2)
        def _(piece=piece, at=at):
            other[:, at] = piece


def modulate(place, states, rows, steps):
    tokens, width = states.shape
    tile = 32
    out = jax.ShapeDtypeStruct((tokens, width // 2), jnp.bfloat16)
    spec = pl.BlockSpec((tile, width // 2), lambda i: (i, 0))
    return pl.pallas_call(
        functools.partial(modulate_kernel, steps),
        grid=(tokens // tile,),
        in_specs=[SMEM, pl.BlockSpec((tile, width), lambda i: (i, 0)), pl.BlockSpec(rows.shape, lambda i: (0, 0, 0))],
        out_specs=[spec, spec],
        out_shape=[out, out],
        compiler_params=params(),
        cost_estimate=cost(10 * tokens * width, 6 * tokens * width),
        name="modulate",
    )(place, states, rows)


def terms(x):
    high = x.astype(jnp.bfloat16).astype(jnp.float32)
    middle = (x - high).astype(jnp.bfloat16).astype(jnp.float32)
    return [high, middle, x - high - middle]


def tell_kernel(place, step_width, states, rows, out):
    current = states[...]
    tokens, columns = current.shape
    width = step_width[0]
    anchor = jnp.where(place[0] == 0, 1.0, 0.0)
    out[0, :tokens] = (width * current + anchor * current).astype(jnp.bfloat16)
    told = terms(rows[0, 2:3, :]) + terms(jnp.full((1, columns), width, jnp.float32))
    told.append(jnp.zeros((10, columns), jnp.float32))
    out[0, tokens:] = jnp.concatenate(told).astype(jnp.bfloat16)


def tell(place, step_width, states, rows, steps):
    tokens, width = states.shape
    columns = width // steps
    return pl.pallas_call(
        tell_kernel,
        grid=(steps,),
        in_specs=[
            SMEM,
            SMEM,
            pl.BlockSpec((tokens, columns), lambda i: (0, i)),
            pl.BlockSpec((1, rows.shape[1], columns), lambda i: (0, 0, i)),
        ],
        out_specs=pl.BlockSpec((1, tokens + 16, columns), lambda i: (i, 0, 0)),
        out_shape=jax.ShapeDtypeStruct((steps, tokens + 16, columns), jnp.bfloat16),
        compiler_params=params(),
        cost_estimate=cost(4 * tokens * width, 6 * tokens * width),
        name="tell",
    )(place, step_width, states, rows)


def project_kernel(size, parts, shard, layout, place, *refs):
    count = 2 * size - 1
    own, below, above = refs[0], refs[1:size], refs[size:count]
    weights = refs[count : count + len(layout)]
    here, there, x_held, w_held, x_sems, w_sems = refs[count + len(layout) :]
    tokens, depth = own.shape[1:]
    step_at, position, shift = place[0], place[2], place[4]
    early = size - 1
    blocks = {"first": range(early), "last": range(early, size), "all": range(size)}[parts]

    def x_copy(ref, clip, block):
        row = (clip * len(blocks) + block - blocks[0]) * tokens
        return pltpu.make_async_copy(
            ref.at[clip], x_held.at[pl.ds(pl.multiple_of(row, tokens), tokens)], x_sems.at[clip, block]
        )

    def w_copies():
        for index, (ref, (offset, row, source, target, count)) in enumerate(zip(weights, layout)):
            at = jnp.bitwise_xor(step_at, offset) * shard + row
            rows = ref.shape[0]
            part = w_held.at[pl.ds(pl.multiple_of(at, rows), rows), pl.ds(target, count)]
            yield pltpu.make_async_copy(ref.at[:, pl.ds(source, count)], part, w_sems.at[index])

    for copy in w_copies():
        copy.start()
    for clip in range(2):
        for away in range(size):
            for sign, held in ((1, above), (-1, below)):
                if away == 0 and sign < 0:
                    continue
                source = own if away == 0 else held[away - 1]
                block_at = position + sign * away
                block = lax.rem(block_at - shift + size, size)
                inside = jnp.logical_and(block_at >= 0, block_at < size)
                inside = jnp.logical_and(inside, jnp.logical_and(block >= blocks[0], block <= blocks[-1]))

                @pl.when(inside)
                def _(source=source, block=block, clip=clip):
                    x_copy(source, clip, block).start()

    for copy in w_copies():
        copy.wait()
    for clip in range(2):
        for block in blocks:
            x_copy(own, clip, block).wait()
    rows, columns = here.shape
    width = columns if columns % 512 else columns // 2
    for start in range(0, columns, width):
        span = slice(start, start + width)
        product = jnp.dot(x_held[...], w_held[:, span], preferred_element_type=jnp.float32)
        here[:, span] = product[:rows]
        there[:, span] = product[rows:]


def project(place, line, shards, parts, name):
    size = lax.axis_size("head")
    below, above = line
    operands = [below[0]] + below[1:] + above[1:]
    _, tokens, depth = operands[0].shape
    weights = [piece[0] for piece in shards]
    layout = [piece[1:] for piece in shards]
    shard, columns = weights[0].shape
    rows = {"first": size - 1, "last": 1, "all": size}[parts] * tokens
    out = jax.ShapeDtypeStruct((rows, columns), jnp.float32)
    moved = 2 * depth * (2 * rows + columns) + 8 * rows * columns
    return pl.pallas_call(
        functools.partial(project_kernel, size, parts, shard, tuple(layout)),
        in_specs=[SMEM] + [ANY] * (len(operands) + len(weights)),
        out_specs=[VMEM, VMEM],
        out_shape=[out, out],
        scratch_shapes=[
            pltpu.VMEM((2 * rows, depth), jnp.bfloat16),
            pltpu.VMEM((depth, columns), jnp.bfloat16),
            pltpu.SemaphoreType.DMA((2, size)),
            pltpu.SemaphoreType.DMA((len(layout),)),
        ],
        compiler_params=params(),
        cost_estimate=cost(4 * rows * depth * columns, moved),
        name=name,
    )(place, *operands, *weights)


def norms_kernel(place, first_a, first_b, last_a, last_b, out):
    width = first_a.shape[1] // 2
    rows = []
    for which in range(2):
        found = []
        for one, other in ((first_a, first_b), (last_a, last_b)):
            lanes = None
            for start in range(which * width, (which + 1) * width, HD):
                total = one[:, start : start + HD] + other[:, start : start + HD]
                lanes = total * total if lanes is None else lanes + total * total
            found.append(jnp.sum(lanes.T, axis=0, keepdims=True))
        straight = jnp.concatenate(found, axis=1)
        wrapped = jnp.concatenate(found[::-1], axis=1)
        rows.append(jnp.where(place[4] == 0, straight, wrapped))
    both = jnp.concatenate(rows, axis=0)
    for peer in range(out.shape[0]):
        out[peer] = both


def norms(place, parts, size):
    rows = parts[0].shape[0] + parts[2].shape[0]
    return pl.pallas_call(
        norms_kernel,
        in_specs=[SMEM] + [VMEM] * 4,
        out_specs=VMEM,
        out_shape=jax.ShapeDtypeStruct((size, 2, rows), jnp.float32),
        compiler_params=params(),
        cost_estimate=cost(4 * rows * parts[0].shape[1], 8 * rows * parts[0].shape[1]),
        name="norms",
    )(place, *parts)


def probs_kernel(tokens, full_width, place, squares, *refs):
    parts, (q_gain, k_gain, out, scales) = refs[:8], refs[8:]
    rows = scales.shape[1]

    @pl.when(pl.program_id(0) == 0)
    def _():
        total = squares[0]
        for peer in range(1, squares.shape[0]):
            total = total + squares[peer]
        turned = jnp.concatenate([total[:, tokens:], total[:, :tokens]], axis=1)
        total = jnp.where(place[4] == 0, total, turned)
        scale = lax.rsqrt(total / full_width + 1e-06)
        for which in range(2):
            scales[which] = jnp.broadcast_to(scale[which : which + 1], (HD, rows)).T

    column = lax.broadcasted_iota(jnp.int32, (1, rows), 1) + place[4] * tokens
    valid = jnp.where(column >= rows, column - rows, column) < place[3]
    for head in range(out.shape[0]):
        span = slice(head * HD, (head + 1) * HD)

        def normed(at, gain, which):
            joined = [parts[at + i][:, span] + parts[at + i + 1][:, span] for i in (0, 2)]
            return (jnp.concatenate(joined) * scales[which] * gain[:, span]).astype(jnp.bfloat16)

        queries, keys = normed(0, q_gain, 0), normed(4, k_gain, 1)
        scores = lax.dot_general(queries, keys, (((1,), (1,)), ((), ())), preferred_element_type=jnp.float32)
        scores = jnp.where(valid, scores * (1.0 / math.sqrt(HD)), -jnp.inf)
        raised = jnp.exp(scores - jnp.max(scores, axis=-1, keepdims=True))
        out[head] = (raised * (1.0 / jnp.sum(raised, axis=-1, keepdims=True))).astype(jnp.bfloat16)


def at_once(heads):
    return 2 if heads % 2 == 0 else 1


def probabilities(place, squares, parts, q_gain, k_gain):
    columns = parts[0].shape[1] // 2
    rows = parts[0].shape[0] + parts[2].shape[0]
    heads = columns // HD
    group = at_once(heads)
    q_blocks = [pl.BlockSpec((part.shape[0], group * HD), lambda i: (0, i)) for part in parts]
    k_blocks = [pl.BlockSpec((part.shape[0], group * HD), lambda i: (0, i + heads // group)) for part in parts]
    gain = pl.BlockSpec((1, group * HD), lambda i: (0, i))
    return pl.pallas_call(
        functools.partial(probs_kernel, parts[2].shape[0], float(columns * squares.shape[0])),
        grid=(heads // group,),
        in_specs=[SMEM, pl.BlockSpec(squares.shape, lambda i: (0, 0, 0))] + q_blocks + k_blocks + [gain] * 2,
        out_specs=pl.BlockSpec((group, rows, rows), lambda i: (i, 0, 0)),
        out_shape=jax.ShapeDtypeStruct((heads, rows, rows), jnp.bfloat16),
        scratch_shapes=[pltpu.VMEM((2, rows, HD), jnp.float32)],
        compiler_params=params(),
        cost_estimate=cost(2 * heads * rows * rows * HD, 16 * rows * columns + 2 * heads * rows * rows, heads * rows * rows),
        name="probs",
    )(place, squares, *parts, *parts, q_gain[None], k_gain[None])


def attend_kernel(place, probs, v_a, v_b, out, held):
    size, tokens, _ = out.shape
    for head in range(probs.shape[0]):
        span = slice(head * HD, (head + 1) * HD)
        values = (v_a[:, span] + v_b[:, span]).astype(jnp.bfloat16)
        held[:, span] = jnp.dot(probs[head], values, preferred_element_type=jnp.float32)
    for block in range(size):
        at = lax.rem(block - place[4] + size, size) * tokens
        out[block] = held[pl.ds(pl.multiple_of(at, tokens), tokens)].astype(jnp.bfloat16)


def attend(place, probs, v_parts, size):
    heads, rows, _ = probs.shape
    tokens = rows // size
    group = at_once(heads)
    by_head = pl.BlockSpec((rows, group * HD), lambda i: (0, i))
    return pl.pallas_call(
        attend_kernel,
        grid=(heads // group,),
        in_specs=[SMEM, pl.BlockSpec((group, rows, rows), lambda i: (i, 0, 0)), by_head, by_head],
        out_specs=pl.BlockSpec((size, tokens, group * HD), lambda i: (0, 0, i)),
        out_shape=jax.ShapeDtypeStruct((size, tokens, heads * HD), jnp.bfloat16),
        scratch_shapes=[pltpu.VMEM((rows, group * HD), jnp.float32)],
        compiler_params=params(),
        cost_estimate=cost(2 * heads * rows * rows * HD, 2 * heads * rows * rows + 10 * rows * heads * HD),
        name="attend",
    )(place, probs, *v_parts)


def out_kernel(size, layout, first, place, *refs):
    count = 2 * size - 1
    pieces, weights = refs[: len(layout)], refs[len(layout) : len(layout) + 2 * count]
    heard, out, a_held, w_held, total, a_sems, w_sems = refs[len(layout) + 2 * count :]
    steps, _, tokens, columns = out.shape
    width = columns // 2
    halves, _, _, span_width = w_held.shape
    joined = halves == 1
    step_at, core, position = place[0], place[1], place[2]

    def a_copies():
        for index, (offset, start, groups) in enumerate(layout):
            row = pl.multiple_of(jnp.bitwise_xor(step_at, offset) * tokens, tokens)
            for group in range(groups):
                yield pltpu.make_async_copy(
                    pieces[index].at[group, pl.ds(first, tokens)],
                    a_held.at[start + group, pl.ds(row, tokens)],
                    a_sems.at[index, group],
                )

    def w_copy(half, away, slot):
        group = lax.rem(position + away, size)
        at = jnp.bitwise_xor(core, half)
        if joined:
            span = pl.ds(pl.multiple_of(at * width, 128), width)
            target = w_held.at[0, group, :, span]
        else:
            target = w_held.at[at, group]
        return pltpu.make_async_copy(weights[half * count + slot], target, w_sems.at[half, away])

    for copy in a_copies():
        copy.start()
    for away in range(size):
        for half in range(2):
            if away == 0:
                w_copy(half, 0, 0).start()
                continue

            @pl.when(position + away < size)
            def _(half=half, away=away):
                w_copy(half, away, size - 1 + away).start()

            @pl.when(position + away >= size)
            def _(half=half, away=away):
                w_copy(half, away, size - away).start()

    for copy in a_copies():
        copy.wait()
    for away in range(size):
        group = lax.rem(position + away, size)
        for half in range(2):
            w_copy(half, away, 0).wait()
        for half in range(halves):
            part = jnp.dot(a_held[group], w_held[half, group], preferred_element_type=jnp.float32)
            part = part.astype(jnp.bfloat16).astype(jnp.float32)
            if away == 0:
                total[half] = part
            else:
                total[half] += part
    for half in range(halves):
        span = slice(half * span_width, (half + 1) * span_width)
        reached = jnp.zeros((tokens, span_width), jnp.float32)
        for step in range(steps):
            told = heard[step, -16:, span].astype(jnp.float32)
            gate = told[0:1] + told[1:2] + told[2:3]
            step_width = told[3:4] + told[4:5] + told[5:6]
            branch = total[half, step * tokens : (step + 1) * tokens] * gate
            out[step, 0, :, span] = branch.astype(jnp.bfloat16)
            reached += branch * step_width
            out[step, 1, :, span] = reached.astype(jnp.bfloat16)
            reached += heard[step, first : first + tokens, span].astype(jnp.float32)


def project_out(place, heard, gathered, weights, part, parts):
    size = lax.axis_size("head")
    steps = len(gathered)
    _, tokens, inner = gathered[0][0].shape
    tokens = tokens // parts
    width = weights[0][0].shape[1]
    layout, pieces = [], []
    for offset, held in enumerate(gathered):
        start = 0
        for piece in held:
            layout.append((offset, start, piece.shape[0]))
            pieces.append(piece)
            start += piece.shape[0]
    rows = steps * tokens
    halves = 1 if width % 128 == 0 else 2
    operands = pieces + [w for half in weights for w in half]
    return pl.pallas_call(
        functools.partial(out_kernel, size, tuple(layout), part * tokens),
        in_specs=[SMEM] + [ANY] * len(operands) + [VMEM],
        out_specs=VMEM,
        out_shape=jax.ShapeDtypeStruct((steps, 2, tokens, 2 * width), jnp.bfloat16),
        scratch_shapes=[
            pltpu.VMEM((size, rows, inner), jnp.bfloat16),
            pltpu.VMEM((halves, size, inner, 2 * width // halves), jnp.bfloat16),
            pltpu.VMEM((halves, rows, 2 * width // halves), jnp.float32),
            pltpu.SemaphoreType.DMA((len(layout), size)),
            pltpu.SemaphoreType.DMA((2, size)),
        ],
        compiler_params=params(),
        cost_estimate=cost(4 * rows * size * inner * width, 2 * size * inner * (rows + 2 * width) + 8 * rows * width),
        name="project_out",
    )(place, *operands, heard)


def finish_kernel(base, *refs):
    reached, update = refs[-2:]
    for part, arrived in enumerate(refs[:-2]):
        tokens = arrived.shape[2]
        rows = slice(part * tokens, (part + 1) * tokens)
        reached[rows] = base[rows] + arrived[0, 1].astype(jnp.float32)
        update[rows] = arrived[0, 0]


def finish(base, parts):
    steps, _, tokens, width = parts[0].shape
    by_columns = pl.BlockSpec((base.shape[0], width), lambda i: (0, i))
    return pl.pallas_call(
        finish_kernel,
        grid=(steps,),
        in_specs=[by_columns] + [pl.BlockSpec((1, 2, tokens, width), lambda i: (i, 0, 0, 0))] * len(parts),
        out_specs=[by_columns, by_columns],
        out_shape=[jax.ShapeDtypeStruct(base.shape, jnp.float32), jax.ShapeDtypeStruct(base.shape, jnp.bfloat16)],
        compiler_params=params(),
        cost_estimate=cost(base.size, 14 * base.size),
        name="finish",
    )(base, *parts)


def body(states, timesteps, lengths, modulation, w_query, w_key, w_value, w_out, q_gain, k_gain):
    steps, size = lax.axis_size("step"), lax.axis_size("head")
    step, core, position = (lax.axis_index(axis) for axis in ("step", "fsdp", "head"))
    current = states[0, 0]
    shift = (position >= size // 2).astype(jnp.int32)
    place = jnp.stack([step, core, position, lengths[0], shift]).astype(jnp.int32)

    w_both = jnp.concatenate([w_query, w_key], axis=1)
    mine, other = modulate(place, current, modulation, steps)
    tokens = jnp.stack([mine, swap(other, "fsdp", 1)])
    below, above = [tokens], [tokens]

    def hop(*awaited):
        count = len(below)
        arrived = (below[-1], above[-1])
        up, down = after(arrived, *awaited) if awaited else arrived
        below.append(lax.ppermute(up, "head", [(i, i + 1) for i in range(count - 1, size - 1)]))
        above.append(lax.ppermute(down, "head", [(i, i - 1) for i in range(1, size - count + 1)]))
        return arrived

    hop()
    if steps == 4 and size > 3 and w_value.shape[1] % 256 == 0:
        both_shards, last_round, finished = in_rounds(w_both, w_value, hop)
    else:
        both = forwarded(w_both, direct(w_both))
        both_shards = placed(both)
        last_round = tuple(both[-1])

        def finished(*awaited):
            return placed(forwarded(w_value, direct(after(w_value, *awaited))))

    while len(below) < size:
        hop()
    line = below, above
    early = tuple(held[: size - 1] + [held[0]] for held in line)
    step_width = (timesteps[0, 1] - timesteps[0, 0]).astype(jnp.float32) / 1000.0
    told = tell(place, step_width[None], current, modulation, steps)
    partner_below, partner_above = [swap(after(w_out, below[1], above[1]), "fsdp", 1)], []
    first_here, first_there = project(after(place, told, *partner_below), early, both_shards, "first", "first")
    ended = (below[-1], above[-1]) + last_round
    first_there = after(first_there, *ended)
    v_shards = finished(*ended, first_here)
    v_last = (v_shards[-1][0], v_shards[-2][0])
    parts = [first_here, swap(first_there, "fsdp", 1)]
    last_here, last_there = project(place, line, both_shards, "last", "last")
    parts += [last_here, swap(after(last_there, *v_last), "fsdp", 1)]
    v_here, v_there = project(after(place, last_here), line, v_shards, "all", "value")
    v_parts = [v_here, swap(v_there, "fsdp", 1)]
    heard = lax.all_to_all(after(told, last_here, *v_last), "step", 0, 0)

    below, above = [w_out], [w_out]
    for count in range(1, size):
        up, down = below[-1], above[-1]
        if count == 1:
            up, down = after((up, down), *ended, first_here)
        if count == 2:
            up, down = after((up, down), v_here)
        if count == size - 1:
            up, down = after((up, down), quarter)
        below.append(lax.ppermute(up, "head", [(i, i + 1) for i in range(count - 1, size - 1)]))
        above.append(lax.ppermute(down, "head", [(i, i - 1) for i in range(1, size - count + 1)]))
        arrived = (below[-1], above[-1])
        if count == size - 1:
            near = direct(quarter)
            gathered = forwarded(quarter, near)
            arrived = after(arrived, *[piece for pieces in near.values() for piece in pieces])
        partner_below.append(swap(arrived[0], "fsdp", 1))
        partner_above.append(swap(arrived[1], "fsdp", 1))
        if count == 1:
            own_squares = norms(after(place, below[-1], above[-1], v_here), parts, 1)
            squares = [own_squares]
            for away in range(1, size):
                squares.append(lax.ppermute(own_squares, "head", [(i, (i + away) % size) for i in range(size)]))
            squares = jnp.concatenate(squares)
        if count == size - 2:
            ready = after(squares, *partner_below[:-1], *partner_above[:-1], below[-1], above[-1], heard)
            probs = probabilities(place, ready, parts, q_gain, k_gain)
            attended = attend(place, probs, v_parts, size)
            quarter = after(lax.all_to_all(attended, "head", 0, 0), partner_below[-1], partner_above[-1])

    raw = [w_out] + below[1:] + above[1:]
    out_weights = (raw, partner_below + partner_above)
    carried = step_width * current + jnp.where(step == 0, current, jnp.zeros_like(current))

    halves = 1
    sent = [project_out(place, heard, gathered, out_weights, part, halves) for part in range(halves)]
    arrived = after(tuple(lax.all_to_all(part, "step", 0, 0) for part in sent), carried)
    reached, update = finish(carried, arrived)
    return reached[None, None], update[None, None]


def solution(mesh):
    in_specs = (
        P("step", "fsdp", "head", None),
        P("step", None),
        P("fsdp"),
        P("step", None, None),
        P(("step", "fsdp"), "head"),
        P(("step", "fsdp"), "head"),
        P(("step", "fsdp"), "head"),
        P("head", ("step", "fsdp")),
        P("head"),
        P("head"),
    )
    out_specs = (P("step", "fsdp", "head", None), P("step", "fsdp", "head", None))
    return jax.shard_map(body, mesh=mesh, in_specs=in_specs, out_specs=out_specs, check_vma=False)
```

```python
import functools
import math

import jax
import jax.numpy as jnp
from jax import lax
from jax.experimental import pallas as pl
from jax.experimental.pallas import tpu as pltpu
from jax.sharding import PartitionSpec as P

HD = 128
MIB = 1 << 20
SMEM = pl.BlockSpec(memory_space=pltpu.SMEM)
VMEM = pl.BlockSpec(memory_space=pltpu.VMEM)
ANY = pl.BlockSpec(memory_space=pl.ANY)


def swap(x, axis, offset):
    return lax.ppermute(x, axis, [(i, i ^ offset) for i in range(lax.axis_size(axis))])


def bits_of(axis):
    return [1 << bit for bit in range(lax.axis_size(axis).bit_length() - 1)]


def direct(x):
    return {bit: [swap(x, "step", bit)] for bit in bits_of("step")}


def forwarded(x, near, *awaited):
    held = {0: [x], **near}
    half = x.shape[0] // 2
    for offset in range(1, lax.axis_size("step")):
        low, high = offset & -offset, 1 << (offset.bit_length() - 1)
        if offset in held:
            continue
        top, bottom = held[offset ^ low], held[offset ^ high]
        top = top[0][:half] if len(top) == 1 else top[0]
        bottom = bottom[0][half:] if len(bottom) == 1 else bottom[1]
        if awaited:
            top, bottom = after((top, bottom), *awaited)
        held[offset] = [swap(top, "step", low), swap(bottom, "step", high)]
    return [held[offset] for offset in range(lax.axis_size("step"))]


def placed(held, column=0):
    found = []
    for offset, pieces in enumerate(held):
        row = 0
        for piece in pieces:
            found.append((piece, offset, row, 0, column, piece.shape[1]))
            row += piece.shape[0]
    return found


def in_rounds(w_both, w_value, hop):
    width = w_value.shape[1]
    a1, a2 = swap(w_both, "step", 1), swap(w_both, "step", 2)
    e1, e2 = after((a1, a2), *hop())
    b1, b2 = swap(e2[:, :width], "step", 1), swap(e1[:, width:], "step", 2)
    v1, v2 = after((w_value, w_value), b1, b2, *hop(b1, b2))
    c1, c2 = swap(v1, "step", 1), swap(v2, "step", 2)
    both = [
        (w_both, 0, 0, 0, 0, 2 * width),
        (a1, 1, 0, 0, 0, 2 * width),
        (a2, 2, 0, 0, 0, 2 * width),
        (b1, 3, 0, 0, 0, width),
        (b2, 3, 0, 0, width, width),
    ]

    def finished(*awaited):
        f1, f2 = after((c1, c2), *awaited)
        d1, d2 = swap(f2[:, : width // 2], "step", 1), swap(f1[:, width // 2 :], "step", 2)
        whole = [(w_value, 0, 0, 0, 0, width), (c1, 1, 0, 0, 0, width), (c2, 2, 0, 0, 0, width)]
        return whole + [(d1, 3, 0, 0, 0, width // 2), (d2, 3, 0, 0, width // 2, width // 2)]

    return both, (c1, c2), finished


def after(x, *others):
    return lax.optimization_barrier((x,) + others)[0]


def params(mib=56):
    return pltpu.CompilerParams(vmem_limit_bytes=mib * MIB)


def cost(flops, moved, raised=0):
    return pl.CostEstimate(flops=int(flops) // 4, bytes_accessed=int(moved) // 4, transcendentals=int(raised) // 4)


def modulate_kernel(steps, place, states, rows, mine, other):
    current = states[...]
    centre = jnp.mean(current, axis=-1, keepdims=True)
    centred = current - centre
    spread_of = jnp.mean(centred * centred, axis=-1, keepdims=True)
    shift, scale = rows[0, 0:1, :], rows[0, 1:2, :]
    modulated = (centred * lax.rsqrt(spread_of + 1e-06) * (1.0 + scale) + shift).astype(jnp.bfloat16)
    core = place[1]
    for block in range(2 * steps):
        width = modulated.shape[1] // (2 * steps)
        piece = modulated[:, block * width : (block + 1) * width]
        at = slice(block // 2 * width, (block // 2 + 1) * width)

        @pl.when(core == block % 2)
        def _(piece=piece, at=at):
            mine[:, at] = piece

        @pl.when(core != block % 2)
        def _(piece=piece, at=at):
            other[:, at] = piece


def modulate(place, states, rows, steps):
    tokens, width = states.shape
    tile = 32
    out = jax.ShapeDtypeStruct((tokens, width // 2), jnp.bfloat16)
    spec = pl.BlockSpec((tile, width // 2), lambda i: (i, 0))
    return pl.pallas_call(
        functools.partial(modulate_kernel, steps),
        grid=(tokens // tile,),
        in_specs=[SMEM, pl.BlockSpec((tile, width), lambda i: (i, 0)), pl.BlockSpec(rows.shape, lambda i: (0, 0, 0))],
        out_specs=[spec, spec],
        out_shape=[out, out],
        compiler_params=params(),
        cost_estimate=cost(10 * tokens * width, 6 * tokens * width),
        name="modulate",
    )(place, states, rows)


def terms(x):
    high = x.astype(jnp.bfloat16).astype(jnp.float32)
    middle = (x - high).astype(jnp.bfloat16).astype(jnp.float32)
    return [high, middle, x - high - middle]


def tell_kernel(place, step_width, states, rows, out):
    current = states[...]
    tokens, columns = current.shape
    width = step_width[0]
    anchor = jnp.where(place[0] == 0, 1.0, 0.0)
    out[0, :tokens] = (width * current + anchor * current).astype(jnp.bfloat16)
    told = terms(rows[0, 2:3, :]) + terms(jnp.full((1, columns), width, jnp.float32))
    told.append(jnp.zeros((10, columns), jnp.float32))
    out[0, tokens:] = jnp.concatenate(told).astype(jnp.bfloat16)


def tell(place, step_width, states, rows, steps):
    tokens, width = states.shape
    columns = width // steps
    return pl.pallas_call(
        tell_kernel,
        grid=(steps,),
        in_specs=[
            SMEM,
            SMEM,
            pl.BlockSpec((tokens, columns), lambda i: (0, i)),
            pl.BlockSpec((1, rows.shape[1], columns), lambda i: (0, 0, i)),
        ],
        out_specs=pl.BlockSpec((1, tokens + 16, columns), lambda i: (i, 0, 0)),
        out_shape=jax.ShapeDtypeStruct((steps, tokens + 16, columns), jnp.bfloat16),
        compiler_params=params(),
        cost_estimate=cost(4 * tokens * width, 6 * tokens * width),
        name="tell",
    )(place, step_width, states, rows)


def project_kernel(size, parts, shard, layout, place, *refs):
    count = 2 * size - 1
    own, below, above = refs[0], refs[1:size], refs[size:count]
    weights = refs[count : count + len(layout)]
    here, there, x_held, w_held, x_sems, w_sems = refs[count + len(layout) :]
    tokens, depth = own.shape[1:]
    step_at, position, shift = place[0], place[2], place[4]
    early = size - 1
    blocks = {"first": range(early), "last": range(early, size), "all": range(size)}[parts]

    def x_copy(ref, clip, block):
        row = (clip * len(blocks) + block - blocks[0]) * tokens
        return pltpu.make_async_copy(
            ref.at[clip], x_held.at[pl.ds(pl.multiple_of(row, tokens), tokens)], x_sems.at[clip, block]
        )

    def w_copies():
        for index, (ref, (offset, row, source, target, count)) in enumerate(zip(weights, layout)):
            at = jnp.bitwise_xor(step_at, offset) * shard + row
            rows = ref.shape[0]
            part = w_held.at[pl.ds(pl.multiple_of(at, rows), rows), pl.ds(target, count)]
            yield pltpu.make_async_copy(ref.at[:, pl.ds(source, count)], part, w_sems.at[index])

    for copy in w_copies():
        copy.start()
    for clip in range(2):
        for away in range(size):
            for sign, held in ((1, above), (-1, below)):
                if away == 0 and sign < 0:
                    continue
                source = own if away == 0 else held[away - 1]
                block_at = position + sign * away
                block = lax.rem(block_at - shift + size, size)
                inside = jnp.logical_and(block_at >= 0, block_at < size)
                inside = jnp.logical_and(inside, jnp.logical_and(block >= blocks[0], block <= blocks[-1]))

                @pl.when(inside)
                def _(source=source, block=block, clip=clip):
                    x_copy(source, clip, block).start()

    for copy in w_copies():
        copy.wait()
    for clip in range(2):
        for block in blocks:
            x_copy(own, clip, block).wait()
    rows, columns = here.shape
    width = columns if columns % 512 else columns // 2
    for start in range(0, columns, width):
        span = slice(start, start + width)
        product = jnp.dot(x_held[...], w_held[:, span], preferred_element_type=jnp.float32)
        here[:, span] = product[:rows]
        there[:, span] = product[rows:]


def project(place, line, shards, parts, name):
    size = lax.axis_size("head")
    below, above = line
    operands = [below[0]] + below[1:] + above[1:]
    _, tokens, depth = operands[0].shape
    weights = [piece[0] for piece in shards]
    layout = [piece[1:] for piece in shards]
    shard, columns = weights[0].shape
    rows = {"first": size - 1, "last": 1, "all": size}[parts] * tokens
    out = jax.ShapeDtypeStruct((rows, columns), jnp.float32)
    moved = 2 * depth * (2 * rows + columns) + 8 * rows * columns
    return pl.pallas_call(
        functools.partial(project_kernel, size, parts, shard, tuple(layout)),
        in_specs=[SMEM] + [ANY] * (len(operands) + len(weights)),
        out_specs=[VMEM, VMEM],
        out_shape=[out, out],
        scratch_shapes=[
            pltpu.VMEM((2 * rows, depth), jnp.bfloat16),
            pltpu.VMEM((depth, columns), jnp.bfloat16),
            pltpu.SemaphoreType.DMA((2, size)),
            pltpu.SemaphoreType.DMA((len(layout),)),
        ],
        compiler_params=params(),
        cost_estimate=cost(4 * rows * depth * columns, moved),
        name=name,
    )(place, *operands, *weights)


def norms_kernel(place, first_a, first_b, last_a, last_b, out):
    width = first_a.shape[1] // 2
    rows = []
    for which in range(2):
        found = []
        for one, other in ((first_a, first_b), (last_a, last_b)):
            lanes = None
            for start in range(which * width, (which + 1) * width, HD):
                total = one[:, start : start + HD] + other[:, start : start + HD]
                lanes = total * total if lanes is None else lanes + total * total
            found.append(jnp.sum(lanes.T, axis=0, keepdims=True))
        straight = jnp.concatenate(found, axis=1)
        wrapped = jnp.concatenate(found[::-1], axis=1)
        rows.append(jnp.where(place[4] == 0, straight, wrapped))
    both = jnp.concatenate(rows, axis=0)
    for peer in range(out.shape[0]):
        out[peer] = both


def norms(place, parts, size):
    rows = parts[0].shape[0] + parts[2].shape[0]
    return pl.pallas_call(
        norms_kernel,
        in_specs=[SMEM] + [VMEM] * 4,
        out_specs=VMEM,
        out_shape=jax.ShapeDtypeStruct((size, 2, rows), jnp.float32),
        compiler_params=params(),
        cost_estimate=cost(4 * rows * parts[0].shape[1], 8 * rows * parts[0].shape[1]),
        name="norms",
    )(place, *parts)


def probs_kernel(tokens, full_width, place, squares, *refs):
    parts, (q_gain, k_gain, out, scales) = refs[:8], refs[8:]
    rows = scales.shape[1]

    @pl.when(pl.program_id(0) == 0)
    def _():
        total = squares[0]
        for peer in range(1, squares.shape[0]):
            total = total + squares[peer]
        turned = jnp.concatenate([total[:, tokens:], total[:, :tokens]], axis=1)
        total = jnp.where(place[4] == 0, total, turned)
        scale = lax.rsqrt(total / full_width + 1e-06)
        for which in range(2):
            scales[which] = jnp.broadcast_to(scale[which : which + 1], (HD, rows)).T

    column = lax.broadcasted_iota(jnp.int32, (1, rows), 1) + place[4] * tokens
    valid = jnp.where(column >= rows, column - rows, column) < place[3]
    for head in range(out.shape[0]):
        span = slice(head * HD, (head + 1) * HD)

        def normed(at, gain, which):
            joined = [parts[at + i][:, span] + parts[at + i + 1][:, span] for i in (0, 2)]
            return (jnp.concatenate(joined) * scales[which] * gain[:, span]).astype(jnp.bfloat16)

        queries, keys = normed(0, q_gain, 0), normed(4, k_gain, 1)
        scores = lax.dot_general(queries, keys, (((1,), (1,)), ((), ())), preferred_element_type=jnp.float32)
        scores = jnp.where(valid, scores * (1.0 / math.sqrt(HD)), -jnp.inf)
        raised = jnp.exp(scores - jnp.max(scores, axis=-1, keepdims=True))
        out[head] = (raised * (1.0 / jnp.sum(raised, axis=-1, keepdims=True))).astype(jnp.bfloat16)


def at_once(heads):
    return 2 if heads % 2 == 0 else 1


def probabilities(place, squares, parts, q_gain, k_gain):
    columns = parts[0].shape[1] // 2
    rows = parts[0].shape[0] + parts[2].shape[0]
    heads = columns // HD
    group = at_once(heads)
    q_blocks = [pl.BlockSpec((part.shape[0], group * HD), lambda i: (0, i)) for part in parts]
    k_blocks = [pl.BlockSpec((part.shape[0], group * HD), lambda i: (0, i + heads // group)) for part in parts]
    gain = pl.BlockSpec((1, group * HD), lambda i: (0, i))
    return pl.pallas_call(
        functools.partial(probs_kernel, parts[2].shape[0], float(columns * squares.shape[0])),
        grid=(heads // group,),
        in_specs=[SMEM, pl.BlockSpec(squares.shape, lambda i: (0, 0, 0))] + q_blocks + k_blocks + [gain] * 2,
        out_specs=pl.BlockSpec((group, rows, rows), lambda i: (i, 0, 0)),
        out_shape=jax.ShapeDtypeStruct((heads, rows, rows), jnp.bfloat16),
        scratch_shapes=[pltpu.VMEM((2, rows, HD), jnp.float32)],
        compiler_params=params(),
        cost_estimate=cost(2 * heads * rows * rows * HD, 16 * rows * columns + 2 * heads * rows * rows, heads * rows * rows),
        name="probs",
    )(place, squares, *parts, *parts, q_gain[None], k_gain[None])


def attend_kernel(place, probs, v_a, v_b, out, held):
    size, tokens, _ = out.shape
    for head in range(probs.shape[0]):
        span = slice(head * HD, (head + 1) * HD)
        values = (v_a[:, span] + v_b[:, span]).astype(jnp.bfloat16)
        held[:, span] = jnp.dot(probs[head], values, preferred_element_type=jnp.float32)
    for block in range(size):
        at = lax.rem(block - place[4] + size, size) * tokens
        out[block] = held[pl.ds(pl.multiple_of(at, tokens), tokens)].astype(jnp.bfloat16)


def attend(place, probs, v_parts, size):
    heads, rows, _ = probs.shape
    tokens = rows // size
    group = at_once(heads)
    by_head = pl.BlockSpec((rows, group * HD), lambda i: (0, i))
    return pl.pallas_call(
        attend_kernel,
        grid=(heads // group,),
        in_specs=[SMEM, pl.BlockSpec((group, rows, rows), lambda i: (i, 0, 0)), by_head, by_head],
        out_specs=pl.BlockSpec((size, tokens, group * HD), lambda i: (0, 0, i)),
        out_shape=jax.ShapeDtypeStruct((size, tokens, heads * HD), jnp.bfloat16),
        scratch_shapes=[pltpu.VMEM((rows, group * HD), jnp.float32)],
        compiler_params=params(),
        cost_estimate=cost(2 * heads * rows * rows * HD, 2 * heads * rows * rows + 10 * rows * heads * HD),
        name="attend",
    )(place, probs, *v_parts)


def out_kernel(size, layout, first, place, *refs):
    count = 2 * size - 1
    pieces, weights = refs[: len(layout)], refs[len(layout) : len(layout) + 2 * count]
    heard, out, a_held, w_held, total, a_sems, w_sems = refs[len(layout) + 2 * count :]
    steps, _, tokens, columns = out.shape
    width = columns // 2
    halves, _, _, span_width = w_held.shape
    joined = halves == 1
    step_at, core, position = place[0], place[1], place[2]

    def a_copies():
        for index, (offset, start, groups) in enumerate(layout):
            row = pl.multiple_of(jnp.bitwise_xor(step_at, offset) * tokens, tokens)
            for group in range(groups):
                yield pltpu.make_async_copy(
                    pieces[index].at[group, pl.ds(first, tokens)],
                    a_held.at[start + group, pl.ds(row, tokens)],
                    a_sems.at[index, group],
                )

    def w_copy(half, away, slot):
        group = lax.rem(position + away, size)
        at = jnp.bitwise_xor(core, half)
        if joined:
            span = pl.ds(pl.multiple_of(at * width, 128), width)
            target = w_held.at[0, group, :, span]
        else:
            target = w_held.at[at, group]
        return pltpu.make_async_copy(weights[half * count + slot], target, w_sems.at[half, away])

    for copy in a_copies():
        copy.start()
    for away in range(size):
        for half in range(2):
            if away == 0:
                w_copy(half, 0, 0).start()
                continue

            @pl.when(position + away < size)
            def _(half=half, away=away):
                w_copy(half, away, size - 1 + away).start()

            @pl.when(position + away >= size)
            def _(half=half, away=away):
                w_copy(half, away, size - away).start()

    for copy in a_copies():
        copy.wait()
    for away in range(size):
        group = lax.rem(position + away, size)
        for half in range(2):
            w_copy(half, away, 0).wait()
        for half in range(halves):
            part = jnp.dot(a_held[group], w_held[half, group], preferred_element_type=jnp.float32)
            part = part.astype(jnp.bfloat16).astype(jnp.float32)
            if away == 0:
                total[half] = part
            else:
                total[half] += part
    for half in range(halves):
        span = slice(half * span_width, (half + 1) * span_width)
        reached = jnp.zeros((tokens, span_width), jnp.float32)
        for step in range(steps):
            told = heard[step, -16:, span].astype(jnp.float32)
            gate = told[0:1] + told[1:2] + told[2:3]
            step_width = told[3:4] + told[4:5] + told[5:6]
            branch = total[half, step * tokens : (step + 1) * tokens] * gate
            out[step, 0, :, span] = branch.astype(jnp.bfloat16)
            reached += branch * step_width
            out[step, 1, :, span] = reached.astype(jnp.bfloat16)
            reached += heard[step, first : first + tokens, span].astype(jnp.float32)


def project_out(place, heard, gathered, weights, part, parts):
    size = lax.axis_size("head")
    steps = len(gathered)
    _, tokens, inner = gathered[0][0].shape
    tokens = tokens // parts
    width = weights[0][0].shape[1]
    layout, pieces = [], []
    for offset, held in enumerate(gathered):
        start = 0
        for piece in held:
            layout.append((offset, start, piece.shape[0]))
            pieces.append(piece)
            start += piece.shape[0]
    rows = steps * tokens
    halves = 1 if width % 128 == 0 else 2
    operands = pieces + [w for half in weights for w in half]
    return pl.pallas_call(
        functools.partial(out_kernel, size, tuple(layout), part * tokens),
        in_specs=[SMEM] + [ANY] * len(operands) + [VMEM],
        out_specs=VMEM,
        out_shape=jax.ShapeDtypeStruct((steps, 2, tokens, 2 * width), jnp.bfloat16),
        scratch_shapes=[
            pltpu.VMEM((size, rows, inner), jnp.bfloat16),
            pltpu.VMEM((halves, size, inner, 2 * width // halves), jnp.bfloat16),
            pltpu.VMEM((halves, rows, 2 * width // halves), jnp.float32),
            pltpu.SemaphoreType.DMA((len(layout), size)),
            pltpu.SemaphoreType.DMA((2, size)),
        ],
        compiler_params=params(),
        cost_estimate=cost(4 * rows * size * inner * width, 2 * size * inner * (rows + 2 * width) + 8 * rows * width),
        name="project_out",
    )(place, *operands, heard)


def finish_kernel(base, *refs):
    reached, update = refs[-2:]
    for part, arrived in enumerate(refs[:-2]):
        tokens = arrived.shape[2]
        rows = slice(part * tokens, (part + 1) * tokens)
        reached[rows] = base[rows] + arrived[0, 1].astype(jnp.float32)
        update[rows] = arrived[0, 0]


def finish(base, parts):
    steps, _, tokens, width = parts[0].shape
    by_columns = pl.BlockSpec((base.shape[0], width), lambda i: (0, i))
    return pl.pallas_call(
        finish_kernel,
        grid=(steps,),
        in_specs=[by_columns] + [pl.BlockSpec((1, 2, tokens, width), lambda i: (i, 0, 0, 0))] * len(parts),
        out_specs=[by_columns, by_columns],
        out_shape=[jax.ShapeDtypeStruct(base.shape, jnp.float32), jax.ShapeDtypeStruct(base.shape, jnp.bfloat16)],
        compiler_params=params(),
        cost_estimate=cost(base.size, 14 * base.size),
        name="finish",
    )(base, *parts)


def body(states, timesteps, lengths, modulation, w_query, w_key, w_value, w_out, q_gain, k_gain):
    steps, size = lax.axis_size("step"), lax.axis_size("head")
    step, core, position = (lax.axis_index(axis) for axis in ("step", "fsdp", "head"))
    current = states[0, 0]
    shift = (position >= size // 2).astype(jnp.int32)
    place = jnp.stack([step, core, position, lengths[0], shift]).astype(jnp.int32)

    w_both = jnp.concatenate([w_query, w_key], axis=1)
    mine, other = modulate(place, current, modulation, steps)
    tokens = jnp.stack([mine, swap(other, "fsdp", 1)])
    below, above = [tokens], [tokens]

    def hop(*awaited):
        count = len(below)
        arrived = (below[-1], above[-1])
        up, down = after(arrived, *awaited) if awaited else arrived
        below.append(lax.ppermute(up, "head", [(i, i + 1) for i in range(count - 1, size - 1)]))
        above.append(lax.ppermute(down, "head", [(i, i - 1) for i in range(1, size - count + 1)]))
        return arrived

    hop()
    if steps == 4 and size > 3 and w_value.shape[1] % 256 == 0:
        both_shards, last_round, finished = in_rounds(w_both, w_value, hop)
    else:
        both = forwarded(w_both, direct(w_both))
        both_shards = placed(both)
        last_round = tuple(both[-1])

        def finished(*awaited):
            return placed(forwarded(w_value, direct(after(w_value, *awaited))))

    while len(below) < size:
        hop()
    line = below, above
    early = tuple(held[: size - 1] + [held[0]] for held in line)
    step_width = (timesteps[0, 1] - timesteps[0, 0]).astype(jnp.float32) / 1000.0
    told = tell(place, step_width[None], current, modulation, steps)
    partner_below, partner_above = [swap(after(w_out, below[1], above[1]), "fsdp", 1)], []
    first_here, first_there = project(after(place, told, *partner_below), early, both_shards, "first", "first")
    ended = (below[-1], above[-1]) + last_round
    first_there = after(first_there, *ended)
    v_shards = finished(*ended, first_here)
    v_last = (v_shards[-1][0], v_shards[-2][0])
    parts = [first_here, swap(first_there, "fsdp", 1)]
    last_here, last_there = project(place, line, both_shards, "last", "last")
    parts += [last_here, swap(after(last_there, *v_last), "fsdp", 1)]
    v_here, v_there = project(after(place, last_here), line, v_shards, "all", "value")
    v_parts = [v_here, swap(v_there, "fsdp", 1)]
    heard = lax.all_to_all(after(told, last_here, *v_last), "step", 0, 0)

    below, above = [w_out], [w_out]
    for count in range(1, size):
        up, down = below[-1], above[-1]
        if count == 1:
            up, down = after((up, down), *ended, first_here)
        if count == 2:
            up, down = after((up, down), v_here)
        if count == size - 1:
            up, down = after((up, down), quarter)
        below.append(lax.ppermute(up, "head", [(i, i + 1) for i in range(count - 1, size - 1)]))
        above.append(lax.ppermute(down, "head", [(i, i - 1) for i in range(1, size - count + 1)]))
        arrived = (below[-1], above[-1])
        if count == size - 1:
            near = direct(quarter)
            gathered = forwarded(quarter, near)
            arrived = after(arrived, *[piece for pieces in near.values() for piece in pieces])
        partner_below.append(swap(arrived[0], "fsdp", 1))
        partner_above.append(swap(arrived[1], "fsdp", 1))
        if count == 1:
            own_squares = norms(after(place, below[-1], above[-1], v_here), parts, 1)
            squares = [own_squares]
            for away in range(1, size):
                squares.append(lax.ppermute(own_squares, "head", [(i, (i + away) % size) for i in range(size)]))
            squares = jnp.concatenate(squares)
        if count == size - 2:
            ready = after(squares, *partner_below[:-1], *partner_above[:-1], heard)
            probs = probabilities(place, ready, parts, q_gain, k_gain)
            attended = after(attend(place, probs, v_parts, size), below[-1], above[-1])
            quarter = after(lax.all_to_all(attended, "head", 0, 0), partner_below[-1], partner_above[-1])

    raw = [w_out] + below[1:] + above[1:]
    out_weights = (raw, partner_below + partner_above)
    carried = step_width * current + jnp.where(step == 0, current, jnp.zeros_like(current))

    halves = 1
    sent = [project_out(place, heard, gathered, out_weights, part, halves) for part in range(halves)]
    arrived = after(tuple(lax.all_to_all(part, "step", 0, 0) for part in sent), carried)
    reached, update = finish(carried, arrived)
    return reached[None, None], update[None, None]


def solution(mesh):
    in_specs = (
        P("step", "fsdp", "head", None),
        P("step", None),
        P("fsdp"),
        P("step", None, None),
        P(("step", "fsdp"), "head"),
        P(("step", "fsdp"), "head"),
        P(("step", "fsdp"), "head"),
        P("head", ("step", "fsdp")),
        P("head"),
        P("head"),
    )
    out_specs = (P("step", "fsdp", "head", None), P("step", "fsdp", "head", None))
    return jax.shard_map(body, mesh=mesh, in_specs=in_specs, out_specs=out_specs, check_vma=False)
```

```python
import functools
import math

import jax
import jax.numpy as jnp
from jax import lax
from jax.experimental import pallas as pl
from jax.experimental.pallas import tpu as pltpu
from jax.sharding import PartitionSpec as P

HD = 128
MIB = 1 << 20
SMEM = pl.BlockSpec(memory_space=pltpu.SMEM)
VMEM = pl.BlockSpec(memory_space=pltpu.VMEM)
ANY = pl.BlockSpec(memory_space=pl.ANY)


def swap(x, axis, offset):
    return lax.ppermute(x, axis, [(i, i ^ offset) for i in range(lax.axis_size(axis))])


def bits_of(axis):
    return [1 << bit for bit in range(lax.axis_size(axis).bit_length() - 1)]


def direct(x):
    return {bit: [swap(x, "step", bit)] for bit in bits_of("step")}


def forwarded(x, near, *awaited):
    held = {0: [x], **near}
    half = x.shape[0] // 2
    for offset in range(1, lax.axis_size("step")):
        low, high = offset & -offset, 1 << (offset.bit_length() - 1)
        if offset in held:
            continue
        top, bottom = held[offset ^ low], held[offset ^ high]
        top = top[0][:half] if len(top) == 1 else top[0]
        bottom = bottom[0][half:] if len(bottom) == 1 else bottom[1]
        if awaited:
            top, bottom = after((top, bottom), *awaited)
        held[offset] = [swap(top, "step", low), swap(bottom, "step", high)]
    return [held[offset] for offset in range(lax.axis_size("step"))]


def placed(held, column=0):
    found = []
    for offset, pieces in enumerate(held):
        row = 0
        for piece in pieces:
            found.append((piece, offset, row, 0, column, piece.shape[1]))
            row += piece.shape[0]
    return found


def in_rounds(w_both, w_value, hop):
    width = w_value.shape[1]
    a1, a2 = swap(w_both, "step", 1), swap(w_both, "step", 2)
    e1, e2 = after((a1, a2), *hop())
    b1, b2 = swap(e2[:, :width], "step", 1), swap(e1[:, width:], "step", 2)
    v1, v2 = after((w_value, w_value), b1, b2, *hop(b1, b2))
    c1, c2 = swap(v1, "step", 1), swap(v2, "step", 2)
    both = [
        (w_both, 0, 0, 0, 0, 2 * width),
        (a1, 1, 0, 0, 0, 2 * width),
        (a2, 2, 0, 0, 0, 2 * width),
        (b1, 3, 0, 0, 0, width),
        (b2, 3, 0, 0, width, width),
    ]

    def finished(*awaited):
        f1, f2 = after((c1, c2), *awaited)
        d1, d2 = swap(f2[:, : width // 2], "step", 1), swap(f1[:, width // 2 :], "step", 2)
        whole = [(w_value, 0, 0, 0, 0, width), (c1, 1, 0, 0, 0, width), (c2, 2, 0, 0, 0, width)]
        return whole + [(d1, 3, 0, 0, 0, width // 2), (d2, 3, 0, 0, width // 2, width // 2)]

    return both, (c1, c2), finished


def after(x, *others):
    return lax.optimization_barrier((x,) + others)[0]


def params(mib=56):
    return pltpu.CompilerParams(vmem_limit_bytes=mib * MIB)


def cost(flops, moved, raised=0):
    return pl.CostEstimate(flops=int(flops) // 4, bytes_accessed=int(moved) // 4, transcendentals=int(raised) // 4)


def modulate_kernel(steps, place, states, rows, mine, other):
    current = states[...]
    centre = jnp.mean(current, axis=-1, keepdims=True)
    centred = current - centre
    spread_of = jnp.mean(centred * centred, axis=-1, keepdims=True)
    shift, scale = rows[0, 0:1, :], rows[0, 1:2, :]
    modulated = (centred * lax.rsqrt(spread_of + 1e-06) * (1.0 + scale) + shift).astype(jnp.bfloat16)
    core = place[1]
    for block in range(2 * steps):
        width = modulated.shape[1] // (2 * steps)
        piece = modulated[:, block * width : (block + 1) * width]
        at = slice(block // 2 * width, (block // 2 + 1) * width)

        @pl.when(core == block % 2)
        def _(piece=piece, at=at):
            mine[:, at] = piece

        @pl.when(core != block % 2)
        def _(piece=piece, at=at):
            other[:, at] = piece


def modulate(place, states, rows, steps):
    tokens, width = states.shape
    tile = 32
    out = jax.ShapeDtypeStruct((tokens, width // 2), jnp.bfloat16)
    spec = pl.BlockSpec((tile, width // 2), lambda i: (i, 0))
    return pl.pallas_call(
        functools.partial(modulate_kernel, steps),
        grid=(tokens // tile,),
        in_specs=[SMEM, pl.BlockSpec((tile, width), lambda i: (i, 0)), pl.BlockSpec(rows.shape, lambda i: (0, 0, 0))],
        out_specs=[spec, spec],
        out_shape=[out, out],
        compiler_params=params(),
        cost_estimate=cost(10 * tokens * width, 6 * tokens * width),
        name="modulate",
    )(place, states, rows)


def terms(x):
    high = x.astype(jnp.bfloat16).astype(jnp.float32)
    middle = (x - high).astype(jnp.bfloat16).astype(jnp.float32)
    return [high, middle, x - high - middle]


def tell_kernel(place, step_width, states, rows, out):
    current = states[...]
    tokens, columns = current.shape
    width = step_width[0]
    anchor = jnp.where(place[0] == 0, 1.0, 0.0)
    out[0, :tokens] = (width * current + anchor * current).astype(jnp.bfloat16)
    told = terms(rows[0, 2:3, :]) + terms(jnp.full((1, columns), width, jnp.float32))
    told.append(jnp.zeros((10, columns), jnp.float32))
    out[0, tokens:] = jnp.concatenate(told).astype(jnp.bfloat16)


def tell(place, step_width, states, rows, steps):
    tokens, width = states.shape
    columns = width // steps
    return pl.pallas_call(
        tell_kernel,
        grid=(steps,),
        in_specs=[
            SMEM,
            SMEM,
            pl.BlockSpec((tokens, columns), lambda i: (0, i)),
            pl.BlockSpec((1, rows.shape[1], columns), lambda i: (0, 0, i)),
        ],
        out_specs=pl.BlockSpec((1, tokens + 16, columns), lambda i: (i, 0, 0)),
        out_shape=jax.ShapeDtypeStruct((steps, tokens + 16, columns), jnp.bfloat16),
        compiler_params=params(),
        cost_estimate=cost(4 * tokens * width, 6 * tokens * width),
        name="tell",
    )(place, step_width, states, rows)


def project_kernel(size, parts, shard, layout, place, *refs):
    count = 2 * size - 1
    own, below, above = refs[0], refs[1:size], refs[size:count]
    weights = refs[count : count + len(layout)]
    here, there, x_held, w_held, x_sems, w_sems = refs[count + len(layout) :]
    tokens, depth = own.shape[1:]
    step_at, position, shift = place[0], place[2], place[4]
    early = size - 1
    blocks = {"first": range(early), "last": range(early, size), "all": range(size)}[parts]

    def x_copy(ref, clip, block):
        row = (clip * len(blocks) + block - blocks[0]) * tokens
        return pltpu.make_async_copy(
            ref.at[clip], x_held.at[pl.ds(pl.multiple_of(row, tokens), tokens)], x_sems.at[clip, block]
        )

    def w_copies():
        for index, (ref, (offset, row, source, target, count)) in enumerate(zip(weights, layout)):
            at = jnp.bitwise_xor(step_at, offset) * shard + row
            rows = ref.shape[0]
            part = w_held.at[pl.ds(pl.multiple_of(at, rows), rows), pl.ds(target, count)]
            yield pltpu.make_async_copy(ref.at[:, pl.ds(source, count)], part, w_sems.at[index])

    for copy in w_copies():
        copy.start()
    for clip in range(2):
        for away in range(size):
            for sign, held in ((1, above), (-1, below)):
                if away == 0 and sign < 0:
                    continue
                source = own if away == 0 else held[away - 1]
                block_at = position + sign * away
                block = lax.rem(block_at - shift + size, size)
                inside = jnp.logical_and(block_at >= 0, block_at < size)
                inside = jnp.logical_and(inside, jnp.logical_and(block >= blocks[0], block <= blocks[-1]))

                @pl.when(inside)
                def _(source=source, block=block, clip=clip):
                    x_copy(source, clip, block).start()

    for copy in w_copies():
        copy.wait()
    for clip in range(2):
        for block in blocks:
            x_copy(own, clip, block).wait()
    rows, columns = here.shape
    width = columns if columns % 512 else columns // 2
    for start in range(0, columns, width):
        span = slice(start, start + width)
        product = jnp.dot(x_held[...], w_held[:, span], preferred_element_type=jnp.float32)
        here[:, span] = product[:rows]
        there[:, span] = product[rows:]


def project(place, line, shards, parts, name):
    size = lax.axis_size("head")
    below, above = line
    operands = [below[0]] + below[1:] + above[1:]
    _, tokens, depth = operands[0].shape
    weights = [piece[0] for piece in shards]
    layout = [piece[1:] for piece in shards]
    shard, columns = weights[0].shape
    rows = {"first": size - 1, "last": 1, "all": size}[parts] * tokens
    out = jax.ShapeDtypeStruct((rows, columns), jnp.float32)
    moved = 2 * depth * (2 * rows + columns) + 8 * rows * columns
    return pl.pallas_call(
        functools.partial(project_kernel, size, parts, shard, tuple(layout)),
        in_specs=[SMEM] + [ANY] * (len(operands) + len(weights)),
        out_specs=[VMEM, VMEM],
        out_shape=[out, out],
        scratch_shapes=[
            pltpu.VMEM((2 * rows, depth), jnp.bfloat16),
            pltpu.VMEM((depth, columns), jnp.bfloat16),
            pltpu.SemaphoreType.DMA((2, size)),
            pltpu.SemaphoreType.DMA((len(layout),)),
        ],
        compiler_params=params(),
        cost_estimate=cost(4 * rows * depth * columns, moved),
        name=name,
    )(place, *operands, *weights)


def norms_kernel(place, first_a, first_b, last_a, last_b, out):
    width = first_a.shape[1] // 2
    rows = []
    for which in range(2):
        found = []
        for one, other in ((first_a, first_b), (last_a, last_b)):
            lanes = None
            for start in range(which * width, (which + 1) * width, HD):
                total = one[:, start : start + HD] + other[:, start : start + HD]
                lanes = total * total if lanes is None else lanes + total * total
            found.append(jnp.sum(lanes.T, axis=0, keepdims=True))
        straight = jnp.concatenate(found, axis=1)
        wrapped = jnp.concatenate(found[::-1], axis=1)
        rows.append(jnp.where(place[4] == 0, straight, wrapped))
    both = jnp.concatenate(rows, axis=0)
    for peer in range(out.shape[0]):
        out[peer] = both


def norms(place, parts, size):
    rows = parts[0].shape[0] + parts[2].shape[0]
    return pl.pallas_call(
        norms_kernel,
        in_specs=[SMEM] + [VMEM] * 4,
        out_specs=VMEM,
        out_shape=jax.ShapeDtypeStruct((size, 2, rows), jnp.float32),
        compiler_params=params(),
        cost_estimate=cost(4 * rows * parts[0].shape[1], 8 * rows * parts[0].shape[1]),
        name="norms",
    )(place, *parts)


def probs_kernel(tokens, full_width, place, squares, *refs):
    parts, (q_gain, k_gain, out, scales) = refs[:8], refs[8:]
    rows = scales.shape[1]

    @pl.when(pl.program_id(0) == 0)
    def _():
        total = squares[0]
        for peer in range(1, squares.shape[0]):
            total = total + squares[peer]
        turned = jnp.concatenate([total[:, tokens:], total[:, :tokens]], axis=1)
        total = jnp.where(place[4] == 0, total, turned)
        scale = lax.rsqrt(total / full_width + 1e-06)
        for which in range(2):
            scales[which] = jnp.broadcast_to(scale[which : which + 1], (HD, rows)).T

    column = lax.broadcasted_iota(jnp.int32, (1, rows), 1) + place[4] * tokens
    valid = jnp.where(column >= rows, column - rows, column) < place[3]
    for head in range(out.shape[0]):
        span = slice(head * HD, (head + 1) * HD)

        def normed(at, gain, which):
            joined = [parts[at + i][:, span] + parts[at + i + 1][:, span] for i in (0, 2)]
            return (jnp.concatenate(joined) * scales[which] * gain[:, span]).astype(jnp.bfloat16)

        queries, keys = normed(0, q_gain, 0), normed(4, k_gain, 1)
        scores = lax.dot_general(queries, keys, (((1,), (1,)), ((), ())), preferred_element_type=jnp.float32)
        scores = jnp.where(valid, scores * (1.0 / math.sqrt(HD)), -jnp.inf)
        raised = jnp.exp(scores - jnp.max(scores, axis=-1, keepdims=True))
        out[head] = (raised * (1.0 / jnp.sum(raised, axis=-1, keepdims=True))).astype(jnp.bfloat16)


def at_once(heads):
    return 2 if heads % 2 == 0 else 1


def probabilities(place, squares, parts, q_gain, k_gain):
    columns = parts[0].shape[1] // 2
    rows = parts[0].shape[0] + parts[2].shape[0]
    heads = columns // HD
    group = at_once(heads)
    q_blocks = [pl.BlockSpec((part.shape[0], group * HD), lambda i: (0, i)) for part in parts]
    k_blocks = [pl.BlockSpec((part.shape[0], group * HD), lambda i: (0, i + heads // group)) for part in parts]
    gain = pl.BlockSpec((1, group * HD), lambda i: (0, i))
    return pl.pallas_call(
        functools.partial(probs_kernel, parts[2].shape[0], float(columns * squares.shape[0])),
        grid=(heads // group,),
        in_specs=[SMEM, pl.BlockSpec(squares.shape, lambda i: (0, 0, 0))] + q_blocks + k_blocks + [gain] * 2,
        out_specs=pl.BlockSpec((group, rows, rows), lambda i: (i, 0, 0)),
        out_shape=jax.ShapeDtypeStruct((heads, rows, rows), jnp.bfloat16),
        scratch_shapes=[pltpu.VMEM((2, rows, HD), jnp.float32)],
        compiler_params=params(),
        cost_estimate=cost(2 * heads * rows * rows * HD, 16 * rows * columns + 2 * heads * rows * rows, heads * rows * rows),
        name="probs",
    )(place, squares, *parts, *parts, q_gain[None], k_gain[None])


def attend_kernel(place, probs, v_a, v_b, out, held):
    size, tokens, _ = out.shape
    for head in range(probs.shape[0]):
        span = slice(head * HD, (head + 1) * HD)
        values = (v_a[:, span] + v_b[:, span]).astype(jnp.bfloat16)
        held[:, span] = jnp.dot(probs[head], values, preferred_element_type=jnp.float32)
    for block in range(size):
        at = lax.rem(block - place[4] + size, size) * tokens
        out[block] = held[pl.ds(pl.multiple_of(at, tokens), tokens)].astype(jnp.bfloat16)


def attend(place, probs, v_parts, size):
    heads, rows, _ = probs.shape
    tokens = rows // size
    group = at_once(heads)
    by_head = pl.BlockSpec((rows, group * HD), lambda i: (0, i))
    return pl.pallas_call(
        attend_kernel,
        grid=(heads // group,),
        in_specs=[SMEM, pl.BlockSpec((group, rows, rows), lambda i: (i, 0, 0)), by_head, by_head],
        out_specs=pl.BlockSpec((size, tokens, group * HD), lambda i: (0, 0, i)),
        out_shape=jax.ShapeDtypeStruct((size, tokens, heads * HD), jnp.bfloat16),
        scratch_shapes=[pltpu.VMEM((rows, group * HD), jnp.float32)],
        compiler_params=params(),
        cost_estimate=cost(2 * heads * rows * rows * HD, 2 * heads * rows * rows + 10 * rows * heads * HD),
        name="attend",
    )(place, probs, *v_parts)


def out_kernel(size, layout, first, place, *refs):
    count = 2 * size - 1
    pieces, weights = refs[: len(layout)], refs[len(layout) : len(layout) + 2 * count]
    heard, out, a_held, w_held, total, a_sems, w_sems = refs[len(layout) + 2 * count :]
    steps, _, tokens, columns = out.shape
    width = columns // 2
    halves, _, _, span_width = w_held.shape
    joined = halves == 1
    step_at, core, position = place[0], place[1], place[2]

    def a_copies():
        for index, (offset, start, groups) in enumerate(layout):
            row = pl.multiple_of(jnp.bitwise_xor(step_at, offset) * tokens, tokens)
            for group in range(groups):
                yield pltpu.make_async_copy(
                    pieces[index].at[group, pl.ds(first, tokens)],
                    a_held.at[start + group, pl.ds(row, tokens)],
                    a_sems.at[index, group],
                )

    def w_copy(half, away, slot):
        group = lax.rem(position + away, size)
        at = jnp.bitwise_xor(core, half)
        if joined:
            span = pl.ds(pl.multiple_of(at * width, 128), width)
            target = w_held.at[0, group, :, span]
        else:
            target = w_held.at[at, group]
        return pltpu.make_async_copy(weights[half * count + slot], target, w_sems.at[half, away])

    for copy in a_copies():
        copy.start()
    for away in range(size):
        for half in range(2):
            if away == 0:
                w_copy(half, 0, 0).start()
                continue

            @pl.when(position + away < size)
            def _(half=half, away=away):
                w_copy(half, away, size - 1 + away).start()

            @pl.when(position + away >= size)
            def _(half=half, away=away):
                w_copy(half, away, size - away).start()

    for copy in a_copies():
        copy.wait()
    for away in range(size):
        group = lax.rem(position + away, size)
        for half in range(2):
            w_copy(half, away, 0).wait()
        for half in range(halves):
            part = jnp.dot(a_held[group], w_held[half, group], preferred_element_type=jnp.float32)
            part = part.astype(jnp.bfloat16).astype(jnp.float32)
            if away == 0:
                total[half] = part
            else:
                total[half] += part
    for half in range(halves):
        span = slice(half * span_width, (half + 1) * span_width)
        reached = jnp.zeros((tokens, span_width), jnp.float32)
        for step in range(steps):
            told = heard[step, -16:, span].astype(jnp.float32)
            gate = told[0:1] + told[1:2] + told[2:3]
            step_width = told[3:4] + told[4:5] + told[5:6]
            branch = total[half, step * tokens : (step + 1) * tokens] * gate
            out[step, 0, :, span] = branch.astype(jnp.bfloat16)
            reached += branch * step_width
            out[step, 1, :, span] = reached.astype(jnp.bfloat16)
            reached += heard[step, first : first + tokens, span].astype(jnp.float32)


def project_out(place, heard, gathered, weights, part, parts):
    size = lax.axis_size("head")
    steps = len(gathered)
    _, tokens, inner = gathered[0][0].shape
    tokens = tokens // parts
    width = weights[0][0].shape[1]
    layout, pieces = [], []
    for offset, held in enumerate(gathered):
        start = 0
        for piece in held:
            layout.append((offset, start, piece.shape[0]))
            pieces.append(piece)
            start += piece.shape[0]
    rows = steps * tokens
    halves = 1 if width % 128 == 0 else 2
    operands = pieces + [w for half in weights for w in half]
    return pl.pallas_call(
        functools.partial(out_kernel, size, tuple(layout), part * tokens),
        in_specs=[SMEM] + [ANY] * len(operands) + [VMEM],
        out_specs=VMEM,
        out_shape=jax.ShapeDtypeStruct((steps, 2, tokens, 2 * width), jnp.bfloat16),
        scratch_shapes=[
            pltpu.VMEM((size, rows, inner), jnp.bfloat16),
            pltpu.VMEM((halves, size, inner, 2 * width // halves), jnp.bfloat16),
            pltpu.VMEM((halves, rows, 2 * width // halves), jnp.float32),
            pltpu.SemaphoreType.DMA((len(layout), size)),
            pltpu.SemaphoreType.DMA((2, size)),
        ],
        compiler_params=params(),
        cost_estimate=cost(4 * rows * size * inner * width, 2 * size * inner * (rows + 2 * width) + 8 * rows * width),
        name="project_out",
    )(place, *operands, heard)


def finish_kernel(base, *refs):
    reached, update = refs[-2:]
    for part, arrived in enumerate(refs[:-2]):
        tokens = arrived.shape[2]
        rows = slice(part * tokens, (part + 1) * tokens)
        reached[rows] = base[rows] + arrived[0, 1].astype(jnp.float32)
        update[rows] = arrived[0, 0]


def finish(base, parts):
    steps, _, tokens, width = parts[0].shape
    by_columns = pl.BlockSpec((base.shape[0], width), lambda i: (0, i))
    return pl.pallas_call(
        finish_kernel,
        grid=(steps,),
        in_specs=[by_columns] + [pl.BlockSpec((1, 2, tokens, width), lambda i: (i, 0, 0, 0))] * len(parts),
        out_specs=[by_columns, by_columns],
        out_shape=[jax.ShapeDtypeStruct(base.shape, jnp.float32), jax.ShapeDtypeStruct(base.shape, jnp.bfloat16)],
        compiler_params=params(),
        cost_estimate=cost(base.size, 14 * base.size),
        name="finish",
    )(base, *parts)


def body(states, timesteps, lengths, modulation, w_query, w_key, w_value, w_out, q_gain, k_gain):
    steps, size = lax.axis_size("step"), lax.axis_size("head")
    step, core, position = (lax.axis_index(axis) for axis in ("step", "fsdp", "head"))
    current = states[0, 0]
    shift = (position >= size // 2).astype(jnp.int32)
    place = jnp.stack([step, core, position, lengths[0], shift]).astype(jnp.int32)

    w_both = jnp.concatenate([w_query, w_key], axis=1)
    mine, other = modulate(place, current, modulation, steps)
    tokens = jnp.stack([mine, swap(other, "fsdp", 1)])
    below, above = [tokens], [tokens]

    def hop(*awaited):
        count = len(below)
        arrived = (below[-1], above[-1])
        up, down = after(arrived, *awaited) if awaited else arrived
        below.append(lax.ppermute(up, "head", [(i, i + 1) for i in range(count - 1, size - 1)]))
        above.append(lax.ppermute(down, "head", [(i, i - 1) for i in range(1, size - count + 1)]))
        return arrived

    hop()
    if steps == 4 and size > 3 and w_value.shape[1] % 256 == 0:
        both_shards, last_round, finished = in_rounds(w_both, w_value, hop)
    else:
        both = forwarded(w_both, direct(w_both))
        both_shards = placed(both)
        last_round = tuple(both[-1])

        def finished(*awaited):
            return placed(forwarded(w_value, direct(after(w_value, *awaited))))

    while len(below) < size:
        hop()
    line = below, above
    early = tuple(held[: size - 1] + [held[0]] for held in line)
    step_width = (timesteps[0, 1] - timesteps[0, 0]).astype(jnp.float32) / 1000.0
    told = tell(place, step_width[None], current, modulation, steps)
    partner_below, partner_above = [swap(after(w_out, below[1], above[1]), "fsdp", 1)], []
    first_here, first_there = project(after(place, told, *partner_below), early, both_shards, "first", "first")
    ended = (below[-1], above[-1]) + last_round
    first_there = after(first_there, *ended)
    v_shards = finished(*ended, first_here)
    v_last = (v_shards[-1][0], v_shards[-2][0])
    parts = [first_here, swap(first_there, "fsdp", 1)]
    last_here, last_there = project(place, line, both_shards, "last", "last")
    parts += [last_here, swap(after(last_there, *v_last), "fsdp", 1)]
    v_here, v_there = project(after(place, last_here), line, v_shards, "all", "value")
    v_parts = [v_here, swap(v_there, "fsdp", 1)]

    below, above = [w_out], [w_out]
    for count in range(1, size):
        up, down = below[-1], above[-1]
        if count == 1:
            up, down = after((up, down), *ended, first_here)
        if count == 2:
            up, down = after((up, down), v_here)
        if count == size - 1:
            up, down = after((up, down), quarter)
        below.append(lax.ppermute(up, "head", [(i, i + 1) for i in range(count - 1, size - 1)]))
        above.append(lax.ppermute(down, "head", [(i, i - 1) for i in range(1, size - count + 1)]))
        arrived = (below[-1], above[-1])
        if count == size - 1:
            near = direct(quarter)
            gathered = forwarded(quarter, near)
            arrived = after(arrived, *[piece for pieces in near.values() for piece in pieces])
        partner_below.append(swap(arrived[0], "fsdp", 1))
        partner_above.append(swap(arrived[1], "fsdp", 1))
        if count == 1:
            own_squares = norms(after(place, below[-1], above[-1], v_here), parts, 1)
            heard = lax.all_to_all(after(told, own_squares), "step", 0, 0)
            squares = [own_squares]
            for away in range(1, size):
                squares.append(lax.ppermute(own_squares, "head", [(i, (i + away) % size) for i in range(size)]))
            squares = jnp.concatenate(squares)
        if count == size - 2:
            ready = after(squares, *partner_below[:-1], *partner_above[:-1])
            probs = probabilities(place, ready, parts, q_gain, k_gain)
            attended = after(attend(place, probs, v_parts, size), below[-1], above[-1], heard)
            quarter = after(lax.all_to_all(attended, "head", 0, 0), partner_below[-1], partner_above[-1])

    raw = [w_out] + below[1:] + above[1:]
    out_weights = (raw, partner_below + partner_above)
    carried = step_width * current + jnp.where(step == 0, current, jnp.zeros_like(current))

    halves = 1
    sent = [project_out(place, heard, gathered, out_weights, part, halves) for part in range(halves)]
    arrived = after(tuple(lax.all_to_all(part, "step", 0, 0) for part in sent), carried)
    reached, update = finish(carried, arrived)
    return reached[None, None], update[None, None]


def solution(mesh):
    in_specs = (
        P("step", "fsdp", "head", None),
        P("step", None),
        P("fsdp"),
        P("step", None, None),
        P(("step", "fsdp"), "head"),
        P(("step", "fsdp"), "head"),
        P(("step", "fsdp"), "head"),
        P("head", ("step", "fsdp")),
        P("head"),
        P("head"),
    )
    out_specs = (P("step", "fsdp", "head", None), P("step", "fsdp", "head", None))
    return jax.shard_map(body, mesh=mesh, in_specs=in_specs, out_specs=out_specs, check_vma=False)
```

```python
import functools
import math

import jax
import jax.numpy as jnp
from jax import lax
from jax.experimental import pallas as pl
from jax.experimental.pallas import tpu as pltpu
from jax.sharding import PartitionSpec as P

HD = 128
MIB = 1 << 20
SMEM = pl.BlockSpec(memory_space=pltpu.SMEM)
VMEM = pl.BlockSpec(memory_space=pltpu.VMEM)
ANY = pl.BlockSpec(memory_space=pl.ANY)


def swap(x, axis, offset):
    return lax.ppermute(x, axis, [(i, i ^ offset) for i in range(lax.axis_size(axis))])


def bits_of(axis):
    return [1 << bit for bit in range(lax.axis_size(axis).bit_length() - 1)]


def direct(x):
    return {bit: [swap(x, "step", bit)] for bit in bits_of("step")}


def forwarded(x, near, *awaited):
    held = {0: [x], **near}
    half = x.shape[0] // 2
    for offset in range(1, lax.axis_size("step")):
        low, high = offset & -offset, 1 << (offset.bit_length() - 1)
        if offset in held:
            continue
        top, bottom = held[offset ^ low], held[offset ^ high]
        top = top[0][:half] if len(top) == 1 else top[0]
        bottom = bottom[0][half:] if len(bottom) == 1 else bottom[1]
        if awaited:
            top, bottom = after((top, bottom), *awaited)
        held[offset] = [swap(top, "step", low), swap(bottom, "step", high)]
    return [held[offset] for offset in range(lax.axis_size("step"))]


def placed(held, column=0):
    found = []
    for offset, pieces in enumerate(held):
        row = 0
        for piece in pieces:
            found.append((piece, offset, row, 0, column, piece.shape[1]))
            row += piece.shape[0]
    return found


def in_rounds(w_both, w_value, hop):
    width = w_value.shape[1]
    a1, a2 = swap(w_both, "step", 1), swap(w_both, "step", 2)
    e1, e2 = after((a1, a2), *hop())
    b1, b2 = swap(e2[:, :width], "step", 1), swap(e1[:, width:], "step", 2)
    v1, v2 = after((w_value, w_value), b1, b2, *hop(b1, b2))
    c1, c2 = swap(v1, "step", 1), swap(v2, "step", 2)
    both = [
        (w_both, 0, 0, 0, 0, 2 * width),
        (a1, 1, 0, 0, 0, 2 * width),
        (a2, 2, 0, 0, 0, 2 * width),
        (b1, 3, 0, 0, 0, width),
        (b2, 3, 0, 0, width, width),
    ]

    def finished(*awaited):
        f1, f2 = after((c1, c2), *awaited)
        d1, d2 = swap(f2[:, : width // 2], "step", 1), swap(f1[:, width // 2 :], "step", 2)
        whole = [(w_value, 0, 0, 0, 0, width), (c1, 1, 0, 0, 0, width), (c2, 2, 0, 0, 0, width)]
        return whole + [(d1, 3, 0, 0, 0, width // 2), (d2, 3, 0, 0, width // 2, width // 2)]

    return both, (c1, c2), finished


def after(x, *others):
    return lax.optimization_barrier((x,) + others)[0]


def params(mib=56):
    return pltpu.CompilerParams(vmem_limit_bytes=mib * MIB)


def cost(flops, moved, raised=0):
    return pl.CostEstimate(flops=int(flops) // 4, bytes_accessed=int(moved) // 4, transcendentals=int(raised) // 4)


def modulate_kernel(steps, place, states, rows, mine, other):
    current = states[...]
    centre = jnp.mean(current, axis=-1, keepdims=True)
    centred = current - centre
    spread_of = jnp.mean(centred * centred, axis=-1, keepdims=True)
    shift, scale = rows[0, 0:1, :], rows[0, 1:2, :]
    modulated = (centred * lax.rsqrt(spread_of + 1e-06) * (1.0 + scale) + shift).astype(jnp.bfloat16)
    core = place[1]
    for block in range(2 * steps):
        width = modulated.shape[1] // (2 * steps)
        piece = modulated[:, block * width : (block + 1) * width]
        at = slice(block // 2 * width, (block // 2 + 1) * width)

        @pl.when(core == block % 2)
        def _(piece=piece, at=at):
            mine[:, at] = piece

        @pl.when(core != block % 2)
        def _(piece=piece, at=at):
            other[:, at] = piece


def modulate(place, states, rows, steps):
    tokens, width = states.shape
    tile = min(tokens, 64)
    out = jax.ShapeDtypeStruct((tokens, width // 2), jnp.bfloat16)
    spec = pl.BlockSpec((tile, width // 2), lambda i: (i, 0))
    return pl.pallas_call(
        functools.partial(modulate_kernel, steps),
        grid=(tokens // tile,),
        in_specs=[SMEM, pl.BlockSpec((tile, width), lambda i: (i, 0)), pl.BlockSpec(rows.shape, lambda i: (0, 0, 0))],
        out_specs=[spec, spec],
        out_shape=[out, out],
        compiler_params=params(),
        cost_estimate=cost(10 * tokens * width, 6 * tokens * width),
        name="modulate",
    )(place, states, rows)


def terms(x):
    high = x.astype(jnp.bfloat16).astype(jnp.float32)
    middle = (x - high).astype(jnp.bfloat16).astype(jnp.float32)
    return [high, middle, x - high - middle]


def tell_kernel(place, step_width, states, rows, out):
    current = states[...]
    tokens, columns = current.shape
    width = step_width[0]
    anchor = jnp.where(place[0] == 0, 1.0, 0.0)
    out[0, :tokens] = (width * current + anchor * current).astype(jnp.bfloat16)
    told = terms(rows[0, 2:3, :]) + terms(jnp.full((1, columns), width, jnp.float32))
    told.append(jnp.zeros((10, columns), jnp.float32))
    out[0, tokens:] = jnp.concatenate(told).astype(jnp.bfloat16)


def tell(place, step_width, states, rows, steps):
    tokens, width = states.shape
    columns = width // steps
    return pl.pallas_call(
        tell_kernel,
        grid=(steps,),
        in_specs=[
            SMEM,
            SMEM,
            pl.BlockSpec((tokens, columns), lambda i: (0, i)),
            pl.BlockSpec((1, rows.shape[1], columns), lambda i: (0, 0, i)),
        ],
        out_specs=pl.BlockSpec((1, tokens + 16, columns), lambda i: (i, 0, 0)),
        out_shape=jax.ShapeDtypeStruct((steps, tokens + 16, columns), jnp.bfloat16),
        compiler_params=params(),
        cost_estimate=cost(4 * tokens * width, 6 * tokens * width),
        name="tell",
    )(place, step_width, states, rows)


def project_kernel(size, parts, shard, layout, place, *refs):
    count = 2 * size - 1
    own, below, above = refs[0], refs[1:size], refs[size:count]
    weights = refs[count : count + len(layout)]
    here, there, x_held, w_held, x_sems, w_sems = refs[count + len(layout) :]
    tokens, depth = own.shape[1:]
    step_at, position, shift = place[0], place[2], place[4]
    early = size - 1
    blocks = {"first": range(early), "last": range(early, size), "all": range(size)}[parts]

    def x_copy(ref, clip, block):
        row = (clip * len(blocks) + block - blocks[0]) * tokens
        return pltpu.make_async_copy(
            ref.at[clip], x_held.at[pl.ds(pl.multiple_of(row, tokens), tokens)], x_sems.at[clip, block]
        )

    def w_copies():
        for index, (ref, (offset, row, source, target, count)) in enumerate(zip(weights, layout)):
            at = jnp.bitwise_xor(step_at, offset) * shard + row
            rows = ref.shape[0]
            part = w_held.at[pl.ds(pl.multiple_of(at, rows), rows), pl.ds(target, count)]
            yield pltpu.make_async_copy(ref.at[:, pl.ds(source, count)], part, w_sems.at[index])

    for copy in w_copies():
        copy.start()
    for clip in range(2):
        for away in range(size):
            for sign, held in ((1, above), (-1, below)):
                if away == 0 and sign < 0:
                    continue
                source = own if away == 0 else held[away - 1]
                block_at = position + sign * away
                block = lax.rem(block_at - shift + size, size)
                inside = jnp.logical_and(block_at >= 0, block_at < size)
                inside = jnp.logical_and(inside, jnp.logical_and(block >= blocks[0], block <= blocks[-1]))

                @pl.when(inside)
                def _(source=source, block=block, clip=clip):
                    x_copy(source, clip, block).start()

    for copy in w_copies():
        copy.wait()
    for clip in range(2):
        for block in blocks:
            x_copy(own, clip, block).wait()
    rows, columns = here.shape
    width = columns if columns % 512 else columns // 2
    for start in range(0, columns, width):
        span = slice(start, start + width)
        product = jnp.dot(x_held[...], w_held[:, span], preferred_element_type=jnp.float32)
        here[:, span] = product[:rows]
        there[:, span] = product[rows:]


def project(place, line, shards, parts, name):
    size = lax.axis_size("head")
    below, above = line
    operands = [below[0]] + below[1:] + above[1:]
    _, tokens, depth = operands[0].shape
    weights = [piece[0] for piece in shards]
    layout = [piece[1:] for piece in shards]
    shard, columns = weights[0].shape
    rows = {"first": size - 1, "last": 1, "all": size}[parts] * tokens
    out = jax.ShapeDtypeStruct((rows, columns), jnp.float32)
    moved = 2 * depth * (2 * rows + columns) + 8 * rows * columns
    return pl.pallas_call(
        functools.partial(project_kernel, size, parts, shard, tuple(layout)),
        in_specs=[SMEM] + [ANY] * (len(operands) + len(weights)),
        out_specs=[VMEM, VMEM],
        out_shape=[out, out],
        scratch_shapes=[
            pltpu.VMEM((2 * rows, depth), jnp.bfloat16),
            pltpu.VMEM((depth, columns), jnp.bfloat16),
            pltpu.SemaphoreType.DMA((2, size)),
            pltpu.SemaphoreType.DMA((len(layout),)),
        ],
        compiler_params=params(),
        cost_estimate=cost(4 * rows * depth * columns, moved),
        name=name,
    )(place, *operands, *weights)


def norms_kernel(place, first_a, first_b, last_a, last_b, out):
    width = first_a.shape[1] // 2
    rows = []
    for which in range(2):
        found = []
        for one, other in ((first_a, first_b), (last_a, last_b)):
            lanes = None
            for start in range(which * width, (which + 1) * width, HD):
                total = one[:, start : start + HD] + other[:, start : start + HD]
                lanes = total * total if lanes is None else lanes + total * total
            found.append(jnp.sum(lanes.T, axis=0, keepdims=True))
        straight = jnp.concatenate(found, axis=1)
        wrapped = jnp.concatenate(found[::-1], axis=1)
        rows.append(jnp.where(place[4] == 0, straight, wrapped))
    both = jnp.concatenate(rows, axis=0)
    for peer in range(out.shape[0]):
        out[peer] = both


def norms(place, parts, size):
    rows = parts[0].shape[0] + parts[2].shape[0]
    return pl.pallas_call(
        norms_kernel,
        in_specs=[SMEM] + [VMEM] * 4,
        out_specs=VMEM,
        out_shape=jax.ShapeDtypeStruct((size, 2, rows), jnp.float32),
        compiler_params=params(),
        cost_estimate=cost(4 * rows * parts[0].shape[1], 8 * rows * parts[0].shape[1]),
        name="norms",
    )(place, *parts)


def probs_kernel(tokens, full_width, place, squares, *refs):
    parts, (q_gain, k_gain, out, scales) = refs[:8], refs[8:]
    rows = scales.shape[1]

    @pl.when(pl.program_id(0) == 0)
    def _():
        total = squares[0]
        for peer in range(1, squares.shape[0]):
            total = total + squares[peer]
        turned = jnp.concatenate([total[:, tokens:], total[:, :tokens]], axis=1)
        total = jnp.where(place[4] == 0, total, turned)
        scale = lax.rsqrt(total / full_width + 1e-06)
        for which in range(2):
            scales[which] = jnp.broadcast_to(scale[which : which + 1], (HD, rows)).T

    column = lax.broadcasted_iota(jnp.int32, (1, rows), 1) + place[4] * tokens
    valid = jnp.where(column >= rows, column - rows, column) < place[3]
    for head in range(out.shape[0]):
        span = slice(head * HD, (head + 1) * HD)

        def normed(at, gain, which):
            joined = [parts[at + i][:, span] + parts[at + i + 1][:, span] for i in (0, 2)]
            return (jnp.concatenate(joined) * scales[which] * gain[:, span]).astype(jnp.bfloat16)

        queries, keys = normed(0, q_gain, 0), normed(4, k_gain, 1)
        scores = lax.dot_general(queries, keys, (((1,), (1,)), ((), ())), preferred_element_type=jnp.float32)
        scores = jnp.where(valid, scores * (1.0 / math.sqrt(HD)), -jnp.inf)
        raised = jnp.exp(scores - jnp.max(scores, axis=-1, keepdims=True))
        out[head] = (raised * (1.0 / jnp.sum(raised, axis=-1, keepdims=True))).astype(jnp.bfloat16)


def at_once(heads):
    return 2 if heads % 2 == 0 else 1


def probabilities(place, squares, parts, q_gain, k_gain):
    columns = parts[0].shape[1] // 2
    rows = parts[0].shape[0] + parts[2].shape[0]
    heads = columns // HD
    group = at_once(heads)
    q_blocks = [pl.BlockSpec((part.shape[0], group * HD), lambda i: (0, i)) for part in parts]
    k_blocks = [pl.BlockSpec((part.shape[0], group * HD), lambda i: (0, i + heads // group)) for part in parts]
    gain = pl.BlockSpec((1, group * HD), lambda i: (0, i))
    return pl.pallas_call(
        functools.partial(probs_kernel, parts[2].shape[0], float(columns * squares.shape[0])),
        grid=(heads // group,),
        in_specs=[SMEM, pl.BlockSpec(squares.shape, lambda i: (0, 0, 0))] + q_blocks + k_blocks + [gain] * 2,
        out_specs=pl.BlockSpec((group, rows, rows), lambda i: (i, 0, 0)),
        out_shape=jax.ShapeDtypeStruct((heads, rows, rows), jnp.bfloat16),
        scratch_shapes=[pltpu.VMEM((2, rows, HD), jnp.float32)],
        compiler_params=params(),
        cost_estimate=cost(2 * heads * rows * rows * HD, 16 * rows * columns + 2 * heads * rows * rows, heads * rows * rows),
        name="probs",
    )(place, squares, *parts, *parts, q_gain[None], k_gain[None])


def attend_kernel(place, probs, v_a, v_b, out, held):
    size, tokens, _ = out.shape
    for head in range(probs.shape[0]):
        span = slice(head * HD, (head + 1) * HD)
        values = (v_a[:, span] + v_b[:, span]).astype(jnp.bfloat16)
        held[:, span] = jnp.dot(probs[head], values, preferred_element_type=jnp.float32)
    for block in range(size):
        at = lax.rem(block - place[4] + size, size) * tokens
        out[block] = held[pl.ds(pl.multiple_of(at, tokens), tokens)].astype(jnp.bfloat16)


def attend(place, probs, v_parts, size):
    heads, rows, _ = probs.shape
    tokens = rows // size
    group = at_once(heads)
    by_head = pl.BlockSpec((rows, group * HD), lambda i: (0, i))
    return pl.pallas_call(
        attend_kernel,
        grid=(heads // group,),
        in_specs=[SMEM, pl.BlockSpec((group, rows, rows), lambda i: (i, 0, 0)), by_head, by_head],
        out_specs=pl.BlockSpec((size, tokens, group * HD), lambda i: (0, 0, i)),
        out_shape=jax.ShapeDtypeStruct((size, tokens, heads * HD), jnp.bfloat16),
        scratch_shapes=[pltpu.VMEM((rows, group * HD), jnp.float32)],
        compiler_params=params(),
        cost_estimate=cost(2 * heads * rows * rows * HD, 2 * heads * rows * rows + 10 * rows * heads * HD),
        name="attend",
    )(place, probs, *v_parts)


def out_kernel(size, layout, first, place, *refs):
    count = 2 * size - 1
    pieces, weights = refs[: len(layout)], refs[len(layout) : len(layout) + 2 * count]
    heard, out, a_held, w_held, total, a_sems, w_sems = refs[len(layout) + 2 * count :]
    steps, _, tokens, columns = out.shape
    width = columns // 2
    halves, _, _, span_width = w_held.shape
    joined = halves == 1
    step_at, core, position = place[0], place[1], place[2]

    def a_copies():
        for index, (offset, start, groups) in enumerate(layout):
            row = pl.multiple_of(jnp.bitwise_xor(step_at, offset) * tokens, tokens)
            for group in range(groups):
                yield pltpu.make_async_copy(
                    pieces[index].at[group, pl.ds(first, tokens)],
                    a_held.at[start + group, pl.ds(row, tokens)],
                    a_sems.at[index, group],
                )

    def w_copy(half, away, slot):
        group = lax.rem(position + away, size)
        at = jnp.bitwise_xor(core, half)
        if joined:
            span = pl.ds(pl.multiple_of(at * width, 128), width)
            target = w_held.at[0, group, :, span]
        else:
            target = w_held.at[at, group]
        return pltpu.make_async_copy(weights[half * count + slot], target, w_sems.at[half, away])

    for copy in a_copies():
        copy.start()
    for away in range(size):
        for half in range(2):
            if away == 0:
                w_copy(half, 0, 0).start()
                continue

            @pl.when(position + away < size)
            def _(half=half, away=away):
                w_copy(half, away, size - 1 + away).start()

            @pl.when(position + away >= size)
            def _(half=half, away=away):
                w_copy(half, away, size - away).start()

    for copy in a_copies():
        copy.wait()
    for away in range(size):
        group = lax.rem(position + away, size)
        for half in range(2):
            w_copy(half, away, 0).wait()
        for half in range(halves):
            part = jnp.dot(a_held[group], w_held[half, group], preferred_element_type=jnp.float32)
            part = part.astype(jnp.bfloat16).astype(jnp.float32)
            if away == 0:
                total[half] = part
            else:
                total[half] += part
    for half in range(halves):
        span = slice(half * span_width, (half + 1) * span_width)
        reached = jnp.zeros((tokens, span_width), jnp.float32)
        for step in range(steps):
            told = heard[step, -16:, span].astype(jnp.float32)
            gate = told[0:1] + told[1:2] + told[2:3]
            step_width = told[3:4] + told[4:5] + told[5:6]
            branch = total[half, step * tokens : (step + 1) * tokens] * gate
            out[step, 0, :, span] = branch.astype(jnp.bfloat16)
            reached += branch * step_width
            out[step, 1, :, span] = reached.astype(jnp.bfloat16)
            reached += heard[step, first : first + tokens, span].astype(jnp.float32)


def project_out(place, heard, gathered, weights, part, parts):
    size = lax.axis_size("head")
    steps = len(gathered)
    _, tokens, inner = gathered[0][0].shape
    tokens = tokens // parts
    width = weights[0][0].shape[1]
    layout, pieces = [], []
    for offset, held in enumerate(gathered):
        start = 0
        for piece in held:
            layout.append((offset, start, piece.shape[0]))
            pieces.append(piece)
            start += piece.shape[0]
    rows = steps * tokens
    halves = 1 if width % 128 == 0 else 2
    operands = pieces + [w for half in weights for w in half]
    return pl.pallas_call(
        functools.partial(out_kernel, size, tuple(layout), part * tokens),
        in_specs=[SMEM] + [ANY] * len(operands) + [VMEM],
        out_specs=VMEM,
        out_shape=jax.ShapeDtypeStruct((steps, 2, tokens, 2 * width), jnp.bfloat16),
        scratch_shapes=[
            pltpu.VMEM((size, rows, inner), jnp.bfloat16),
            pltpu.VMEM((halves, size, inner, 2 * width // halves), jnp.bfloat16),
            pltpu.VMEM((halves, rows, 2 * width // halves), jnp.float32),
            pltpu.SemaphoreType.DMA((len(layout), size)),
            pltpu.SemaphoreType.DMA((2, size)),
        ],
        compiler_params=params(),
        cost_estimate=cost(4 * rows * size * inner * width, 2 * size * inner * (rows + 2 * width) + 8 * rows * width),
        name="project_out",
    )(place, *operands, heard)


def finish_kernel(base, *refs):
    reached, update = refs[-2:]
    for part, arrived in enumerate(refs[:-2]):
        tokens = arrived.shape[2]
        rows = slice(part * tokens, (part + 1) * tokens)
        reached[rows] = base[rows] + arrived[0, 1].astype(jnp.float32)
        update[rows] = arrived[0, 0]


def finish(base, parts):
    steps, _, tokens, width = parts[0].shape
    cuts = 2 if width % 256 == 0 else 1
    width = width // cuts
    by_columns = pl.BlockSpec((base.shape[0], width), lambda i: (0, i))
    by_step = pl.BlockSpec((1, 2, tokens, width), lambda i: (i // cuts, 0, 0, i % cuts))
    return pl.pallas_call(
        finish_kernel,
        grid=(steps * cuts,),
        in_specs=[by_columns] + [by_step] * len(parts),
        out_specs=[by_columns, by_columns],
        out_shape=[jax.ShapeDtypeStruct(base.shape, jnp.float32), jax.ShapeDtypeStruct(base.shape, jnp.bfloat16)],
        compiler_params=params(),
        cost_estimate=cost(base.size, 14 * base.size),
        name="finish",
    )(base, *parts)


def body(states, timesteps, lengths, modulation, w_query, w_key, w_value, w_out, q_gain, k_gain):
    steps, size = lax.axis_size("step"), lax.axis_size("head")
    step, core, position = (lax.axis_index(axis) for axis in ("step", "fsdp", "head"))
    current = states[0, 0]
    shift = (position >= size // 2).astype(jnp.int32)
    place = jnp.stack([step, core, position, lengths[0], shift]).astype(jnp.int32)

    w_both = jnp.concatenate([w_query, w_key], axis=1)
    mine, other = modulate(place, current, modulation, steps)
    tokens = jnp.stack([mine, swap(other, "fsdp", 1)])
    below, above = [tokens], [tokens]

    def hop(*awaited):
        count = len(below)
        arrived = (below[-1], above[-1])
        up, down = after(arrived, *awaited) if awaited else arrived
        below.append(lax.ppermute(up, "head", [(i, i + 1) for i in range(count - 1, size - 1)]))
        above.append(lax.ppermute(down, "head", [(i, i - 1) for i in range(1, size - count + 1)]))
        return arrived

    hop()
    if steps == 4 and size > 3 and w_value.shape[1] % 256 == 0:
        both_shards, last_round, finished = in_rounds(w_both, w_value, hop)
    else:
        both = forwarded(w_both, direct(w_both))
        both_shards = placed(both)
        last_round = tuple(both[-1])

        def finished(*awaited):
            return placed(forwarded(w_value, direct(after(w_value, *awaited))))

    while len(below) < size:
        hop()
    line = below, above
    early = tuple(held[: size - 1] + [held[0]] for held in line)
    step_width = (timesteps[0, 1] - timesteps[0, 0]).astype(jnp.float32) / 1000.0
    told = tell(place, step_width[None], current, modulation, steps)
    partner_below, partner_above = [swap(after(w_out, below[1], above[1]), "fsdp", 1)], []
    first_here, first_there = project(after(place, told, *partner_below), early, both_shards, "first", "first")
    ended = (below[-1], above[-1]) + last_round
    first_there = after(first_there, *ended)
    v_shards = finished(*ended, first_here)
    v_last = (v_shards[-1][0], v_shards[-2][0])
    parts = [first_here, swap(first_there, "fsdp", 1)]
    last_here, last_there = project(place, line, both_shards, "last", "last")
    parts += [last_here, swap(after(last_there, *v_last), "fsdp", 1)]
    v_here, v_there = project(after(place, last_here), line, v_shards, "all", "value")
    v_parts = [v_here, swap(v_there, "fsdp", 1)]
    heard = lax.all_to_all(after(told, last_here, *v_last), "step", 0, 0)

    below, above = [w_out], [w_out]
    for count in range(1, size):
        up, down = below[-1], above[-1]
        if count == 1:
            up, down = after((up, down), *ended, first_here)
        if count == 2:
            up, down = after((up, down), v_here)
        if count == size - 1:
            up, down = after((up, down), quarter)
        below.append(lax.ppermute(up, "head", [(i, i + 1) for i in range(count - 1, size - 1)]))
        above.append(lax.ppermute(down, "head", [(i, i - 1) for i in range(1, size - count + 1)]))
        arrived = (below[-1], above[-1])
        if count == size - 1:
            near = direct(quarter)
            gathered = forwarded(quarter, near)
            arrived = after(arrived, *[piece for pieces in near.values() for piece in pieces])
        partner_below.append(swap(arrived[0], "fsdp", 1))
        partner_above.append(swap(arrived[1], "fsdp", 1))
        if count == 1:
            own_squares = norms(after(place, below[-1], above[-1], v_here), parts, 1)
            squares = [own_squares]
            for away in range(1, size):
                squares.append(lax.ppermute(own_squares, "head", [(i, (i + away) % size) for i in range(size)]))
            squares = jnp.concatenate(squares)
        if count == size - 2:
            ready = after(squares, *partner_below[:-1], *partner_above[:-1], heard)
            probs = probabilities(place, ready, parts, q_gain, k_gain)
            attended = after(attend(place, probs, v_parts, size), below[-1], above[-1])
            quarter = after(lax.all_to_all(attended, "head", 0, 0), partner_below[-1], partner_above[-1])

    raw = [w_out] + below[1:] + above[1:]
    out_weights = (raw, partner_below + partner_above)
    carried = step_width * current + jnp.where(step == 0, current, jnp.zeros_like(current))

    halves = 1
    sent = [project_out(place, heard, gathered, out_weights, part, halves) for part in range(halves)]
    arrived = after(tuple(lax.all_to_all(part, "step", 0, 0) for part in sent), carried)
    reached, update = finish(carried, arrived)
    return reached[None, None], update[None, None]


def solution(mesh):
    in_specs = (
        P("step", "fsdp", "head", None),
        P("step", None),
        P("fsdp"),
        P("step", None, None),
        P(("step", "fsdp"), "head"),
        P(("step", "fsdp"), "head"),
        P(("step", "fsdp"), "head"),
        P("head", ("step", "fsdp")),
        P("head"),
        P("head"),
    )
    out_specs = (P("step", "fsdp", "head", None), P("step", "fsdp", "head", None))
    return jax.shard_map(body, mesh=mesh, in_specs=in_specs, out_specs=out_specs, check_vma=False)
```
